128 devices in a mesh: gz: 16 (over z, y), xy: 8 (over x, core).
Axes of the slice: x: 4, y: 4, z: 4, core: 2. Of those that a mesh axis runs over, the one named last changes fastest.
Arguments:
- volume: float32 [256, 256, 128], P('gz', 'xy'), may hold values from -6 to 6
- owners: int32 [8, 64, 1], P('xy', 'gz'), may hold values from 0 to 15; in each aligned block of 4 rows (0 to 3, 4 to 7, ..., all dimensions but the last counted through in order) at most 2 rows name the same one
Outputs:
- denoised: float32 [256, 256, 128], P('gz', 'xy')
- routed: float32 [8, 512, 128, 128], P('xy', 'gz')
The draws below stay inside these ranges and needn't reach their ends.
Inputs may be any that keep to these rules, and one draw needn't show every extreme that they name: `owners`: among the 4 blocks of one device no destination is named more than 2 times, a bound that some block reaches.
All inputs are finite; a program needn't handle non-finite values.
Results may differ from the reference program's by a relative error of at most 0.0003.
Values sent between devices are 32-bit elements; how exact they have to be, the bound alone decides.
A program may use at most 64 MiB of HBM per device.

```python
import math
import jax
import jax.numpy as jnp
import numpy as np
from jax import lax

CZ = 16
CY = 32
NX = 128
STEPS = 2
MOST = 2
BLOCK_ROWS = 128
NZ = 256
NY = 256
BLK_DEV = 4
BLOCKS = 64
N_GZ = 16
N_XY = 8


def draw_volume(key, part):
    key_level = jax.random.fold_in(key, 11)
    shape = (NZ, NY, NX)
    return jax.random.uniform(key_level, shape, jnp.float32, -6.0, 6.0)


def deal_out(stream_key, own, number, rows, count, top, limit, skew):
    ranking = jax.random.permutation(stream_key, count)
    heavy_load, ordinary = shares(count, rows * top, limit, skew, True), shares(count, rows * top, limit, skew, False)
    places = jnp.arange(count)

    def named(sizes, turn):
        used = int((sizes > 0).sum())
        fixed = max(1, used // 4)
        moved = fixed + (places - fixed + turn * (used - fixed)) % max(1, count - fixed)
        return jnp.zeros((count,), jnp.int32).at[ranking[jnp.where(places < fixed, places, moved)]].set(jnp.asarray(sizes, jnp.int32))

    sizes = jnp.where(number % 4 == 0, named(heavy_load, number // 4), named(ordinary, number - number // 4 - 1))
    mixed = jax.random.permutation(jax.random.fold_in(own, 3), count)
    source_of, taker = mixed[0:count // 2 * 2:2], mixed[1:count // 2 * 2:2]
    margin = jnp.minimum(sizes[source_of] - 1, limit - sizes[taker]) // 2
    margin = jnp.where((source_of == ranking[0]) | (taker == ranking[0]) | (sizes[taker] == 0), 0, jnp.maximum(margin, 0))
    moved = jax.random.randint(jax.random.fold_in(own, 4), (count // 2,), 0, 1 << 20) % (margin + 1)
    sizes = sizes.at[source_of].add(-moved).at[taker].add(moved)
    labels = jnp.searchsorted(jnp.cumsum(sizes), jnp.arange(rows * top), side="right").astype(jnp.int32)
    table = labels.reshape(top, rows).T
    table = table[jax.random.permutation(jax.random.fold_in(own, 1), rows)]
    turn = jax.random.randint(jax.random.fold_in(own, 2), (rows, 1), 0, top)
    return jnp.take_along_axis(table, (jnp.arange(top)[None, :] + turn) % top, axis=1)


def shares(count, total, bound, skew, full):
    portions = [(1 << 20) // math.isqrt(standing ** skew) + 1 for standing in range(1, count + 1)]
    largest = bound if full else min(bound, max(-(-total // count), total * portions[0] // sum(portions)))
    least = 1 if total - largest >= count - 1 else 0
    given, spare = [largest] + [least] * (count - 1), total - largest - least * (count - 1)
    while spare > 0:
        free = [i for i in range(1, count) if given[i] < largest] or [i for i in range(1, count) if given[i] < bound]
        mass, budget = sum([portions[i] for i in free]), spare
        for i in free:
            extra = min(bound - given[i], max(1, budget * portions[i] // mass), spare)
            given[i] = given[i] + extra
            spare = spare - extra
    return np.array(given)


def setup_inputs(seed: int = 0) -> dict:
    keys = jax.random.split(jax.random.key(seed), 3)
    volume = draw_volume(jax.random.fold_in(keys[2], 71), 0)
    owners_keys = jax.random.split(jax.random.fold_in(keys[1], 1), N_XY * BLOCKS // BLK_DEV)
    owners_turns = jax.random.permutation(jax.random.fold_in(keys[1], 3), N_XY * BLOCKS // BLK_DEV)
    owners = jax.vmap(lambda own, number: deal_out(jax.random.fold_in(keys[1], 2), own, number, BLK_DEV, N_GZ, 1, MOST, 2))(owners_keys, owners_turns).reshape((N_XY, BLOCKS, 1))
    return dict(volume=volume, owners=owners)


TIME_STEP = 30.0
CONTRAST = 4.0


def shifted(field, stride, line_axis, fill, before):
    length = field.shape[line_axis]
    if stride >= length:
        return jnp.full_like(field, fill)
    shape = list(field.shape)
    shape[line_axis] = stride
    padding = jnp.full(tuple(shape), fill, field.dtype)
    if before:
        return jnp.concatenate([padding, lax.slice_in_dim(field, 0, length - stride, axis=line_axis)], axis=line_axis)
    return jnp.concatenate([lax.slice_in_dim(field, stride, length, axis=line_axis), padding], axis=line_axis)


def cyclic_solve(low_diag, main_diag, high_diag, right_side, line_axis, side_axis):
    length = main_diag.shape[line_axis]
    stride = 1
    while stride < length:
        low_prev = shifted(low_diag, stride, line_axis, 0.0, True)
        main_prev = shifted(main_diag, stride, line_axis, 1.0, True)
        high_prev = shifted(high_diag, stride, line_axis, 0.0, True)
        side_prev = shifted(right_side, stride, side_axis, 0.0, True)
        low_next = shifted(low_diag, stride, line_axis, 0.0, False)
        main_next = shifted(main_diag, stride, line_axis, 1.0, False)
        high_next = shifted(high_diag, stride, line_axis, 0.0, False)
        side_next = shifted(right_side, stride, side_axis, 0.0, False)
        factor_low = -low_diag / main_prev
        factor_high = -high_diag / main_next
        main_diag = main_diag + factor_low * high_prev + factor_high * low_next
        right_side = right_side + factor_low * side_prev + factor_high * side_next
        low_diag = factor_low * low_prev
        high_diag = factor_high * high_next
        stride = stride * 2
    return right_side / main_diag


def coefficients(g_line, line_axis, has_before, has_after):
    length = g_line.shape[line_axis] - 2
    weight = 0.5 * (lax.slice_in_dim(g_line, 0, length + 1, axis=line_axis) + lax.slice_in_dim(g_line, 1, length + 2, axis=line_axis))
    shape = [1] * weight.ndim
    shape[line_axis] = length + 1
    edge_index = lax.broadcasted_iota(jnp.int32, tuple(shape), line_axis)
    keep_mask = jnp.where(edge_index == 0, has_before, 1.0) * jnp.where(edge_index == length, has_after, 1.0)
    weight = weight * keep_mask
    low_diag = -3.0 * TIME_STEP * lax.slice_in_dim(weight, 0, length, axis=line_axis)
    high_diag = -3.0 * TIME_STEP * lax.slice_in_dim(weight, 1, length + 1, axis=line_axis)
    main_diag = 1.0 - low_diag - high_diag
    return low_diag, main_diag, high_diag


def pad_zero(field, line_axis):
    widths = [(0, 0)] * field.ndim
    widths[line_axis] = (1, 1)
    return jnp.pad(field, widths)


def diffusivity(field):
    squares = None
    for line_axis in range(3):
        length = field.shape[line_axis]
        later = jnp.concatenate([lax.slice_in_dim(field, 1, length, axis=line_axis), lax.slice_in_dim(field, length - 1, length, axis=line_axis)], axis=line_axis)
        earlier = jnp.concatenate([lax.slice_in_dim(field, 0, 1, axis=line_axis), lax.slice_in_dim(field, 0, length - 1, axis=line_axis)], axis=line_axis)
        slope = (later - earlier) * 0.5
        squares = slope * slope if squares is None else squares + slope * slope
    return 1.0 / (1.0 + squares / CONTRAST)


def line_solve(g_field, right_side, line_axis):
    low_diag, main_diag, high_diag = coefficients(pad_zero(g_field, line_axis), line_axis, 0.0, 0.0)
    return cyclic_solve(low_diag, main_diag, high_diag, right_side, line_axis, line_axis)


def reference(volume, owners):
    field = volume
    for section_index in range(STEPS):
        g_field = diffusivity(field)
        along_x = line_solve(g_field, field, 2)
        along_y = line_solve(g_field, field, 1)
        along_z = line_solve(g_field, field, 0)
        field = (along_x + along_y + along_z) / 3.0
    blocks_all = field.reshape(N_GZ, CZ, N_XY, CY, NX).transpose(2, 0, 1, 3, 4).reshape(N_XY, N_GZ, BLK_DEV, BLOCK_ROWS, NX)
    targets = owners[:, :, 0].reshape(N_XY, N_GZ, BLK_DEV)
    same = targets[..., :, None] == targets[..., None, :]
    block_iota = jnp.arange(BLK_DEV, dtype=jnp.int32)
    earlier = block_iota[:, None] < block_iota[None, :]
    order_rank = jnp.sum((same & earlier).astype(jnp.int32), axis=-2)
    source_iota = jnp.arange(N_GZ, dtype=jnp.int32).reshape(1, N_GZ, 1)
    slot_index = targets * (N_GZ * MOST) + source_iota * MOST + order_rank
    column_iota = jnp.arange(N_XY, dtype=jnp.int32).reshape(N_XY, 1, 1)
    routed = jnp.zeros((N_XY, N_GZ * N_GZ * MOST, BLOCK_ROWS, NX), field.dtype)
    routed = routed.at[column_iota, slot_index].set(blocks_all)
    return field, routed
```

```python
import jax
import jax.numpy as jnp
from jax import lax
from jax.experimental import pallas as pl
from jax.experimental.pallas import tpu as pltpu
from jax.sharding import PartitionSpec as P

STEPS = 2
MOST = 2
BLOCK_ROWS = 128

TIME_STEP = 30.0
CONTRAST = 4.0
HALF_K = 1.5 * TIME_STEP

CZ = 16
CY = 32
NX = 128
ROWS = CZ * CY
N_GZ = 16
N_XY = 8
FIELDS = 7
MESH = pl.DeviceIdType.MESH

Z_PEERS = sorted(
    [(a, b) for a in range(4) for b in range(4) if (a, b) != (0, 0)],
    key=lambda p: -(min(p[0], 4 - p[0]) + min(p[1], 4 - p[1])),
)
Y_PEERS = sorted(
    [(a, b) for a in range(4) for b in range(2) if (a, b) != (0, 0)],
    key=lambda p: -(2 * min(p[0], 4 - p[0]) + p[1]),
)


def recip(value):
    return 1.0 / value


def pcr(diag, coupling, side, count, axis):
    stride = 1
    while stride < count:
        inverse = recip(diag)
        scaled = coupling * inverse
        side_scaled = side * inverse
        side = (
            side
            + pltpu.roll(coupling * side_scaled, stride, axis)
            + coupling * pltpu.roll(side_scaled, count - stride, axis)
        )
        diag = (
            diag
            - pltpu.roll(coupling * scaled, stride, axis)
            - coupling * coupling * pltpu.roll(inverse, count - stride, axis)
        )
        stride *= 2
        if stride < count:
            coupling = coupling * pltpu.roll(scaled, count - stride // 2, axis)
    return side * recip(diag)


def forward_sweep(count, load_v, load_g, store):
    g_here = load_g(0)
    g_first = g_here
    total = jnp.ones_like(g_here)
    side = load_v(0)
    unit = jnp.ones_like(g_here)
    first_side = jnp.zeros_like(g_here)
    first_unit = jnp.zeros_like(g_here)
    for i in range(count - 1):
        g_next = load_g(i + 1)
        weight = HALF_K * (g_here + g_next)
        inverse = recip(total + weight)
        ratio = weight * inverse
        side_scaled = side * inverse
        unit_scaled = unit * inverse
        store(i, ratio, side_scaled, unit_scaled)
        first_side = first_side + unit * side_scaled
        first_unit = first_unit + unit * unit_scaled
        total = 1.0 + ratio * total
        side = load_v(i + 1) + ratio * side
        unit = ratio * unit
        g_here = g_next
    inverse = recip(total)
    last_side = side * inverse
    last_unit = unit * inverse
    store(count - 1, inverse, last_side, last_unit)
    first_side = first_side + unit * last_side
    first_unit = first_unit + unit * last_unit
    return (first_side, last_side, first_unit, last_unit, inverse, g_first, g_here)


def backward_sweep(count, load, store):
    high_unit, side, low_unit = load(count - 1)
    store(count - 1, side, low_unit, high_unit)
    for i in range(count - 2, -1, -1):
        ratio, side_scaled, unit_scaled = load(i)
        side = side_scaled + ratio * side
        low_unit = unit_scaled + ratio * low_unit
        high_unit = ratio * high_unit
        store(i, side, low_unit, high_unit)


def interface_fluxes(received, count, half):
    first_side, last_side, first_unit, cross, last_unit, g_first, g_last = [received(j) for j in range(FIELDS)]
    index = lax.broadcasted_iota(jnp.int32, (count, NX), 0)

    def following(field):
        return pltpu.roll(field, count - 1, 0)

    weight = HALF_K * (g_last + following(g_first))
    diag = recip(weight) + last_unit + following(first_unit)
    side = last_side - following(first_side)
    diag = jnp.where(index < count - 1, diag, 1.0)
    side = jnp.where(index < count - 1, side, 0.0)
    coupling = jnp.where(index < count - 2, following(cross), 0.0)
    return pcr(diag, coupling, side, count, 0)


def solver_kernel(
    volume_ref,
    out_ref,
    middle,
    z_halo,
    y_halo_out,
    y_halo,
    g_ref,
    z_keep,
    y_keep,
    natural,
    base,
    z_out,
    z_in,
    y_out,
    y_in,
    z_back_out,
    z_back,
    y_back_out,
    y_back,
    halo_send,
    halo_recv,
    z_send,
    z_recv,
    y_send,
    y_recv,
    zb_send,
    zb_recv,
    yb_send,
    yb_recv,
):
    gz = lax.axis_index("gz")
    xy = lax.axis_index("xy")
    z_targets = [
        lax.rem(gz // 4 + dz, 4) * 4 + lax.rem(lax.rem(gz, 4) + dy, 4) for dz, dy in Z_PEERS
    ]
    y_targets = [
        lax.rem(xy // 2 + dx, 4) * 2 + lax.rem(lax.rem(xy, 2) + core, 2) for dx, core in Y_PEERS
    ]
    barrier = pltpu.get_barrier_semaphore()
    for target in z_targets:
        pl.semaphore_signal(barrier, 1, device_id={"gz": target}, device_id_type=MESH)
    for target in y_targets:
        pl.semaphore_signal(barrier, 1, device_id={"xy": target}, device_id_type=MESH)
    pl.semaphore_wait(barrier, N_GZ + N_XY - 2)

    row_index = lax.broadcasted_iota(jnp.int32, (CY, NX), 0)
    lane_index = lax.broadcasted_iota(jnp.int32, (CY, NX), 1)

    def send_all(source, landing, send_sem, recv_sem, axis, targets, me):
        for target in targets:
            pltpu.make_async_remote_copy(
                source.at[target], landing.at[me], send_sem, recv_sem,
                device_id={axis: target}, device_id_type=MESH,
            ).start()

    def wait_all(buffer, count, semaphore):
        part = buffer.at[pl.ds(0, count)]
        pltpu.make_async_copy(part, part, semaphore).wait()

    for step in range(STEPS):
        v = volume_ref if step == 0 else middle
        new = out_ref if step == STEPS - 1 else middle

        y_halo_out[step, 0] = v[pl.ds(0, CZ, stride=CY), :]
        y_halo_out[step, 1] = v[pl.ds(CY - 1, CZ, stride=CY), :]
        copies = []
        for k, (axis, me, count, forward) in enumerate(
            [("gz", gz, N_GZ, 0), ("gz", gz, N_GZ, 1), ("xy", xy, N_XY, 0), ("xy", xy, N_XY, 1)]
        ):
            target = lax.rem(me + (1 if forward else count - 1), count)
            if axis == "gz":
                source = v.at[pl.ds((CZ - 1) * CY if forward else 0, CY)]
                landing = z_halo.at[step, 1 - forward]
            else:
                source = y_halo_out.at[step, forward]
                landing = y_halo.at[step, 1 - forward]
            copies.append(
                pltpu.make_async_remote_copy(
                    source, landing, halo_send.at[step, k], halo_recv.at[step, k],
                    device_id={axis: target}, device_id_type=MESH,
                )
            )
        for copy in copies:
            copy.start()
        for copy in copies:
            copy.wait_recv()

        def plane(i):
            return v[i * CY : (i + 1) * CY, :]

        before = jnp.where(gz == 0, plane(0), z_halo[step, 0])
        after = jnp.where(gz == N_GZ - 1, plane(CZ - 1), z_halo[step, 1])
        here = plane(0)
        for i in range(CZ):
            above = plane(i + 1) if i < CZ - 1 else after
            slope_z = above - before
            y_low = jnp.where(xy == 0, here[0:1, :], y_halo[step, 0, i : i + 1, :])
            y_high = jnp.where(xy == N_XY - 1, here[CY - 1 : CY, :], y_halo[step, 1, i : i + 1, :])
            y_prev = jnp.where(row_index == 0, y_low, pltpu.roll(here, 1, 0))
            y_next = jnp.where(row_index == CY - 1, y_high, pltpu.roll(here, CY - 1, 0))
            slope_y = y_next - y_prev
            x_prev = jnp.where(lane_index == 0, here, pltpu.roll(here, 1, 1))
            x_next = jnp.where(lane_index == NX - 1, here, pltpu.roll(here, NX - 1, 1))
            slope_x = x_next - x_prev
            squares = slope_z * slope_z + slope_y * slope_y + slope_x * slope_x
            g_ref[i * CY : (i + 1) * CY, :] = recip(1.0 + squares * (0.25 / CONTRAST))
            before, here = here, above

        def z_store(i, ratio, side, unit):
            z_keep[0, i] = ratio
            z_keep[1, i] = side
            z_keep[2, i] = unit

        ends = forward_sweep(CZ, plane, lambda i: g_ref[i * CY : (i + 1) * CY, :], z_store)
        for j, field in enumerate(ends):
            for half in range(2):
                z_out[step, pl.ds(2 * j + half, N_GZ, stride=16), :] = field[half * N_GZ : (half + 1) * N_GZ, :]
        z_in_blocks = z_in.at[step].reshape(N_GZ, 16, NX)
        z_out_blocks = z_out.at[step].reshape(N_GZ, 16, NX)
        send_all(z_out_blocks, z_in_blocks, z_send.at[step], z_recv.at[step], "gz", z_targets, gz)

        def y_store(i, ratio, side, unit):
            y_keep[0, i] = ratio
            y_keep[1, i] = side
            y_keep[2, i] = unit

        ends = forward_sweep(
            CY,
            lambda i: v[pl.ds(i, CZ, stride=CY), :],
            lambda i: g_ref[pl.ds(i, CZ, stride=CY), :],
            y_store,
        )
        for j, field in enumerate(ends):
            for half in range(2):
                y_out[step, pl.ds(2 * j + half, N_XY, stride=16), :] = field[half * N_XY : (half + 1) * N_XY, :]
        y_in_blocks = y_in.at[step].reshape(N_XY, 16, NX)
        y_out_blocks = y_out.at[step].reshape(N_XY, 16, NX)
        send_all(y_out_blocks, y_in_blocks, y_send.at[step], y_recv.at[step], "xy", y_targets, xy)
        z_in_blocks[gz] = z_out_blocks[gz]
        y_in_blocks[xy] = y_out_blocks[xy]

        def solve_x(i, carry):
            rows = pl.ds(pl.multiple_of(i * 2 * CY, 2 * CY), 2 * CY)
            g = g_ref[rows, :]
            lanes = lax.broadcasted_iota(jnp.int32, (2 * CY, NX), 1)
            weight = jnp.where(lanes < NX - 1, HALF_K * (g + pltpu.roll(g, NX - 1, 1)), 0.0)
            diag = 1.0 + weight + pltpu.roll(weight, 1, 1)
            base[rows, :] = pcr(diag, weight, v[rows, :], NX, 1)
            return carry

        lax.fori_loop(0, CZ // 2, solve_x, 0)

        def z_load(i):
            return z_keep[0, i], z_keep[1, i], z_keep[2, i]

        def z_restore(i, side, low, high):
            base[i * CY : (i + 1) * CY, :] += side
            z_keep[1, i] = low
            z_keep[2, i] = high

        backward_sweep(CZ, z_load, z_restore)

        def y_load(i):
            return y_keep[0, i], y_keep[1, i], y_keep[2, i]

        def y_restore(i, side, low, high):
            rows = pl.ds(i, CZ, stride=CY)
            natural[0, rows, :] = side
            natural[1, rows, :] = low
            natural[2, rows, :] = high

        backward_sweep(CY, y_load, y_restore)

        wait_all(z_in_blocks, N_GZ - 1, z_recv.at[step])
        zb_out = z_back_out.at[step].reshape(N_GZ, 8, NX)
        zb_in = z_back.at[step].reshape(N_GZ, 8, NX)
        for half in range(2):
            flux = interface_fluxes(
                lambda j: z_in[step, pl.ds(2 * j + half, N_GZ, stride=16), :], N_GZ, half
            )
            z_back_out[step, pl.ds(half, N_GZ, stride=8), :] = pltpu.roll(flux, 1, 0)
            z_back_out[step, pl.ds(2 + half, N_GZ, stride=8), :] = flux
        send_all(zb_out, zb_in, zb_send.at[step], zb_recv.at[step], "gz", z_targets, gz)
        zb_in[gz] = zb_out[gz]

        wait_all(y_in_blocks, N_XY - 1, y_recv.at[step])
        yb_out = y_back_out.at[step].reshape(N_XY, 8, NX)
        yb_in = y_back.at[step].reshape(N_XY, 8, NX)
        for half in range(2):
            flux = interface_fluxes(
                lambda j: y_in[step, pl.ds(2 * j + half, N_XY, stride=16), :], N_XY, half
            )
            y_back_out[step, pl.ds(half, N_XY, stride=8), :] = pltpu.roll(flux, 1, 0)
            y_back_out[step, pl.ds(2 + half, N_XY, stride=8), :] = flux
        send_all(yb_out, yb_in, yb_send.at[step], yb_recv.at[step], "xy", y_targets, xy)
        yb_in[xy] = yb_out[xy]

        wait_all(yb_in, N_XY - 1, yb_recv.at[step])
        wait_all(zb_in, N_GZ - 1, zb_recv.at[step])
        low_z = jnp.concatenate([z_back[step, pl.ds(h, N_GZ, stride=8), :] for h in (0, 1)], axis=0)
        high_z = jnp.concatenate([z_back[step, pl.ds(2 + h, N_GZ, stride=8), :] for h in (0, 1)], axis=0)
        for i in range(CZ):
            rows = slice(i * CY, (i + 1) * CY)
            at = (i % N_XY) * 8 + i // N_XY
            low_y = y_back[step, at : at + 1, :]
            high_y = y_back[step, at + 2 : at + 3, :]
            total = base[rows, :] + natural[0, rows, :]
            total = total + (low_z * z_keep[1, i] - high_z * z_keep[2, i])
            total = total + (low_y * natural[1, rows, :] - high_y * natural[2, rows, :])
            new[rows, :] = total * (1.0 / 3.0)

        if step == STEPS - 1:
            continue

    for step in range(STEPS):
        v = volume_ref if step == 0 else middle
        for k in range(4):
            part = v.at[pl.ds(0, CY)] if k < 2 else y_halo_out.at[step, 0]
            pltpu.make_async_copy(part, part, halo_send.at[step, k]).wait()
        wait_all(z_out.at[step].reshape(N_GZ, 16, NX), N_GZ - 1, z_send.at[step])
        wait_all(y_out.at[step].reshape(N_XY, 16, NX), N_XY - 1, y_send.at[step])
        wait_all(z_back_out.at[step].reshape(N_GZ, 8, NX), N_GZ - 1, zb_send.at[step])
        wait_all(y_back_out.at[step].reshape(N_XY, 8, NX), N_XY - 1, yb_send.at[step])


def vmem(*shape):
    return pltpu.VMEM(shape, jnp.float32)


def solve(volume):
    dma = pltpu.SemaphoreType.DMA
    return pl.pallas_call(
        solver_kernel,
        out_shape=jax.ShapeDtypeStruct((ROWS, NX), jnp.float32),
        in_specs=[pl.BlockSpec(memory_space=pltpu.VMEM)],
        out_specs=pl.BlockSpec(memory_space=pltpu.VMEM),
        scratch_shapes=[
            vmem(ROWS, NX),
            vmem(STEPS, 2, CY, NX),
            vmem(STEPS, 2, CZ, NX),
            vmem(STEPS, 2, CZ, NX),
            vmem(ROWS, NX),
            vmem(3, CZ, CY, NX),
            vmem(3, CY, CZ, NX),
            vmem(3, ROWS, NX),
            vmem(ROWS, NX),
            vmem(STEPS, N_GZ * 16, NX),
            vmem(STEPS, N_GZ * 16, NX),
            vmem(STEPS, N_XY * 16, NX),
            vmem(STEPS, N_XY * 16, NX),
            vmem(STEPS, N_GZ * 8, NX),
            vmem(STEPS, N_GZ * 8, NX),
            vmem(STEPS, N_XY * 8, NX),
            vmem(STEPS, N_XY * 8, NX),
            dma((STEPS, 4)),
            dma((STEPS, 4)),
        ]
        + [dma((STEPS,))] * 8,
        compiler_params=pltpu.CompilerParams(
            collective_id=0, has_side_effects=True, vmem_limit_bytes=32 << 20
        ),
    )(volume)


def on_device(volume, owners):
    depth, height, width = volume.shape
    z_count = lax.axis_size("gz")
    field = solve(volume.reshape(depth * height, width))
    blocks = field.reshape(-1, BLOCK_ROWS, width)
    targets = owners.reshape(-1)
    block_count = targets.shape[0]
    same = targets[:, None] == targets[None, :]
    block_iota = jnp.arange(block_count, dtype=jnp.int32)
    earlier = block_iota[:, None] < block_iota[None, :]
    order_rank = jnp.sum((same & earlier).astype(jnp.int32), axis=0)
    slot_index = targets * MOST + order_rank
    outgoing = (
        jnp.zeros((z_count * MOST, BLOCK_ROWS, width), field.dtype).at[slot_index].set(blocks)
    )
    incoming = lax.all_to_all(outgoing, "gz", split_axis=0, concat_axis=0, tiled=True)
    return (field.reshape(volume.shape), incoming.reshape(1, z_count * MOST, BLOCK_ROWS, width))


def solution(mesh):
    in_specs = (P("gz", "xy", None), P("xy", "gz", None))
    out_specs = (P("gz", "xy", None), P("xy", "gz", None, None))
    return jax.shard_map(
        on_device, mesh=mesh, in_specs=in_specs, out_specs=out_specs, check_vma=False
    )
```

```python
import jax
import jax.numpy as jnp
from jax import lax
from jax.experimental import pallas as pl
from jax.experimental.pallas import tpu as pltpu
from jax.sharding import PartitionSpec as P

STEPS = 2
MOST = 2
BLOCK_ROWS = 128

TIME_STEP = 30.0
CONTRAST = 4.0
HALF_K = 1.5 * TIME_STEP

CZ = 16
CY = 32
NX = 128
ROWS = CZ * CY
N_GZ = 16
N_XY = 8
FIELDS = 7
BLOCKS_HERE = 4
HALF_ROWS = BLOCK_ROWS // 2
CHUNKS = 2
CHUNK_ROWS = HALF_ROWS // CHUNKS
MESH = pl.DeviceIdType.MESH

Z_PEERS = sorted(
    [(a, b) for a in range(4) for b in range(4) if (a, b) != (0, 0)],
    key=lambda p: -(min(p[0], 4 - p[0]) + min(p[1], 4 - p[1])),
)
Y_PEERS = sorted(
    [(a, b) for a in range(4) for b in range(2) if (a, b) != (0, 0)],
    key=lambda p: -(2 * min(p[0], 4 - p[0]) + p[1]),
)


def recip(value):
    return 1.0 / value


def pcr(diag, coupling, side, count, axis):
    stride = 1
    while stride < count:
        inverse = recip(diag)
        scaled = coupling * inverse
        side_scaled = side * inverse
        side = (
            side
            + pltpu.roll(coupling * side_scaled, stride, axis)
            + coupling * pltpu.roll(side_scaled, count - stride, axis)
        )
        diag = (
            diag
            - pltpu.roll(coupling * scaled, stride, axis)
            - coupling * coupling * pltpu.roll(inverse, count - stride, axis)
        )
        stride *= 2
        if stride < count:
            coupling = coupling * pltpu.roll(scaled, count - stride // 2, axis)
    return side * recip(diag)


def forward_sweep(count, load_v, load_g, store):
    g_here = load_g(0)
    g_first = g_here
    total = jnp.ones_like(g_here)
    side = load_v(0)
    unit = jnp.ones_like(g_here)
    first_side = jnp.zeros_like(g_here)
    first_unit = jnp.zeros_like(g_here)
    for i in range(count - 1):
        g_next = load_g(i + 1)
        weight = HALF_K * (g_here + g_next)
        inverse = recip(total + weight)
        ratio = weight * inverse
        side_scaled = side * inverse
        unit_scaled = unit * inverse
        store(i, ratio, side_scaled, unit_scaled)
        first_side = first_side + unit * side_scaled
        first_unit = first_unit + unit * unit_scaled
        total = 1.0 + ratio * total
        side = load_v(i + 1) + ratio * side
        unit = ratio * unit
        g_here = g_next
    inverse = recip(total)
    last_side = side * inverse
    last_unit = unit * inverse
    store(count - 1, inverse, last_side, last_unit)
    first_side = first_side + unit * last_side
    first_unit = first_unit + unit * last_unit
    return (first_side, last_side, first_unit, last_unit, inverse, g_first, g_here)


def backward_sweep(count, load, store):
    high_unit, side, low_unit = load(count - 1)
    store(count - 1, side, low_unit, high_unit)
    for i in range(count - 2, -1, -1):
        ratio, side_scaled, unit_scaled = load(i)
        side = side_scaled + ratio * side
        low_unit = unit_scaled + ratio * low_unit
        high_unit = ratio * high_unit
        store(i, side, low_unit, high_unit)


def interface_fluxes(received, count, half):
    first_side, last_side, first_unit, cross, last_unit, g_first, g_last = [received(j) for j in range(FIELDS)]
    index = lax.broadcasted_iota(jnp.int32, (count, NX), 0)

    def following(field):
        return pltpu.roll(field, count - 1, 0)

    weight = HALF_K * (g_last + following(g_first))
    diag = recip(weight) + last_unit + following(first_unit)
    side = last_side - following(first_side)
    diag = jnp.where(index < count - 1, diag, 1.0)
    side = jnp.where(index < count - 1, side, 0.0)
    coupling = jnp.where(index < count - 2, following(cross), 0.0)
    return pcr(diag, coupling, side, count, 0)


def diffuse_and_route_kernel(
    volume_hbm,
    owners_ref,
    out_ref,
    routed_ref,
    volume_ref,
    middle,
    z_halo,
    y_halo_out,
    y_halo,
    g_ref,
    z_keep,
    y_keep,
    natural,
    base,
    z_out,
    z_in,
    y_out,
    y_in,
    z_back_out,
    z_back,
    y_back_out,
    y_back,
    halo_send,
    halo_recv,
    z_send,
    z_recv,
    y_send,
    y_recv,
    zb_send,
    zb_recv,
    yb_send,
    yb_recv,
    codes_out,
    codes_in,
    codes,
    gathered,
    packed,
    volume_sem,
    codes_send,
    codes_recv,
    codes_sem,
    own_sem,
    gather_send,
    gather_recv,
    spread_send,
    spread_recv,
):
    load_volume = pltpu.make_async_copy(volume_hbm, volume_ref, volume_sem)
    load_volume.start()
    gz = lax.axis_index("gz")
    xy = lax.axis_index("xy")
    z_targets = [
        lax.rem(gz // 4 + dz, 4) * 4 + lax.rem(lax.rem(gz, 4) + dy, 4) for dz, dy in Z_PEERS
    ]
    y_targets = [
        lax.rem(xy // 2 + dx, 4) * 2 + lax.rem(lax.rem(xy, 2) + core, 2) for dx, core in Y_PEERS
    ]
    barrier = pltpu.get_barrier_semaphore()
    for target in z_targets:
        pl.semaphore_signal(barrier, 1, device_id={"gz": target}, device_id_type=MESH)
    for target in y_targets:
        pl.semaphore_signal(barrier, 1, device_id={"xy": target}, device_id_type=MESH)
    pl.semaphore_wait(barrier, N_GZ + N_XY - 2)

    chip_z, chip_y = gz // 4, lax.rem(gz, 4)
    places = [chip_y, chip_z]

    def partner(way, offset):
        if way == 0:
            return chip_z * 4 + lax.rem(chip_y + offset, 4)
        return lax.rem(chip_z + offset, 4) * 4 + chip_y

    own_codes = []
    lanes = lax.broadcasted_iota(jnp.int32, (8, NX), 1)
    code_tile = jnp.zeros((8, NX), jnp.int32)
    for b in range(BLOCKS_HERE):
        rank = 0
        for earlier in range(b):
            rank = rank + (owners_ref[earlier] == owners_ref[b]).astype(jnp.int32)
        code_tile = jnp.where(lanes == b, owners_ref[b] * MOST + rank, code_tile)
    codes_out[...] = code_tile
    for way in range(2):
        codes_in[way, places[way]] = code_tile
        for offset in (2, 1, 3):
            pltpu.make_async_remote_copy(
                codes_out, codes_in.at[way, places[way]], codes_send.at[way], codes_recv.at[way],
                device_id={"gz": partner(way, offset)}, device_id_type=MESH,
            ).start()
    load_volume.wait()

    row_index = lax.broadcasted_iota(jnp.int32, (CY, NX), 0)
    lane_index = lax.broadcasted_iota(jnp.int32, (CY, NX), 1)

    def send_all(source, landing, send_sem, recv_sem, axis, targets, me):
        for target in targets:
            pltpu.make_async_remote_copy(
                source.at[target], landing.at[me], send_sem, recv_sem,
                device_id={axis: target}, device_id_type=MESH,
            ).start()

    def wait_all(buffer, count, semaphore):
        part = buffer.at[pl.ds(0, count)]
        pltpu.make_async_copy(part, part, semaphore).wait()

    for step in range(STEPS):
        v = volume_ref if step == 0 else middle
        new = out_ref if step == STEPS - 1 else middle

        y_halo_out[step, 0] = v[pl.ds(0, CZ, stride=CY), :]
        y_halo_out[step, 1] = v[pl.ds(CY - 1, CZ, stride=CY), :]
        copies = []
        for k, (axis, me, count, forward) in enumerate(
            [("gz", gz, N_GZ, 0), ("gz", gz, N_GZ, 1), ("xy", xy, N_XY, 0), ("xy", xy, N_XY, 1)]
        ):
            target = lax.rem(me + (1 if forward else count - 1), count)
            if axis == "gz":
                source = v.at[pl.ds((CZ - 1) * CY if forward else 0, CY)]
                landing = z_halo.at[step, 1 - forward]
            else:
                source = y_halo_out.at[step, forward]
                landing = y_halo.at[step, 1 - forward]
            copies.append(
                pltpu.make_async_remote_copy(
                    source, landing, halo_send.at[step, k], halo_recv.at[step, k],
                    device_id={axis: target}, device_id_type=MESH,
                )
            )
        for copy in copies:
            copy.start()
        for copy in copies:
            copy.wait_recv()

        def plane(i):
            return v[i * CY : (i + 1) * CY, :]

        before = jnp.where(gz == 0, plane(0), z_halo[step, 0])
        after = jnp.where(gz == N_GZ - 1, plane(CZ - 1), z_halo[step, 1])
        here = plane(0)
        for i in range(CZ):
            above = plane(i + 1) if i < CZ - 1 else after
            slope_z = above - before
            y_low = jnp.where(xy == 0, here[0:1, :], y_halo[step, 0, i : i + 1, :])
            y_high = jnp.where(xy == N_XY - 1, here[CY - 1 : CY, :], y_halo[step, 1, i : i + 1, :])
            y_prev = jnp.where(row_index == 0, y_low, pltpu.roll(here, 1, 0))
            y_next = jnp.where(row_index == CY - 1, y_high, pltpu.roll(here, CY - 1, 0))
            slope_y = y_next - y_prev
            x_prev = jnp.where(lane_index == 0, here, pltpu.roll(here, 1, 1))
            x_next = jnp.where(lane_index == NX - 1, here, pltpu.roll(here, NX - 1, 1))
            slope_x = x_next - x_prev
            squares = slope_z * slope_z + slope_y * slope_y + slope_x * slope_x
            g_ref[i * CY : (i + 1) * CY, :] = recip(1.0 + squares * (0.25 / CONTRAST))
            before, here = here, above

        def z_store(i, ratio, side, unit):
            z_keep[0, i] = ratio
            z_keep[1, i] = side
            z_keep[2, i] = unit

        ends = forward_sweep(CZ, plane, lambda i: g_ref[i * CY : (i + 1) * CY, :], z_store)
        for j, field in enumerate(ends):
            for half in range(2):
                z_out[step, pl.ds(2 * j + half, N_GZ, stride=16), :] = field[half * N_GZ : (half + 1) * N_GZ, :]
        z_in_blocks = z_in.at[step].reshape(N_GZ, 16, NX)
        z_out_blocks = z_out.at[step].reshape(N_GZ, 16, NX)
        send_all(z_out_blocks, z_in_blocks, z_send.at[step], z_recv.at[step], "gz", z_targets, gz)

        def y_store(i, ratio, side, unit):
            y_keep[0, i] = ratio
            y_keep[1, i] = side
            y_keep[2, i] = unit

        ends = forward_sweep(
            CY,
            lambda i: v[pl.ds(i, CZ, stride=CY), :],
            lambda i: g_ref[pl.ds(i, CZ, stride=CY), :],
            y_store,
        )
        for j, field in enumerate(ends):
            for half in range(2):
                y_out[step, pl.ds(2 * j + half, N_XY, stride=16), :] = field[half * N_XY : (half + 1) * N_XY, :]
        y_in_blocks = y_in.at[step].reshape(N_XY, 16, NX)
        y_out_blocks = y_out.at[step].reshape(N_XY, 16, NX)
        send_all(y_out_blocks, y_in_blocks, y_send.at[step], y_recv.at[step], "xy", y_targets, xy)
        z_in_blocks[gz] = z_out_blocks[gz]
        y_in_blocks[xy] = y_out_blocks[xy]

        def solve_x(i, carry):
            rows = pl.ds(pl.multiple_of(i * 2 * CY, 2 * CY), 2 * CY)
            g = g_ref[rows, :]
            lanes = lax.broadcasted_iota(jnp.int32, (2 * CY, NX), 1)
            weight = jnp.where(lanes < NX - 1, HALF_K * (g + pltpu.roll(g, NX - 1, 1)), 0.0)
            diag = 1.0 + weight + pltpu.roll(weight, 1, 1)
            base[rows, :] = pcr(diag, weight, v[rows, :], NX, 1)
            return carry

        lax.fori_loop(0, CZ // 2, solve_x, 0)

        def z_load(i):
            return z_keep[0, i], z_keep[1, i], z_keep[2, i]

        def z_restore(i, side, low, high):
            base[i * CY : (i + 1) * CY, :] += side
            z_keep[1, i] = low
            z_keep[2, i] = high

        backward_sweep(CZ, z_load, z_restore)

        def y_load(i):
            return y_keep[0, i], y_keep[1, i], y_keep[2, i]

        def y_restore(i, side, low, high):
            rows = pl.ds(i, CZ, stride=CY)
            natural[0, rows, :] = side
            natural[1, rows, :] = low
            natural[2, rows, :] = high

        backward_sweep(CY, y_load, y_restore)

        wait_all(z_in_blocks, N_GZ - 1, z_recv.at[step])
        zb_out = z_back_out.at[step].reshape(N_GZ, 8, NX)
        zb_in = z_back.at[step].reshape(N_GZ, 8, NX)
        for half in range(2):
            flux = interface_fluxes(
                lambda j: z_in[step, pl.ds(2 * j + half, N_GZ, stride=16), :], N_GZ, half
            )
            z_back_out[step, pl.ds(half, N_GZ, stride=8), :] = pltpu.roll(flux, 1, 0)
            z_back_out[step, pl.ds(2 + half, N_GZ, stride=8), :] = flux
        send_all(zb_out, zb_in, zb_send.at[step], zb_recv.at[step], "gz", z_targets, gz)
        zb_in[gz] = zb_out[gz]

        wait_all(y_in_blocks, N_XY - 1, y_recv.at[step])
        yb_out = y_back_out.at[step].reshape(N_XY, 8, NX)
        yb_in = y_back.at[step].reshape(N_XY, 8, NX)
        for half in range(2):
            flux = interface_fluxes(
                lambda j: y_in[step, pl.ds(2 * j + half, N_XY, stride=16), :], N_XY, half
            )
            y_back_out[step, pl.ds(half, N_XY, stride=8), :] = pltpu.roll(flux, 1, 0)
            y_back_out[step, pl.ds(2 + half, N_XY, stride=8), :] = flux
        send_all(yb_out, yb_in, yb_send.at[step], yb_recv.at[step], "xy", y_targets, xy)
        yb_in[xy] = yb_out[xy]

        wait_all(yb_in, N_XY - 1, yb_recv.at[step])
        wait_all(zb_in, N_GZ - 1, zb_recv.at[step])
        low_z = jnp.concatenate([z_back[step, pl.ds(h, N_GZ, stride=8), :] for h in (0, 1)], axis=0)
        high_z = jnp.concatenate([z_back[step, pl.ds(2 + h, N_GZ, stride=8), :] for h in (0, 1)], axis=0)
        for i in range(CZ):
            rows = slice(i * CY, (i + 1) * CY)
            at = (i % N_XY) * 8 + i // N_XY
            low_y = y_back[step, at : at + 1, :]
            high_y = y_back[step, at + 2 : at + 3, :]
            total = base[rows, :] + natural[0, rows, :]
            total = total + (low_z * z_keep[1, i] - high_z * z_keep[2, i])
            total = total + (low_y * natural[1, rows, :] - high_y * natural[2, rows, :])
            new[rows, :] = total * (1.0 / 3.0)

    for way in range(2):
        wait_all(codes_in.at[way], 3, codes_recv.at[way])
    to_scalars = pltpu.make_async_copy(codes_in, codes, codes_sem)
    to_scalars.start()
    blocks = out_ref.reshape(BLOCKS_HERE, BLOCK_ROWS, NX)
    for chunk in range(CHUNKS):
        for way in range(2):
            here = pl.ds(way * HALF_ROWS + chunk * CHUNK_ROWS, CHUNK_ROWS)
            for offset in (2, 1, 3):
                pltpu.make_async_remote_copy(
                    blocks.at[:, here, :], gathered[way][chunk].at[places[way]],
                    gather_send.at[chunk, way], gather_recv.at[chunk, way],
                    device_id={"gz": partner(way, offset)}, device_id_type=MESH,
                ).start()
    for way in range(2):
        for chunk in range(CHUNKS):
            here = pl.ds(way * HALF_ROWS + chunk * CHUNK_ROWS, CHUNK_ROWS)
            gathered[way][chunk][places[way]] = blocks[:, here, :]
    to_scalars.wait()
    choice = {}
    for way in range(2):
        for offset in range(4):
            target = partner(1 - way, offset)
            for source in range(4):
                for rank in range(MOST):
                    index, found = 0, 0
                    for b in range(BLOCKS_HERE):
                        hit = (codes[way, source, 0, b] == target * MOST + rank).astype(jnp.int32)
                        index = index + b * hit
                        found = found + hit
                    choice[way, offset, source, rank] = index, found
    for chunk in range(CHUNKS):
        for way in range(2):
            there = pl.ds(chunk * CHUNK_ROWS, CHUNK_ROWS)
            final = pl.ds(way * HALF_ROWS + chunk * CHUNK_ROWS, CHUNK_ROWS)
            wait_all(gathered[way][chunk], 3, gather_recv.at[chunk, way])
            for offset in (2, 1, 3, 0):
                for source in range(4):
                    for rank in range(MOST):
                        index, found = choice[way, offset, source, rank]
                        rows = gathered[way][chunk][source, index]
                        packed[way, offset, source, rank, there, :] = jnp.where(found > 0, rows, 0.0)
                landing = routed_ref.at[chip_z, :, :, final, :] if way == 0 else routed_ref.at[:, chip_y, :, final, :]
                if offset:
                    pltpu.make_async_remote_copy(
                        packed.at[way, offset, :, :, there, :], landing,
                        spread_send.at[chunk, way], spread_recv.at[chunk, way],
                        device_id={"gz": partner(1 - way, offset)}, device_id_type=MESH,
                    ).start()
                else:
                    pltpu.make_async_copy(
                        packed.at[way, offset, :, :, there, :], landing, own_sem.at[chunk, way]
                    ).start()
    for chunk in range(CHUNKS):
        for way in range(2):
            there = pl.ds(chunk * CHUNK_ROWS, CHUNK_ROWS)
            part = packed.at[way, pl.ds(0, 3), :, :, there, :]
            pltpu.make_async_copy(part, part, spread_recv.at[chunk, way]).wait()
            pltpu.make_async_copy(part, part, spread_send.at[chunk, way]).wait()
            part = packed.at[way, 0, :, :, there, :]
            pltpu.make_async_copy(part, part, own_sem.at[chunk, way]).wait()
            wait_all(gathered[way][chunk], 3, gather_send.at[chunk, way])
    for way in range(2):
        wait_all(codes_in.at[way], 3, codes_send.at[way])
    for step in range(STEPS):
        v = volume_ref if step == 0 else middle
        for k in range(4):
            part = v.at[pl.ds(0, CY)] if k < 2 else y_halo_out.at[step, 0]
            pltpu.make_async_copy(part, part, halo_send.at[step, k]).wait()
        wait_all(z_out.at[step].reshape(N_GZ, 16, NX), N_GZ - 1, z_send.at[step])
        wait_all(y_out.at[step].reshape(N_XY, 16, NX), N_XY - 1, y_send.at[step])
        wait_all(z_back_out.at[step].reshape(N_GZ, 8, NX), N_GZ - 1, zb_send.at[step])
        wait_all(y_back_out.at[step].reshape(N_XY, 8, NX), N_XY - 1, yb_send.at[step])


def vmem(*shape):
    return pltpu.VMEM(shape, jnp.float32)


def diffuse_and_route(volume, owners):
    dma = pltpu.SemaphoreType.DMA
    return pl.pallas_call(
        diffuse_and_route_kernel,
        out_shape=(
            jax.ShapeDtypeStruct((ROWS, NX), jnp.float32),
            jax.ShapeDtypeStruct((4, 4, MOST, BLOCK_ROWS, NX), jnp.float32),
        ),
        in_specs=[
            pl.BlockSpec(memory_space=pl.ANY),
            pl.BlockSpec(memory_space=pltpu.SMEM),
        ],
        out_specs=(pl.BlockSpec(memory_space=pltpu.VMEM), pl.BlockSpec(memory_space=pl.ANY)),
        scratch_shapes=[
            vmem(ROWS, NX),
            vmem(ROWS, NX),
            vmem(STEPS, 2, CY, NX),
            vmem(STEPS, 2, CZ, NX),
            vmem(STEPS, 2, CZ, NX),
            vmem(ROWS, NX),
            vmem(3, CZ, CY, NX),
            vmem(3, CY, CZ, NX),
            vmem(3, ROWS, NX),
            vmem(ROWS, NX),
            vmem(STEPS, N_GZ * 16, NX),
            vmem(STEPS, N_GZ * 16, NX),
            vmem(STEPS, N_XY * 16, NX),
            vmem(STEPS, N_XY * 16, NX),
            vmem(STEPS, N_GZ * 8, NX),
            vmem(STEPS, N_GZ * 8, NX),
            vmem(STEPS, N_XY * 8, NX),
            vmem(STEPS, N_XY * 8, NX),
            dma((STEPS, 4)),
            dma((STEPS, 4)),
        ]
        + [dma((STEPS,))] * 8
        + [
            pltpu.VMEM((8, NX), jnp.int32),
            pltpu.VMEM((2, 4, 8, NX), jnp.int32),
            pltpu.SMEM((2, 4, 8, NX), jnp.int32),
            [[vmem(4, BLOCKS_HERE, CHUNK_ROWS, NX) for _ in range(CHUNKS)] for _ in range(2)],
            vmem(2, 4, 4, MOST, HALF_ROWS, NX),
            dma,
            dma((2,)),
            dma((2,)),
            dma,
        ]
        + [dma((CHUNKS, 2))] * 5,
        compiler_params=pltpu.CompilerParams(
            collective_id=0, has_side_effects=True, vmem_limit_bytes=40 << 20
        ),
    )(volume, owners)


def on_device(volume, owners):
    depth, height, width = volume.shape
    field, routed = diffuse_and_route(volume.reshape(depth * height, width), owners.reshape(-1))
    return (field.reshape(volume.shape), routed.reshape(1, N_GZ * MOST, BLOCK_ROWS, width))


def solution(mesh):
    in_specs = (P("gz", "xy", None), P("xy", "gz", None))
    out_specs = (P("gz", "xy", None), P("xy", "gz", None, None))
    return jax.shard_map(
        on_device, mesh=mesh, in_specs=in_specs, out_specs=out_specs, check_vma=False
    )
```

```python
import jax
import jax.numpy as jnp
from jax import lax
from jax.experimental import pallas as pl
from jax.experimental.pallas import tpu as pltpu
from jax.sharding import PartitionSpec as P

STEPS = 2
MOST = 2
BLOCK_ROWS = 128

TIME_STEP = 30.0
CONTRAST = 4.0
HALF_K = 1.5 * TIME_STEP

CZ = 16
CY = 32
NX = 128
ROWS = CZ * CY
N_GZ = 16
N_XY = 8
FIELDS = 7
BLOCKS_HERE = 4
HALF_ROWS = BLOCK_ROWS // 2
CHUNKS = 2
CHUNK_ROWS = HALF_ROWS // CHUNKS
MESH = pl.DeviceIdType.MESH

Z_PEERS = sorted(
    [(a, b) for a in range(4) for b in range(4) if (a, b) != (0, 0)],
    key=lambda p: -(min(p[0], 4 - p[0]) + min(p[1], 4 - p[1])),
)
Y_PEERS = sorted(
    [(a, b) for a in range(4) for b in range(2) if (a, b) != (0, 0)],
    key=lambda p: -(2 * min(p[0], 4 - p[0]) + p[1]),
)


def recip(value):
    return 1.0 / value


def pcr(diag, coupling, side, count, axis):
    stride = 1
    while stride < count:
        inverse = recip(diag)
        scaled = coupling * inverse
        side_scaled = side * inverse
        side = (
            side
            + pltpu.roll(coupling * side_scaled, stride, axis)
            + coupling * pltpu.roll(side_scaled, count - stride, axis)
        )
        diag = (
            diag
            - pltpu.roll(coupling * scaled, stride, axis)
            - coupling * coupling * pltpu.roll(inverse, count - stride, axis)
        )
        stride *= 2
        if stride < count:
            coupling = coupling * pltpu.roll(scaled, count - stride // 2, axis)
    return side * recip(diag)


def forward_sweep(count, load_v, load_g, store):
    g_here = load_g(0)
    g_first = g_here
    total = jnp.ones_like(g_here)
    side = load_v(0)
    unit = jnp.ones_like(g_here)
    first_side = jnp.zeros_like(g_here)
    first_unit = jnp.zeros_like(g_here)
    for i in range(count - 1):
        g_next = load_g(i + 1)
        weight = HALF_K * (g_here + g_next)
        inverse = recip(total + weight)
        ratio = weight * inverse
        side_scaled = side * inverse
        unit_scaled = unit * inverse
        store(i, ratio, side_scaled, unit_scaled)
        first_side = first_side + unit * side_scaled
        first_unit = first_unit + unit * unit_scaled
        total = 1.0 + ratio * total
        side = load_v(i + 1) + ratio * side
        unit = ratio * unit
        g_here = g_next
    inverse = recip(total)
    last_side = side * inverse
    last_unit = unit * inverse
    store(count - 1, inverse, last_side, last_unit)
    first_side = first_side + unit * last_side
    first_unit = first_unit + unit * last_unit
    return (first_side, last_side, first_unit, last_unit, inverse, g_first, g_here)


def backward_sweep(count, load, store):
    high_unit, side, low_unit = load(count - 1)
    store(count - 1, side, low_unit, high_unit)
    for i in range(count - 2, -1, -1):
        ratio, side_scaled, unit_scaled = load(i)
        side = side_scaled + ratio * side
        low_unit = unit_scaled + ratio * low_unit
        high_unit = ratio * high_unit
        store(i, side, low_unit, high_unit)


def interface_fluxes(received, count, half):
    first_side, last_side, first_unit, cross, last_unit, g_first, g_last = [received(j) for j in range(FIELDS)]
    index = lax.broadcasted_iota(jnp.int32, (count, NX), 0)

    def following(field):
        return pltpu.roll(field, count - 1, 0)

    weight = HALF_K * (g_last + following(g_first))
    diag = recip(weight) + last_unit + following(first_unit)
    side = last_side - following(first_side)
    diag = jnp.where(index < count - 1, diag, 1.0)
    side = jnp.where(index < count - 1, side, 0.0)
    coupling = jnp.where(index < count - 2, following(cross), 0.0)
    return pcr(diag, coupling, side, count, 0)


def diffuse_and_route_kernel(
    volume_hbm,
    owners_hbm,
    out_ref,
    routed_ref,
    volume_ref,
    middle,
    z_halo,
    y_halo_out,
    y_halo,
    g_ref,
    z_keep,
    y_keep,
    natural,
    base,
    z_out,
    z_in,
    y_out,
    y_in,
    z_back_out,
    z_back,
    y_back_out,
    y_back,
    halo_send,
    halo_recv,
    z_send,
    z_recv,
    y_send,
    y_recv,
    zb_send,
    zb_recv,
    yb_send,
    yb_recv,
    owners_ref,
    owners_sem,
    codes_out,
    codes_in,
    codes,
    gathered,
    packed,
    volume_sem,
    codes_send,
    codes_recv,
    codes_sem,
    own_sem,
    gather_send,
    gather_recv,
    spread_send,
    spread_recv,
):
    load_volume = pltpu.make_async_copy(volume_hbm, volume_ref, volume_sem)
    load_volume.start()
    load_owners = pltpu.make_async_copy(owners_hbm, owners_ref, owners_sem)
    load_owners.start()
    gz = lax.axis_index("gz")
    xy = lax.axis_index("xy")
    z_targets = [
        lax.rem(gz // 4 + dz, 4) * 4 + lax.rem(lax.rem(gz, 4) + dy, 4) for dz, dy in Z_PEERS
    ]
    y_targets = [
        lax.rem(xy // 2 + dx, 4) * 2 + lax.rem(lax.rem(xy, 2) + core, 2) for dx, core in Y_PEERS
    ]
    barrier = pltpu.get_barrier_semaphore()
    for target in z_targets:
        pl.semaphore_signal(barrier, 1, device_id={"gz": target}, device_id_type=MESH)
    for target in y_targets:
        pl.semaphore_signal(barrier, 1, device_id={"xy": target}, device_id_type=MESH)
    pl.semaphore_wait(barrier, N_GZ + N_XY - 2)

    chip_z, chip_y = gz // 4, lax.rem(gz, 4)
    places = [chip_y, chip_z]

    def partner(way, offset):
        if way == 0:
            return chip_z * 4 + lax.rem(chip_y + offset, 4)
        return lax.rem(chip_z + offset, 4) * 4 + chip_y

    load_owners.wait()
    lanes = lax.broadcasted_iota(jnp.int32, (8, NX), 1)
    code_tile = jnp.zeros((8, NX), jnp.int32)
    for b in range(BLOCKS_HERE):
        rank = 0
        for earlier in range(b):
            rank = rank + (owners_ref[earlier] == owners_ref[b]).astype(jnp.int32)
        code_tile = jnp.where(lanes == b, owners_ref[b] * MOST + rank, code_tile)
    codes_out[...] = code_tile
    for way in range(2):
        codes_in[way, places[way]] = code_tile
        for offset in (2, 1, 3):
            pltpu.make_async_remote_copy(
                codes_out, codes_in.at[way, places[way]], codes_send.at[way], codes_recv.at[way],
                device_id={"gz": partner(way, offset)}, device_id_type=MESH,
            ).start()
    load_volume.wait()

    row_index = lax.broadcasted_iota(jnp.int32, (CY, NX), 0)
    lane_index = lax.broadcasted_iota(jnp.int32, (CY, NX), 1)

    def send_all(source, landing, send_sem, recv_sem, axis, targets, me):
        for target in targets:
            pltpu.make_async_remote_copy(
                source.at[target], landing.at[me], send_sem, recv_sem,
                device_id={axis: target}, device_id_type=MESH,
            ).start()

    def wait_all(buffer, count, semaphore):
        part = buffer.at[pl.ds(0, count)]
        pltpu.make_async_copy(part, part, semaphore).wait()

    for step in range(STEPS):
        v = volume_ref if step == 0 else middle
        new = out_ref if step == STEPS - 1 else middle

        y_halo_out[step, 0] = v[pl.ds(0, CZ, stride=CY), :]
        y_halo_out[step, 1] = v[pl.ds(CY - 1, CZ, stride=CY), :]
        copies = []
        for k, (axis, me, count, forward) in enumerate(
            [("gz", gz, N_GZ, 0), ("gz", gz, N_GZ, 1), ("xy", xy, N_XY, 0), ("xy", xy, N_XY, 1)]
        ):
            target = lax.rem(me + (1 if forward else count - 1), count)
            if axis == "gz":
                source = v.at[pl.ds((CZ - 1) * CY if forward else 0, CY)]
                landing = z_halo.at[step, 1 - forward]
            else:
                source = y_halo_out.at[step, forward]
                landing = y_halo.at[step, 1 - forward]
            copies.append(
                pltpu.make_async_remote_copy(
                    source, landing, halo_send.at[step, k], halo_recv.at[step, k],
                    device_id={axis: target}, device_id_type=MESH,
                )
            )
        for copy in copies:
            copy.start()
        for copy in copies:
            copy.wait_recv()

        def plane(i):
            return v[i * CY : (i + 1) * CY, :]

        before = jnp.where(gz == 0, plane(0), z_halo[step, 0])
        after = jnp.where(gz == N_GZ - 1, plane(CZ - 1), z_halo[step, 1])
        here = plane(0)
        for i in range(CZ):
            above = plane(i + 1) if i < CZ - 1 else after
            slope_z = above - before
            y_low = jnp.where(xy == 0, here[0:1, :], y_halo[step, 0, i : i + 1, :])
            y_high = jnp.where(xy == N_XY - 1, here[CY - 1 : CY, :], y_halo[step, 1, i : i + 1, :])
            y_prev = jnp.where(row_index == 0, y_low, pltpu.roll(here, 1, 0))
            y_next = jnp.where(row_index == CY - 1, y_high, pltpu.roll(here, CY - 1, 0))
            slope_y = y_next - y_prev
            x_prev = jnp.where(lane_index == 0, here, pltpu.roll(here, 1, 1))
            x_next = jnp.where(lane_index == NX - 1, here, pltpu.roll(here, NX - 1, 1))
            slope_x = x_next - x_prev
            squares = slope_z * slope_z + slope_y * slope_y + slope_x * slope_x
            g_ref[i * CY : (i + 1) * CY, :] = recip(1.0 + squares * (0.25 / CONTRAST))
            before, here = here, above

        def z_store(i, ratio, side, unit):
            z_keep[0, i] = ratio
            z_keep[1, i] = side
            z_keep[2, i] = unit

        ends = forward_sweep(CZ, plane, lambda i: g_ref[i * CY : (i + 1) * CY, :], z_store)
        for j, field in enumerate(ends):
            for half in range(2):
                z_out[step, pl.ds(2 * j + half, N_GZ, stride=16), :] = field[half * N_GZ : (half + 1) * N_GZ, :]
        z_in_blocks = z_in.at[step].reshape(N_GZ, 16, NX)
        z_out_blocks = z_out.at[step].reshape(N_GZ, 16, NX)
        send_all(z_out_blocks, z_in_blocks, z_send.at[step], z_recv.at[step], "gz", z_targets, gz)

        def y_store(i, ratio, side, unit):
            y_keep[0, i] = ratio
            y_keep[1, i] = side
            y_keep[2, i] = unit

        ends = forward_sweep(
            CY,
            lambda i: v[pl.ds(i, CZ, stride=CY), :],
            lambda i: g_ref[pl.ds(i, CZ, stride=CY), :],
            y_store,
        )
        for j, field in enumerate(ends):
            for half in range(2):
                y_out[step, pl.ds(2 * j + half, N_XY, stride=16), :] = field[half * N_XY : (half + 1) * N_XY, :]
        y_in_blocks = y_in.at[step].reshape(N_XY, 16, NX)
        y_out_blocks = y_out.at[step].reshape(N_XY, 16, NX)
        send_all(y_out_blocks, y_in_blocks, y_send.at[step], y_recv.at[step], "xy", y_targets, xy)
        z_in_blocks[gz] = z_out_blocks[gz]
        y_in_blocks[xy] = y_out_blocks[xy]

        def solve_x(i, carry):
            rows = pl.ds(pl.multiple_of(i * 2 * CY, 2 * CY), 2 * CY)
            g = g_ref[rows, :]
            lanes = lax.broadcasted_iota(jnp.int32, (2 * CY, NX), 1)
            weight = jnp.where(lanes < NX - 1, HALF_K * (g + pltpu.roll(g, NX - 1, 1)), 0.0)
            diag = 1.0 + weight + pltpu.roll(weight, 1, 1)
            base[rows, :] = pcr(diag, weight, v[rows, :], NX, 1)
            return carry

        lax.fori_loop(0, CZ // 4, solve_x, 0)

        def z_load(i):
            return z_keep[0, i], z_keep[1, i], z_keep[2, i]

        def z_restore(i, side, low, high):
            natural[3, i * CY : (i + 1) * CY, :] = side
            z_keep[1, i] = low
            z_keep[2, i] = high

        backward_sweep(CZ, z_load, z_restore)

        def y_load(i):
            return y_keep[0, i], y_keep[1, i], y_keep[2, i]

        def y_restore(i, side, low, high):
            rows = pl.ds(i, CZ, stride=CY)
            natural[0, rows, :] = side
            natural[1, rows, :] = low
            natural[2, rows, :] = high

        backward_sweep(CY, y_load, y_restore)

        wait_all(z_in_blocks, N_GZ - 1, z_recv.at[step])
        zb_out = z_back_out.at[step].reshape(N_GZ, 8, NX)
        zb_in = z_back.at[step].reshape(N_GZ, 8, NX)
        for half in range(2):
            flux = interface_fluxes(
                lambda j: z_in[step, pl.ds(2 * j + half, N_GZ, stride=16), :], N_GZ, half
            )
            z_back_out[step, pl.ds(half, N_GZ, stride=8), :] = pltpu.roll(flux, 1, 0)
            z_back_out[step, pl.ds(2 + half, N_GZ, stride=8), :] = flux
        send_all(zb_out, zb_in, zb_send.at[step], zb_recv.at[step], "gz", z_targets, gz)
        zb_in[gz] = zb_out[gz]

        wait_all(y_in_blocks, N_XY - 1, y_recv.at[step])
        yb_out = y_back_out.at[step].reshape(N_XY, 8, NX)
        yb_in = y_back.at[step].reshape(N_XY, 8, NX)
        for half in range(2):
            flux = interface_fluxes(
                lambda j: y_in[step, pl.ds(2 * j + half, N_XY, stride=16), :], N_XY, half
            )
            y_back_out[step, pl.ds(half, N_XY, stride=8), :] = pltpu.roll(flux, 1, 0)
            y_back_out[step, pl.ds(2 + half, N_XY, stride=8), :] = flux
        send_all(yb_out, yb_in, yb_send.at[step], yb_recv.at[step], "xy", y_targets, xy)
        yb_in[xy] = yb_out[xy]

        lax.fori_loop(CZ // 4, CZ // 2, solve_x, 0)
        wait_all(yb_in, N_XY - 1, yb_recv.at[step])
        wait_all(zb_in, N_GZ - 1, zb_recv.at[step])
        low_z = jnp.concatenate([z_back[step, pl.ds(h, N_GZ, stride=8), :] for h in (0, 1)], axis=0)
        high_z = jnp.concatenate([z_back[step, pl.ds(2 + h, N_GZ, stride=8), :] for h in (0, 1)], axis=0)
        for i in range(CZ):
            rows = slice(i * CY, (i + 1) * CY)
            at = (i % N_XY) * 8 + i // N_XY
            low_y = y_back[step, at : at + 1, :]
            high_y = y_back[step, at + 2 : at + 3, :]
            total = base[rows, :] + natural[0, rows, :] + natural[3, rows, :]
            total = total + (low_z * z_keep[1, i] - high_z * z_keep[2, i])
            total = total + (low_y * natural[1, rows, :] - high_y * natural[2, rows, :])
            new[rows, :] = total * (1.0 / 3.0)

    for way in range(2):
        wait_all(codes_in.at[way], 3, codes_recv.at[way])
    to_scalars = pltpu.make_async_copy(codes_in, codes, codes_sem)
    to_scalars.start()
    blocks = out_ref.reshape(BLOCKS_HERE, BLOCK_ROWS, NX)
    for chunk in range(CHUNKS):
        for way in range(2):
            here = pl.ds(way * HALF_ROWS + chunk * CHUNK_ROWS, CHUNK_ROWS)
            for offset in (2, 1, 3):
                pltpu.make_async_remote_copy(
                    blocks.at[:, here, :], gathered[way][chunk].at[places[way]],
                    gather_send.at[chunk, way], gather_recv.at[chunk, way],
                    device_id={"gz": partner(way, offset)}, device_id_type=MESH,
                ).start()
    for way in range(2):
        for chunk in range(CHUNKS):
            here = pl.ds(way * HALF_ROWS + chunk * CHUNK_ROWS, CHUNK_ROWS)
            gathered[way][chunk][places[way]] = blocks[:, here, :]
    to_scalars.wait()
    choice = {}
    for way in range(2):
        for offset in range(4):
            target = partner(1 - way, offset)
            for source in range(4):
                for rank in range(MOST):
                    index, found = 0, 0
                    for b in range(BLOCKS_HERE):
                        hit = (codes[way, source, 0, b] == target * MOST + rank).astype(jnp.int32)
                        index = index + b * hit
                        found = found + hit
                    choice[way, offset, source, rank] = index, found
    for chunk in range(CHUNKS):
        for way in range(2):
            there = pl.ds(chunk * CHUNK_ROWS, CHUNK_ROWS)
            final = pl.ds(way * HALF_ROWS + chunk * CHUNK_ROWS, CHUNK_ROWS)
            wait_all(gathered[way][chunk], 3, gather_recv.at[chunk, way])
            for offset in (2, 1, 3, 0):
                for source in range(4):
                    for rank in range(MOST):
                        index, found = choice[way, offset, source, rank]
                        rows = gathered[way][chunk][source, index]
                        packed[way, offset, source, rank, there, :] = jnp.where(found > 0, rows, 0.0)
                landing = routed_ref.at[chip_z, :, :, final, :] if way == 0 else routed_ref.at[:, chip_y, :, final, :]
                if offset:
                    pltpu.make_async_remote_copy(
                        packed.at[way, offset, :, :, there, :], landing,
                        spread_send.at[chunk, way], spread_recv.at[chunk, way],
                        device_id={"gz": partner(1 - way, offset)}, device_id_type=MESH,
                    ).start()
                else:
                    pltpu.make_async_copy(
                        packed.at[way, offset, :, :, there, :], landing, own_sem.at[chunk, way]
                    ).start()
    for chunk in range(CHUNKS):
        for way in range(2):
            there = pl.ds(chunk * CHUNK_ROWS, CHUNK_ROWS)
            part = packed.at[way, pl.ds(0, 3), :, :, there, :]
            pltpu.make_async_copy(part, part, spread_recv.at[chunk, way]).wait()
            pltpu.make_async_copy(part, part, spread_send.at[chunk, way]).wait()
            part = packed.at[way, 0, :, :, there, :]
            pltpu.make_async_copy(part, part, own_sem.at[chunk, way]).wait()
            wait_all(gathered[way][chunk], 3, gather_send.at[chunk, way])
    for way in range(2):
        wait_all(codes_in.at[way], 3, codes_send.at[way])
    for step in range(STEPS):
        v = volume_ref if step == 0 else middle
        for k in range(4):
            part = v.at[pl.ds(0, CY)] if k < 2 else y_halo_out.at[step, 0]
            pltpu.make_async_copy(part, part, halo_send.at[step, k]).wait()
        wait_all(z_out.at[step].reshape(N_GZ, 16, NX), N_GZ - 1, z_send.at[step])
        wait_all(y_out.at[step].reshape(N_XY, 16, NX), N_XY - 1, y_send.at[step])
        wait_all(z_back_out.at[step].reshape(N_GZ, 8, NX), N_GZ - 1, zb_send.at[step])
        wait_all(y_back_out.at[step].reshape(N_XY, 8, NX), N_XY - 1, yb_send.at[step])


def vmem(*shape):
    return pltpu.VMEM(shape, jnp.float32)


def diffuse_and_route(volume, owners):
    dma = pltpu.SemaphoreType.DMA
    return pl.pallas_call(
        diffuse_and_route_kernel,
        out_shape=(
            jax.ShapeDtypeStruct((ROWS, NX), jnp.float32),
            jax.ShapeDtypeStruct((4, 4, MOST, BLOCK_ROWS, NX), jnp.float32),
        ),
        in_specs=[
            pl.BlockSpec(memory_space=pltpu.HBM),
            pl.BlockSpec(memory_space=pltpu.HBM),
        ],
        out_specs=(pl.BlockSpec(memory_space=pltpu.VMEM), pl.BlockSpec(memory_space=pl.ANY)),
        scratch_shapes=[
            vmem(ROWS, NX),
            vmem(ROWS, NX),
            vmem(STEPS, 2, CY, NX),
            vmem(STEPS, 2, CZ, NX),
            vmem(STEPS, 2, CZ, NX),
            vmem(ROWS, NX),
            vmem(3, CZ, CY, NX),
            vmem(3, CY, CZ, NX),
            vmem(4, ROWS, NX),
            vmem(ROWS, NX),
            vmem(STEPS, N_GZ * 16, NX),
            vmem(STEPS, N_GZ * 16, NX),
            vmem(STEPS, N_XY * 16, NX),
            vmem(STEPS, N_XY * 16, NX),
            vmem(STEPS, N_GZ * 8, NX),
            vmem(STEPS, N_GZ * 8, NX),
            vmem(STEPS, N_XY * 8, NX),
            vmem(STEPS, N_XY * 8, NX),
            dma((STEPS, 4)),
            dma((STEPS, 4)),
        ]
        + [dma((STEPS,))] * 8
        + [
            pltpu.SMEM((BLOCKS_HERE,), jnp.int32),
            dma,
            pltpu.VMEM((8, NX), jnp.int32),
            pltpu.VMEM((2, 4, 8, NX), jnp.int32),
            pltpu.SMEM((2, 4, 8, NX), jnp.int32),
            [[vmem(4, BLOCKS_HERE, CHUNK_ROWS, NX) for _ in range(CHUNKS)] for _ in range(2)],
            vmem(2, 4, 4, MOST, HALF_ROWS, NX),
            dma,
            dma((2,)),
            dma((2,)),
            dma,
        ]
        + [dma((CHUNKS, 2))] * 5,
        compiler_params=pltpu.CompilerParams(
            collective_id=0, has_side_effects=True, vmem_limit_bytes=48 << 20
        ),
    )(volume, owners)


def on_device(volume, owners):
    depth, height, width = volume.shape
    field, routed = diffuse_and_route(volume.reshape(depth * height, width), owners.reshape(-1))
    return (field.reshape(volume.shape), routed.reshape(1, N_GZ * MOST, BLOCK_ROWS, width))


def solution(mesh):
    in_specs = (P("gz", "xy", None), P("xy", "gz", None))
    out_specs = (P("gz", "xy", None), P("xy", "gz", None, None))
    return jax.shard_map(
        on_device, mesh=mesh, in_specs=in_specs, out_specs=out_specs, check_vma=False
    )
```

```python
import jax
import jax.numpy as jnp
from jax import lax
from jax.experimental import pallas as pl
from jax.experimental.pallas import tpu as pltpu
from jax.sharding import PartitionSpec as P

STEPS = 2
MOST = 2
BLOCK_ROWS = 128

TIME_STEP = 30.0
CONTRAST = 4.0
HALF_K = 1.5 * TIME_STEP

CZ = 16
CY = 32
NX = 128
ROWS = CZ * CY
N_GZ = 16
N_XY = 8
FIELDS = 7
Z_OWNERS = 8
Y_OWNERS = 4
LINES = 4
BLOCKS_HERE = 4
HALF_ROWS = BLOCK_ROWS // 2
CHUNKS = 2
X_FIRST = 4
CHUNK_ROWS = HALF_ROWS // CHUNKS
MESH = pl.DeviceIdType.MESH

Z_PEERS = sorted(
    [(a, b) for a in range(4) for b in range(4) if (a, b) != (0, 0)],
    key=lambda p: -(min(p[0], 4 - p[0]) + min(p[1], 4 - p[1])),
)
Y_PEERS = sorted(
    [(a, b) for a in range(4) for b in range(2) if (a, b) != (0, 0)],
    key=lambda p: -(2 * min(p[0], 4 - p[0]) + p[1]),
)


def recip(value):
    return 1.0 / value


def pcr(diag, coupling, side, count, axis):
    stride = 1
    while stride < count:
        inverse = recip(diag)
        scaled = coupling * inverse
        side_scaled = side * inverse
        side = (
            side
            + pltpu.roll(coupling * side_scaled, stride, axis)
            + coupling * pltpu.roll(side_scaled, count - stride, axis)
        )
        diag = (
            diag
            - pltpu.roll(coupling * scaled, stride, axis)
            - coupling * coupling * pltpu.roll(inverse, count - stride, axis)
        )
        stride *= 2
        if stride < count:
            coupling = coupling * pltpu.roll(scaled, count - stride // 2, axis)
    return side * recip(diag)


def forward_sweep(count, load_v, load_g, store):
    g_here = load_g(0)
    g_first = g_here
    total = jnp.ones_like(g_here)
    side = load_v(0)
    unit = jnp.ones_like(g_here)
    first_side = jnp.zeros_like(g_here)
    first_unit = jnp.zeros_like(g_here)
    for i in range(count - 1):
        g_next = load_g(i + 1)
        weight = HALF_K * (g_here + g_next)
        inverse = recip(total + weight)
        ratio = weight * inverse
        side_scaled = side * inverse
        unit_scaled = unit * inverse
        store(i, ratio, side_scaled, unit_scaled)
        first_side = first_side + unit * side_scaled
        first_unit = first_unit + unit * unit_scaled
        total = 1.0 + ratio * total
        side = load_v(i + 1) + ratio * side
        unit = ratio * unit
        g_here = g_next
    inverse = recip(total)
    last_side = side * inverse
    last_unit = unit * inverse
    store(count - 1, inverse, last_side, last_unit)
    first_side = first_side + unit * last_side
    first_unit = first_unit + unit * last_unit
    return (first_side, last_side, first_unit, last_unit, inverse, g_first, g_here)


def backward_sweep(count, load, store):
    high_unit, side, low_unit = load(count - 1)
    store(count - 1, side, low_unit, high_unit)
    for i in range(count - 2, -1, -1):
        ratio, side_scaled, unit_scaled = load(i)
        side = side_scaled + ratio * side
        low_unit = unit_scaled + ratio * low_unit
        high_unit = ratio * high_unit
        store(i, side, low_unit, high_unit)


def interface_fluxes(received, count):
    first_side, last_side, first_unit, cross, last_unit, g_first, g_last = [received(j) for j in range(FIELDS)]
    index = lax.broadcasted_iota(jnp.int32, (count, NX), 0)

    def following(field):
        return pltpu.roll(field, count - 1, 0)

    weight = HALF_K * (g_last + following(g_first))
    diag = recip(weight) + last_unit + following(first_unit)
    side = last_side - following(first_side)
    diag = jnp.where(index < count - 1, diag, 1.0)
    side = jnp.where(index < count - 1, side, 0.0)
    coupling = jnp.where(index < count - 2, following(cross), 0.0)
    return pcr(diag, coupling, side, count, 0)


def diffuse_and_route_kernel(
    volume_hbm,
    owners_hbm,
    out_ref,
    routed_ref,
    volume_ref,
    middle,
    z_halo,
    y_halo_out,
    y_halo,
    g_ref,
    z_keep,
    y_keep,
    natural,
    base,
    z_out,
    z_in,
    y_out,
    y_in,
    z_back_out,
    z_back,
    y_back_out,
    y_back,
    halo_send,
    halo_recv,
    z_send,
    z_recv,
    y_send,
    y_recv,
    zb_send,
    zb_recv,
    yb_send,
    yb_recv,
    owners_ref,
    owners_sem,
    codes_out,
    codes_in,
    codes,
    gathered,
    packed,
    volume_sem,
    codes_send,
    codes_recv,
    codes_sem,
    own_sem,
    gather_send,
    gather_recv,
    spread_send,
    spread_recv,
):
    load_volume = pltpu.make_async_copy(volume_hbm, volume_ref, volume_sem)
    load_volume.start()
    load_owners = pltpu.make_async_copy(owners_hbm, owners_ref, owners_sem)
    load_owners.start()
    gz = lax.axis_index("gz")
    xy = lax.axis_index("xy")
    z_targets = [
        lax.rem(gz // 4 + dz, 4) * 4 + lax.rem(lax.rem(gz, 4) + dy, 4) for dz, dy in Z_PEERS
    ]
    y_targets = [
        lax.rem(xy // 2 + dx, 4) * 2 + lax.rem(lax.rem(xy, 2) + core, 2) for dx, core in Y_PEERS
    ]
    odd = lax.rem(gz + xy, 2)
    joins_z = odd == 0
    joins_y = odd == 1
    z_owners = [
        (lax.rem(gz // 4 + dz, 4) * 4 + lax.rem(lax.rem(gz, 4) + dy + odd, 4), (dz, dy) == (0, 0))
        for dz, dy in ((2, 2), (1, 2), (3, 2), (2, 0), (1, 0), (3, 0), (0, 2), (0, 0))
    ]
    y_owners = [
        (lax.rem(xy // 2 + dx, 4) * 2 + lax.rem(lax.rem(xy, 2) + 1 - odd, 2), dx == 0) for dx in (2, 1, 3, 0)
    ]
    barrier = pltpu.get_barrier_semaphore()
    for target in z_targets:
        pl.semaphore_signal(barrier, 1, device_id={"gz": target}, device_id_type=MESH)
    for target in y_targets:
        pl.semaphore_signal(barrier, 1, device_id={"xy": target}, device_id_type=MESH)
    pl.semaphore_wait(barrier, N_GZ + N_XY - 2)

    chip_z, chip_y = gz // 4, lax.rem(gz, 4)
    places = [chip_y, chip_z]

    def partner(way, offset):
        if way == 0:
            return chip_z * 4 + lax.rem(chip_y + offset, 4)
        return lax.rem(chip_z + offset, 4) * 4 + chip_y

    load_owners.wait()
    lanes = lax.broadcasted_iota(jnp.int32, (8, NX), 1)
    code_tile = jnp.zeros((8, NX), jnp.int32)
    for b in range(BLOCKS_HERE):
        rank = 0
        for earlier in range(b):
            rank = rank + (owners_ref[earlier] == owners_ref[b]).astype(jnp.int32)
        code_tile = jnp.where(lanes == b, owners_ref[b] * MOST + rank, code_tile)
    codes_out[...] = code_tile
    for way in range(2):
        codes_in[way, places[way]] = code_tile
        for offset in (2, 1, 3):
            pltpu.make_async_remote_copy(
                codes_out, codes_in.at[way, places[way]], codes_send.at[way], codes_recv.at[way],
                device_id={"gz": partner(way, offset)}, device_id_type=MESH,
            ).start()
    load_volume.wait()

    row_index = lax.broadcasted_iota(jnp.int32, (CY, NX), 0)
    lane_index = lax.broadcasted_iota(jnp.int32, (CY, NX), 1)

    def send_all(source, landing, send_sem, recv_sem, axis, targets, me):
        for target in targets:
            pltpu.make_async_remote_copy(
                source.at[target], landing.at[me], send_sem, recv_sem,
                device_id={axis: target}, device_id_type=MESH,
            ).start()

    def send_parts(source, landing, send_sem, recv_sem, axis, owners, me, is_owner):
        for target, may_be_self in owners:
            copy = pltpu.make_async_remote_copy(
                source.at[target // 2], landing.at[me], send_sem, recv_sem,
                device_id={axis: target}, device_id_type=MESH,
            )
            if may_be_self:
                pl.when(jnp.logical_not(is_owner))(copy.start)

                @pl.when(is_owner)
                def _():
                    landing[me] = source[target // 2]

            else:
                copy.start()

    def wait_parts(buffer, count, semaphore, is_owner):
        @pl.when(is_owner)
        def _():
            wait_all(buffer, count - 1, semaphore)

        @pl.when(jnp.logical_not(is_owner))
        def _():
            wait_all(buffer, count, semaphore)

    def wait_all(buffer, count, semaphore):
        part = buffer.at[pl.ds(0, count)]
        pltpu.make_async_copy(part, part, semaphore).wait()

    for step in range(STEPS):
        v = volume_ref if step == 0 else middle
        new = out_ref if step == STEPS - 1 else middle

        y_halo_out[step, 0] = v[pl.ds(0, CZ, stride=CY), :]
        y_halo_out[step, 1] = v[pl.ds(CY - 1, CZ, stride=CY), :]
        copies = []
        for k, (axis, me, count, forward) in enumerate(
            [("gz", gz, N_GZ, 0), ("gz", gz, N_GZ, 1), ("xy", xy, N_XY, 0), ("xy", xy, N_XY, 1)]
        ):
            target = lax.rem(me + (1 if forward else count - 1), count)
            if axis == "gz":
                source = v.at[pl.ds((CZ - 1) * CY if forward else 0, CY)]
                landing = z_halo.at[step, 1 - forward]
            else:
                source = y_halo_out.at[step, forward]
                landing = y_halo.at[step, 1 - forward]
            copies.append(
                pltpu.make_async_remote_copy(
                    source, landing, halo_send.at[step, k], halo_recv.at[step, k],
                    device_id={axis: target}, device_id_type=MESH,
                )
            )
        for copy in copies:
            copy.start()
        for copy in copies:
            copy.wait_recv()

        def plane(i):
            return v[i * CY : (i + 1) * CY, :]

        before = jnp.where(gz == 0, plane(0), z_halo[step, 0])
        after = jnp.where(gz == N_GZ - 1, plane(CZ - 1), z_halo[step, 1])
        here = plane(0)
        for i in range(CZ):
            above = plane(i + 1) if i < CZ - 1 else after
            slope_z = above - before
            y_low = jnp.where(xy == 0, here[0:1, :], y_halo[step, 0, i : i + 1, :])
            y_high = jnp.where(xy == N_XY - 1, here[CY - 1 : CY, :], y_halo[step, 1, i : i + 1, :])
            y_prev = jnp.where(row_index == 0, y_low, pltpu.roll(here, 1, 0))
            y_next = jnp.where(row_index == CY - 1, y_high, pltpu.roll(here, CY - 1, 0))
            slope_y = y_next - y_prev
            x_prev = jnp.where(lane_index == 0, here, pltpu.roll(here, 1, 1))
            x_next = jnp.where(lane_index == NX - 1, here, pltpu.roll(here, NX - 1, 1))
            slope_x = x_next - x_prev
            squares = slope_z * slope_z + slope_y * slope_y + slope_x * slope_x
            g_ref[i * CY : (i + 1) * CY, :] = recip(1.0 + squares * (0.25 / CONTRAST))
            before, here = here, above

        def z_store(i, ratio, side, unit):
            z_keep[0, i] = ratio
            z_keep[1, i] = side
            z_keep[2, i] = unit

        ends = forward_sweep(CZ, plane, lambda i: g_ref[i * CY : (i + 1) * CY, :], z_store)
        for j, field in enumerate(ends):
            for h in range(LINES):
                z_out[step, pl.ds(LINES * j + h, Z_OWNERS, stride=32), :] = field[h * Z_OWNERS : (h + 1) * Z_OWNERS, :]
        z_in_blocks = z_in.at[step].reshape(N_GZ, 32, NX)
        z_out_blocks = z_out.at[step].reshape(Z_OWNERS, 32, NX)
        send_parts(z_out_blocks, z_in_blocks, z_send.at[step], z_recv.at[step], "gz", z_owners, gz, joins_z)

        def y_store(i, ratio, side, unit):
            y_keep[0, i] = ratio
            y_keep[1, i] = side
            y_keep[2, i] = unit

        ends = forward_sweep(
            CY,
            lambda i: v[pl.ds(i, CZ, stride=CY), :],
            lambda i: g_ref[pl.ds(i, CZ, stride=CY), :],
            y_store,
        )
        for j, field in enumerate(ends):
            for h in range(LINES):
                y_out[step, pl.ds(LINES * j + h, Y_OWNERS, stride=32), :] = field[h * Y_OWNERS : (h + 1) * Y_OWNERS, :]
        y_in_blocks = y_in.at[step].reshape(N_XY, 32, NX)
        y_out_blocks = y_out.at[step].reshape(Y_OWNERS, 32, NX)
        send_parts(y_out_blocks, y_in_blocks, y_send.at[step], y_recv.at[step], "xy", y_owners, xy, joins_y)

        def solve_x(i, carry):
            rows = pl.ds(pl.multiple_of(i * 2 * CY, 2 * CY), 2 * CY)
            g = g_ref[rows, :]
            lanes = lax.broadcasted_iota(jnp.int32, (2 * CY, NX), 1)
            weight = jnp.where(lanes < NX - 1, HALF_K * (g + pltpu.roll(g, NX - 1, 1)), 0.0)
            diag = 1.0 + weight + pltpu.roll(weight, 1, 1)
            base[rows, :] = pcr(diag, weight, v[rows, :], NX, 1)
            return carry

        lax.fori_loop(0, X_FIRST, solve_x, 0)

        def z_load(i):
            return z_keep[0, i], z_keep[1, i], z_keep[2, i]

        def z_restore(i, side, low, high):
            natural[3, i * CY : (i + 1) * CY, :] = side
            z_keep[1, i] = low
            z_keep[2, i] = high

        backward_sweep(CZ, z_load, z_restore)

        def y_load(i):
            return y_keep[0, i], y_keep[1, i], y_keep[2, i]

        def y_restore(i, side, low, high):
            rows = pl.ds(i, CZ, stride=CY)
            natural[0, rows, :] = side
            natural[1, rows, :] = low
            natural[2, rows, :] = high

        backward_sweep(CY, y_load, y_restore)

        zb_out = z_back_out.at[step].reshape(N_GZ, 8, NX)
        zb_in = z_back.at[step].reshape(Z_OWNERS, 8, NX)
        yb_out = y_back_out.at[step].reshape(N_XY, 8, NX)
        yb_in = y_back.at[step].reshape(Y_OWNERS, 8, NX)

        @pl.when(joins_z)
        def _():
            wait_all(z_in_blocks, N_GZ - 1, z_recv.at[step])
            for h in range(LINES):
                flux = interface_fluxes(
                    lambda j: z_in[step, pl.ds(LINES * j + h, N_GZ, stride=32), :], N_GZ
                )
                z_back_out[step, pl.ds(h, N_GZ, stride=8), :] = pltpu.roll(flux, 1, 0)
                z_back_out[step, pl.ds(LINES + h, N_GZ, stride=8), :] = flux
            send_all(zb_out, zb_in, zb_send.at[step], zb_recv.at[step], "gz", z_targets, gz // 2)
            zb_in[gz // 2] = zb_out[gz]

        @pl.when(joins_y)
        def _():
            wait_all(y_in_blocks, N_XY - 1, y_recv.at[step])
            for h in range(LINES):
                flux = interface_fluxes(
                    lambda j: y_in[step, pl.ds(LINES * j + h, N_XY, stride=32), :], N_XY
                )
                y_back_out[step, pl.ds(h, N_XY, stride=8), :] = pltpu.roll(flux, 1, 0)
                y_back_out[step, pl.ds(LINES + h, N_XY, stride=8), :] = flux
            send_all(yb_out, yb_in, yb_send.at[step], yb_recv.at[step], "xy", y_targets, xy // 2)
            yb_in[xy // 2] = yb_out[xy]

        lax.fori_loop(X_FIRST, CZ // 2, solve_x, 0)
        wait_parts(yb_in, Y_OWNERS, yb_recv.at[step], joins_y)
        wait_parts(zb_in, Z_OWNERS, zb_recv.at[step], joins_z)
        low_z = jnp.concatenate([z_back[step, pl.ds(h, Z_OWNERS, stride=8), :] for h in range(LINES)], axis=0)
        high_z = jnp.concatenate(
            [z_back[step, pl.ds(LINES + h, Z_OWNERS, stride=8), :] for h in range(LINES)], axis=0
        )
        for i in range(CZ):
            rows = slice(i * CY, (i + 1) * CY)
            at = (i % Y_OWNERS) * 8 + i // Y_OWNERS
            low_y = y_back[step, at : at + 1, :]
            high_y = y_back[step, at + LINES : at + LINES + 1, :]
            total = base[rows, :] + natural[0, rows, :] + natural[3, rows, :]
            total = total + (low_z * z_keep[1, i] - high_z * z_keep[2, i])
            total = total + (low_y * natural[1, rows, :] - high_y * natural[2, rows, :])
            new[rows, :] = total * (1.0 / 3.0)

    for way in range(2):
        wait_all(codes_in.at[way], 3, codes_recv.at[way])
    to_scalars = pltpu.make_async_copy(codes_in, codes, codes_sem)
    to_scalars.start()
    blocks = out_ref.reshape(BLOCKS_HERE, BLOCK_ROWS, NX)
    for chunk in range(CHUNKS):
        for way in range(2):
            here = pl.ds(way * HALF_ROWS + chunk * CHUNK_ROWS, CHUNK_ROWS)
            for offset in (2, 1, 3):
                pltpu.make_async_remote_copy(
                    blocks.at[:, here, :], gathered[way][chunk].at[places[way]],
                    gather_send.at[chunk, way], gather_recv.at[chunk, way],
                    device_id={"gz": partner(way, offset)}, device_id_type=MESH,
                ).start()
    for way in range(2):
        for chunk in range(CHUNKS):
            here = pl.ds(way * HALF_ROWS + chunk * CHUNK_ROWS, CHUNK_ROWS)
            gathered[way][chunk][places[way]] = blocks[:, here, :]
    to_scalars.wait()
    choice = {}
    for way in range(2):
        for offset in range(4):
            target = partner(1 - way, offset)
            for source in range(4):
                for rank in range(MOST):
                    index, found = 0, 0
                    for b in range(BLOCKS_HERE):
                        hit = (codes[way, source, 0, b] == target * MOST + rank).astype(jnp.int32)
                        index = index + b * hit
                        found = found + hit
                    choice[way, offset, source, rank] = index, found
    for chunk in range(CHUNKS):
        for way in range(2):
            there = pl.ds(chunk * CHUNK_ROWS, CHUNK_ROWS)
            final = pl.ds(way * HALF_ROWS + chunk * CHUNK_ROWS, CHUNK_ROWS)
            wait_all(gathered[way][chunk], 3, gather_recv.at[chunk, way])
            for offset in (2, 1, 3, 0):
                for source in range(4):
                    for rank in range(MOST):
                        index, found = choice[way, offset, source, rank]
                        rows = gathered[way][chunk][source, index]
                        packed[way, offset, source, rank, there, :] = jnp.where(found > 0, rows, 0.0)
                landing = routed_ref.at[chip_z, :, :, final, :] if way == 0 else routed_ref.at[:, chip_y, :, final, :]
                if offset:
                    pltpu.make_async_remote_copy(
                        packed.at[way, offset, :, :, there, :], landing,
                        spread_send.at[chunk, way], spread_recv.at[chunk, way],
                        device_id={"gz": partner(1 - way, offset)}, device_id_type=MESH,
                    ).start()
                else:
                    pltpu.make_async_copy(
                        packed.at[way, offset, :, :, there, :], landing, own_sem.at[chunk, way]
                    ).start()
    for chunk in range(CHUNKS):
        for way in range(2):
            there = pl.ds(chunk * CHUNK_ROWS, CHUNK_ROWS)
            part = packed.at[way, pl.ds(0, 3), :, :, there, :]
            pltpu.make_async_copy(part, part, spread_recv.at[chunk, way]).wait()
            pltpu.make_async_copy(part, part, spread_send.at[chunk, way]).wait()
            part = packed.at[way, 0, :, :, there, :]
            pltpu.make_async_copy(part, part, own_sem.at[chunk, way]).wait()
            wait_all(gathered[way][chunk], 3, gather_send.at[chunk, way])
    for way in range(2):
        wait_all(codes_in.at[way], 3, codes_send.at[way])
    for step in range(STEPS):
        v = volume_ref if step == 0 else middle
        for k in range(4):
            part = v.at[pl.ds(0, CY)] if k < 2 else y_halo_out.at[step, 0]
            pltpu.make_async_copy(part, part, halo_send.at[step, k]).wait()
        wait_parts(z_out.at[step].reshape(Z_OWNERS, 32, NX), Z_OWNERS, z_send.at[step], joins_z)
        wait_parts(y_out.at[step].reshape(Y_OWNERS, 32, NX), Y_OWNERS, y_send.at[step], joins_y)

        @pl.when(joins_z)
        def _():
            wait_all(z_back_out.at[step].reshape(N_GZ, 8, NX), N_GZ - 1, zb_send.at[step])

        @pl.when(joins_y)
        def _():
            wait_all(y_back_out.at[step].reshape(N_XY, 8, NX), N_XY - 1, yb_send.at[step])


def vmem(*shape):
    return pltpu.VMEM(shape, jnp.float32)


def diffuse_and_route(volume, owners):
    dma = pltpu.SemaphoreType.DMA
    return pl.pallas_call(
        diffuse_and_route_kernel,
        out_shape=(
            jax.ShapeDtypeStruct((ROWS, NX), jnp.float32),
            jax.ShapeDtypeStruct((4, 4, MOST, BLOCK_ROWS, NX), jnp.float32),
        ),
        in_specs=[
            pl.BlockSpec(memory_space=pltpu.HBM),
            pl.BlockSpec(memory_space=pltpu.HBM),
        ],
        out_specs=(pl.BlockSpec(memory_space=pltpu.VMEM), pl.BlockSpec(memory_space=pl.ANY)),
        scratch_shapes=[
            vmem(ROWS, NX),
            vmem(ROWS, NX),
            vmem(STEPS, 2, CY, NX),
            vmem(STEPS, 2, CZ, NX),
            vmem(STEPS, 2, CZ, NX),
            vmem(ROWS, NX),
            vmem(3, CZ, CY, NX),
            vmem(3, CY, CZ, NX),
            vmem(4, ROWS, NX),
            vmem(ROWS, NX),
            vmem(STEPS, Z_OWNERS * 32, NX),
            vmem(STEPS, N_GZ * 32, NX),
            vmem(STEPS, Y_OWNERS * 32, NX),
            vmem(STEPS, N_XY * 32, NX),
            vmem(STEPS, N_GZ * 8, NX),
            vmem(STEPS, Z_OWNERS * 8, NX),
            vmem(STEPS, N_XY * 8, NX),
            vmem(STEPS, Y_OWNERS * 8, NX),
            dma((STEPS, 4)),
            dma((STEPS, 4)),
        ]
        + [dma((STEPS,))] * 8
        + [
            pltpu.SMEM((BLOCKS_HERE,), jnp.int32),
            dma,
            pltpu.VMEM((8, NX), jnp.int32),
            pltpu.VMEM((2, 4, 8, NX), jnp.int32),
            pltpu.SMEM((2, 4, 8, NX), jnp.int32),
            [[vmem(4, BLOCKS_HERE, CHUNK_ROWS, NX) for _ in range(CHUNKS)] for _ in range(2)],
            vmem(2, 4, 4, MOST, HALF_ROWS, NX),
            dma,
            dma((2,)),
            dma((2,)),
            dma,
        ]
        + [dma((CHUNKS, 2))] * 5,
        compiler_params=pltpu.CompilerParams(
            collective_id=0, has_side_effects=True, vmem_limit_bytes=48 << 20
        ),
    )(volume, owners)


def on_device(volume, owners):
    depth, height, width = volume.shape
    field, routed = diffuse_and_route(volume.reshape(depth * height, width), owners.reshape(-1))
    return (field.reshape(volume.shape), routed.reshape(1, N_GZ * MOST, BLOCK_ROWS, width))


def solution(mesh):
    in_specs = (P("gz", "xy", None), P("xy", "gz", None))
    out_specs = (P("gz", "xy", None), P("xy", "gz", None, None))
    return jax.shard_map(
        on_device, mesh=mesh, in_specs=in_specs, out_specs=out_specs, check_vma=False
    )
```

```python
import jax
import jax.numpy as jnp
from jax import lax
from jax.experimental import pallas as pl
from jax.experimental.pallas import tpu as pltpu
from jax.sharding import PartitionSpec as P

STEPS = 2
MOST = 2
BLOCK_ROWS = 128

TIME_STEP = 30.0
CONTRAST = 4.0
HALF_K = 1.5 * TIME_STEP

CZ = 16
CY = 32
NX = 128
ROWS = CZ * CY
N_GZ = 16
N_XY = 8
FIELDS = 7
Z_OWNERS = 8
Y_OWNERS = 4
LINES = 4
BLOCKS_HERE = 4
HALF_ROWS = BLOCK_ROWS // 2
CHUNKS = 2
X_FIRST = 4
CHUNK_ROWS = HALF_ROWS // CHUNKS
MESH = pl.DeviceIdType.MESH

Z_PEERS = sorted(
    [(a, b) for a in range(4) for b in range(4) if (a, b) != (0, 0)],
    key=lambda p: -(min(p[0], 4 - p[0]) + min(p[1], 4 - p[1])),
)
Y_PEERS = sorted(
    [(a, b) for a in range(4) for b in range(2) if (a, b) != (0, 0)],
    key=lambda p: -(2 * min(p[0], 4 - p[0]) + p[1]),
)


def recip(value):
    return 1.0 / value


def pcr(diag, coupling, side, count, axis):
    stride = 1
    while stride < count:
        inverse = recip(diag)
        scaled = coupling * inverse
        side_scaled = side * inverse
        side = (
            side
            + pltpu.roll(coupling * side_scaled, stride, axis)
            + coupling * pltpu.roll(side_scaled, count - stride, axis)
        )
        diag = (
            diag
            - pltpu.roll(coupling * scaled, stride, axis)
            - coupling * coupling * pltpu.roll(inverse, count - stride, axis)
        )
        stride *= 2
        if stride < count:
            coupling = coupling * pltpu.roll(scaled, count - stride // 2, axis)
    return side * recip(diag)


def forward_sweep(count, load_v, load_g, store):
    g_here = load_g(0)
    g_first = g_here
    total = jnp.ones_like(g_here)
    side = load_v(0)
    unit = jnp.ones_like(g_here)
    first_side = jnp.zeros_like(g_here)
    first_unit = jnp.zeros_like(g_here)
    for i in range(count - 1):
        g_next = load_g(i + 1)
        weight = HALF_K * (g_here + g_next)
        inverse = recip(total + weight)
        ratio = weight * inverse
        side_scaled = side * inverse
        unit_scaled = unit * inverse
        store(i, ratio, side_scaled, unit_scaled)
        first_side = first_side + unit * side_scaled
        first_unit = first_unit + unit * unit_scaled
        total = 1.0 + ratio * total
        side = load_v(i + 1) + ratio * side
        unit = ratio * unit
        g_here = g_next
    inverse = recip(total)
    last_side = side * inverse
    last_unit = unit * inverse
    store(count - 1, inverse, last_side, last_unit)
    first_side = first_side + unit * last_side
    first_unit = first_unit + unit * last_unit
    return (first_side, last_side, first_unit, last_unit, inverse, g_first, g_here)


def backward_sweep(count, load, store):
    high_unit, side, low_unit = load(count - 1)
    store(count - 1, side, low_unit, high_unit)
    for i in range(count - 2, -1, -1):
        ratio, side_scaled, unit_scaled = load(i)
        side = side_scaled + ratio * side
        low_unit = unit_scaled + ratio * low_unit
        high_unit = ratio * high_unit
        store(i, side, low_unit, high_unit)


def interface_fluxes(received, count):
    first_side, last_side, first_unit, cross, last_unit, g_first, g_last = [received(j) for j in range(FIELDS)]
    index = lax.broadcasted_iota(jnp.int32, (count, NX), 0)

    def following(field):
        return pltpu.roll(field, count - 1, 0)

    weight = HALF_K * (g_last + following(g_first))
    diag = recip(weight) + last_unit + following(first_unit)
    side = last_side - following(first_side)
    diag = jnp.where(index < count - 1, diag, 1.0)
    side = jnp.where(index < count - 1, side, 0.0)
    coupling = jnp.where(index < count - 2, following(cross), 0.0)
    return pcr(diag, coupling, side, count, 0)


def diffuse_and_route_kernel(
    volume_hbm,
    owners_hbm,
    out_ref,
    routed_ref,
    volume_ref,
    middle,
    z_halo,
    y_halo_out,
    y_halo,
    g_ref,
    z_keep,
    y_keep,
    natural,
    base,
    z_out,
    z_in,
    y_out,
    y_in,
    z_back_out,
    z_back,
    y_back_out,
    y_back,
    halo_send,
    halo_recv,
    z_send,
    z_recv,
    y_send,
    y_recv,
    zb_send,
    zb_recv,
    yb_send,
    yb_recv,
    owners_ref,
    owners_sem,
    codes_out,
    codes_in,
    codes,
    gathered,
    packed,
    volume_sem,
    codes_send,
    codes_recv,
    codes_sem,
    own_sem,
    gather_send,
    gather_recv,
    spread_send,
    spread_recv,
):
    load_volume = pltpu.make_async_copy(volume_hbm, volume_ref, volume_sem)
    load_volume.start()
    load_owners = pltpu.make_async_copy(owners_hbm, owners_ref, owners_sem)
    load_owners.start()
    gz = lax.axis_index("gz")
    xy = lax.axis_index("xy")
    z_targets = [
        lax.rem(gz // 4 + dz, 4) * 4 + lax.rem(lax.rem(gz, 4) + dy, 4) for dz, dy in Z_PEERS
    ]
    y_targets = [
        lax.rem(xy // 2 + dx, 4) * 2 + lax.rem(lax.rem(xy, 2) + core, 2) for dx, core in Y_PEERS
    ]
    odd = lax.rem(gz + xy, 2)
    joins_z = odd == 0
    joins_y = odd == 1
    z_owners = [
        (lax.rem(gz // 4 + dz, 4) * 4 + lax.rem(lax.rem(gz, 4) + dy + odd, 4), (dz, dy) == (0, 0))
        for dz, dy in ((2, 2), (1, 2), (3, 2), (2, 0), (1, 0), (3, 0), (0, 2), (0, 0))
    ]
    y_owners = [
        (lax.rem(xy // 2 + dx, 4) * 2 + lax.rem(lax.rem(xy, 2) + 1 - odd, 2), dx == 0) for dx in (2, 1, 3, 0)
    ]
    barrier = pltpu.get_barrier_semaphore()
    for target in z_targets:
        pl.semaphore_signal(barrier, 1, device_id={"gz": target}, device_id_type=MESH)
    for target in y_targets:
        pl.semaphore_signal(barrier, 1, device_id={"xy": target}, device_id_type=MESH)
    pl.semaphore_wait(barrier, N_GZ + N_XY - 2)

    chip_z, chip_y = gz // 4, lax.rem(gz, 4)
    places = [chip_y, chip_z]

    def partner(way, offset):
        if way == 0:
            return chip_z * 4 + lax.rem(chip_y + offset, 4)
        return lax.rem(chip_z + offset, 4) * 4 + chip_y

    load_owners.wait()
    lanes = lax.broadcasted_iota(jnp.int32, (8, NX), 1)
    code_tile = jnp.zeros((8, NX), jnp.int32)
    for b in range(BLOCKS_HERE):
        rank = 0
        for earlier in range(b):
            rank = rank + (owners_ref[earlier] == owners_ref[b]).astype(jnp.int32)
        code_tile = jnp.where(lanes == b, owners_ref[b] * MOST + rank, code_tile)
    codes_out[...] = code_tile
    for way in range(2):
        codes_in[way, places[way]] = code_tile
        for offset in (2, 1, 3):
            pltpu.make_async_remote_copy(
                codes_out, codes_in.at[way, places[way]], codes_send.at[way], codes_recv.at[way],
                device_id={"gz": partner(way, offset)}, device_id_type=MESH,
            ).start()
    load_volume.wait()

    row_index = lax.broadcasted_iota(jnp.int32, (CY, NX), 0)
    lane_index = lax.broadcasted_iota(jnp.int32, (CY, NX), 1)

    def send_all(source, landing, send_sem, recv_sem, axis, targets, me):
        for target in targets:
            pltpu.make_async_remote_copy(
                source.at[target], landing.at[me], send_sem, recv_sem,
                device_id={axis: target}, device_id_type=MESH,
            ).start()

    def send_parts(source, landing, send_sem, recv_sem, axis, owners, me, is_owner):
        for target, may_be_self in owners:
            copy = pltpu.make_async_remote_copy(
                source.at[target // 2], landing.at[me], send_sem, recv_sem,
                device_id={axis: target}, device_id_type=MESH,
            )
            if may_be_self:
                pl.when(jnp.logical_not(is_owner))(copy.start)

                @pl.when(is_owner)
                def _():
                    landing[me] = source[target // 2]

            else:
                copy.start()

    def wait_parts(buffer, count, semaphore, is_owner):
        @pl.when(is_owner)
        def _():
            wait_all(buffer, count - 1, semaphore)

        @pl.when(jnp.logical_not(is_owner))
        def _():
            wait_all(buffer, count, semaphore)

    def wait_all(buffer, count, semaphore):
        part = buffer.at[pl.ds(0, count)]
        pltpu.make_async_copy(part, part, semaphore).wait()

    for step in range(STEPS):
        v = volume_ref if step == 0 else middle
        new = out_ref if step == STEPS - 1 else middle

        y_halo_out[step, 0] = v[pl.ds(0, CZ, stride=CY), :]
        y_halo_out[step, 1] = v[pl.ds(CY - 1, CZ, stride=CY), :]
        copies = []
        for k, (axis, me, count, forward) in enumerate(
            [("gz", gz, N_GZ, 0), ("gz", gz, N_GZ, 1), ("xy", xy, N_XY, 0), ("xy", xy, N_XY, 1)]
        ):
            target = lax.rem(me + (1 if forward else count - 1), count)
            if axis == "gz":
                source = v.at[pl.ds((CZ - 1) * CY if forward else 0, CY)]
                landing = z_halo.at[step, 1 - forward]
            else:
                source = y_halo_out.at[step, forward]
                landing = y_halo.at[step, 1 - forward]
            copies.append(
                pltpu.make_async_remote_copy(
                    source, landing, halo_send.at[step, k], halo_recv.at[step, k],
                    device_id={axis: target}, device_id_type=MESH,
                )
            )
        for copy in copies:
            copy.start()
        for copy in copies:
            copy.wait_recv()

        def plane(i):
            return v[i * CY : (i + 1) * CY, :]

        before = jnp.where(gz == 0, plane(0), z_halo[step, 0])
        after = jnp.where(gz == N_GZ - 1, plane(CZ - 1), z_halo[step, 1])
        here = plane(0)
        for i in range(CZ):
            above = plane(i + 1) if i < CZ - 1 else after
            slope_z = above - before
            y_low = jnp.where(xy == 0, here[0:1, :], y_halo[step, 0, i : i + 1, :])
            y_high = jnp.where(xy == N_XY - 1, here[CY - 1 : CY, :], y_halo[step, 1, i : i + 1, :])
            y_prev = jnp.where(row_index == 0, y_low, pltpu.roll(here, 1, 0))
            y_next = jnp.where(row_index == CY - 1, y_high, pltpu.roll(here, CY - 1, 0))
            slope_y = y_next - y_prev
            x_prev = jnp.where(lane_index == 0, here, pltpu.roll(here, 1, 1))
            x_next = jnp.where(lane_index == NX - 1, here, pltpu.roll(here, NX - 1, 1))
            slope_x = x_next - x_prev
            squares = slope_z * slope_z + slope_y * slope_y + slope_x * slope_x
            g_ref[i * CY : (i + 1) * CY, :] = recip(1.0 + squares * (0.25 / CONTRAST))
            before, here = here, above

        def z_store(i, ratio, side, unit):
            z_keep[0, i] = ratio
            z_keep[1, i] = side
            z_keep[2, i] = unit

        ends = forward_sweep(CZ, plane, lambda i: g_ref[i * CY : (i + 1) * CY, :], z_store)
        for j, field in enumerate(ends):
            for h in range(LINES):
                z_out[step, pl.ds(LINES * j + h, Z_OWNERS, stride=32), :] = field[h * Z_OWNERS : (h + 1) * Z_OWNERS, :]
        z_in_blocks = z_in.at[step].reshape(N_GZ, 32, NX)
        z_out_blocks = z_out.at[step].reshape(Z_OWNERS, 32, NX)
        send_parts(z_out_blocks, z_in_blocks, z_send.at[step], z_recv.at[step], "gz", z_owners, gz, joins_z)

        def y_store(i, ratio, side, unit):
            y_keep[0, i] = ratio
            y_keep[1, i] = side
            y_keep[2, i] = unit

        ends = forward_sweep(
            CY,
            lambda i: v[pl.ds(i, CZ, stride=CY), :],
            lambda i: g_ref[pl.ds(i, CZ, stride=CY), :],
            y_store,
        )
        for j, field in enumerate(ends):
            for h in range(LINES):
                y_out[step, pl.ds(LINES * j + h, Y_OWNERS, stride=32), :] = field[h * Y_OWNERS : (h + 1) * Y_OWNERS, :]
        y_in_blocks = y_in.at[step].reshape(N_XY, 32, NX)
        y_out_blocks = y_out.at[step].reshape(Y_OWNERS, 32, NX)
        send_parts(y_out_blocks, y_in_blocks, y_send.at[step], y_recv.at[step], "xy", y_owners, xy, joins_y)

        def solve_x(i, carry):
            rows = pl.ds(pl.multiple_of(i * 2 * CY, 2 * CY), 2 * CY)
            g = g_ref[rows, :]
            lanes = lax.broadcasted_iota(jnp.int32, (2 * CY, NX), 1)
            weight = jnp.where(lanes < NX - 1, HALF_K * (g + pltpu.roll(g, NX - 1, 1)), 0.0)
            diag = 1.0 + weight + pltpu.roll(weight, 1, 1)
            base[rows, :] = pcr(diag, weight, v[rows, :], NX, 1)
            return carry

        lax.fori_loop(0, X_FIRST, solve_x, 0)

        def z_load(i):
            return z_keep[0, i], z_keep[1, i], z_keep[2, i]

        def z_restore(i, side, low, high):
            natural[3, i * CY : (i + 1) * CY, :] = side
            z_keep[1, i] = low
            z_keep[2, i] = high

        backward_sweep(CZ, z_load, z_restore)

        def y_load(i):
            return y_keep[0, i], y_keep[1, i], y_keep[2, i]

        def y_restore(i, side, low, high):
            rows = pl.ds(i, CZ, stride=CY)
            natural[0, rows, :] = side
            natural[1, rows, :] = low
            natural[2, rows, :] = high

        backward_sweep(CY, y_load, y_restore)

        zb_out = z_back_out.at[step].reshape(N_GZ, 8, NX)
        zb_in = z_back.at[step].reshape(Z_OWNERS, 8, NX)
        yb_out = y_back_out.at[step].reshape(N_XY, 8, NX)
        yb_in = y_back.at[step].reshape(Y_OWNERS, 8, NX)

        @pl.when(joins_z)
        def _():
            wait_all(z_in_blocks, N_GZ - 1, z_recv.at[step])
            for h in range(LINES):
                flux = interface_fluxes(
                    lambda j: z_in[step, pl.ds(LINES * j + h, N_GZ, stride=32), :], N_GZ
                )
                z_back_out[step, pl.ds(h, N_GZ, stride=8), :] = pltpu.roll(flux, 1, 0)
                z_back_out[step, pl.ds(LINES + h, N_GZ, stride=8), :] = flux
            send_all(zb_out, zb_in, zb_send.at[step], zb_recv.at[step], "gz", z_targets, gz // 2)
            zb_in[gz // 2] = zb_out[gz]

        @pl.when(joins_y)
        def _():
            wait_all(y_in_blocks, N_XY - 1, y_recv.at[step])
            for h in range(LINES):
                flux = interface_fluxes(
                    lambda j: y_in[step, pl.ds(LINES * j + h, N_XY, stride=32), :], N_XY
                )
                y_back_out[step, pl.ds(h, N_XY, stride=8), :] = pltpu.roll(flux, 1, 0)
                y_back_out[step, pl.ds(LINES + h, N_XY, stride=8), :] = flux
            send_all(yb_out, yb_in, yb_send.at[step], yb_recv.at[step], "xy", y_targets, xy // 2)
            yb_in[xy // 2] = yb_out[xy]

        lax.fori_loop(X_FIRST, CZ // 2, solve_x, 0)
        wait_parts(yb_in, Y_OWNERS, yb_recv.at[step], joins_y)
        wait_parts(zb_in, Z_OWNERS, zb_recv.at[step], joins_z)
        low_z = jnp.concatenate([z_back[step, pl.ds(h, Z_OWNERS, stride=8), :] for h in range(LINES)], axis=0)
        high_z = jnp.concatenate(
            [z_back[step, pl.ds(LINES + h, Z_OWNERS, stride=8), :] for h in range(LINES)], axis=0
        )
        for i in range(CZ):
            rows = slice(i * CY, (i + 1) * CY)
            at = (i % Y_OWNERS) * 8 + i // Y_OWNERS
            low_y = y_back[step, at : at + 1, :]
            high_y = y_back[step, at + LINES : at + LINES + 1, :]
            total = base[rows, :] + natural[0, rows, :] + natural[3, rows, :]
            total = total + (low_z * z_keep[1, i] - high_z * z_keep[2, i])
            total = total + (low_y * natural[1, rows, :] - high_y * natural[2, rows, :])
            new[rows, :] = total * (1.0 / 3.0)

    for way in range(2):
        wait_all(codes_in.at[way], 3, codes_recv.at[way])
    to_scalars = pltpu.make_async_copy(codes_in, codes, codes_sem)
    to_scalars.start()
    blocks = out_ref.reshape(BLOCKS_HERE, BLOCK_ROWS, NX)
    for chunk in range(CHUNKS):
        for way in range(2):
            here = pl.ds(way * HALF_ROWS + chunk * CHUNK_ROWS, CHUNK_ROWS)
            for offset in (2, 1, 3):
                pltpu.make_async_remote_copy(
                    blocks.at[:, here, :], gathered[way][chunk].at[places[way]],
                    gather_send.at[chunk, way], gather_recv.at[chunk, way],
                    device_id={"gz": partner(way, offset)}, device_id_type=MESH,
                ).start()
    for way in range(2):
        for chunk in range(CHUNKS):
            here = pl.ds(way * HALF_ROWS + chunk * CHUNK_ROWS, CHUNK_ROWS)
            gathered[way][chunk][places[way]] = blocks[:, here, :]
    to_scalars.wait()
    choice = {}
    for way in range(2):
        for offset in range(4):
            target = partner(1 - way, offset)
            for source in range(4):
                for rank in range(MOST):
                    index, found = 0, 0
                    for b in range(BLOCKS_HERE):
                        hit = (codes[way, source, 0, b] == target * MOST + rank).astype(jnp.int32)
                        index = index + b * hit
                        found = found + hit
                    choice[way, offset, source, rank] = index, found
    for chunk in range(CHUNKS):
        for way in range(2):
            there = pl.ds(chunk * CHUNK_ROWS, CHUNK_ROWS)
            final = pl.ds(way * HALF_ROWS + chunk * CHUNK_ROWS, CHUNK_ROWS)
            wait_all(gathered[way][chunk], 3, gather_recv.at[chunk, way])
            for offset in (2, 1, 3, 0):
                for source in range(4):
                    for rank in range(MOST):
                        index, found = choice[way, offset, source, rank]
                        rows = gathered[way][chunk][source, index]
                        packed[way, offset, source, rank, there, :] = jnp.where(found > 0, rows, 0.0)
                landing = routed_ref.at[chip_z, :, :, final, :] if way == 0 else routed_ref.at[:, chip_y, :, final, :]
                if offset:
                    pltpu.make_async_remote_copy(
                        packed.at[way, offset, :, :, there, :], landing,
                        spread_send.at[chunk, way], spread_recv.at[chunk, way],
                        device_id={"gz": partner(1 - way, offset)}, device_id_type=MESH,
                    ).start()
                else:
                    pltpu.make_async_copy(
                        packed.at[way, offset, :, :, there, :], landing, own_sem.at[chunk, way]
                    ).start()
    for chunk in range(CHUNKS):
        for way in range(2):
            there = pl.ds(chunk * CHUNK_ROWS, CHUNK_ROWS)
            part = packed.at[way, pl.ds(0, 3), :, :, there, :]
            pltpu.make_async_copy(part, part, spread_recv.at[chunk, way]).wait()
            pltpu.make_async_copy(part, part, spread_send.at[chunk, way]).wait()
            part = packed.at[way, 0, :, :, there, :]
            pltpu.make_async_copy(part, part, own_sem.at[chunk, way]).wait()
            wait_all(gathered[way][chunk], 3, gather_send.at[chunk, way])
    for way in range(2):
        wait_all(codes_in.at[way], 3, codes_send.at[way])
    for step in range(STEPS):
        v = volume_ref if step == 0 else middle
        for k in range(4):
            part = v.at[pl.ds(0, CY)] if k < 2 else y_halo_out.at[step, 0]
            pltpu.make_async_copy(part, part, halo_send.at[step, k]).wait()
        wait_parts(z_out.at[step].reshape(Z_OWNERS, 32, NX), Z_OWNERS, z_send.at[step], joins_z)
        wait_parts(y_out.at[step].reshape(Y_OWNERS, 32, NX), Y_OWNERS, y_send.at[step], joins_y)

        @pl.when(joins_z)
        def _():
            wait_all(z_back_out.at[step].reshape(N_GZ, 8, NX), N_GZ - 1, zb_send.at[step])

        @pl.when(joins_y)
        def _():
            wait_all(y_back_out.at[step].reshape(N_XY, 8, NX), N_XY - 1, yb_send.at[step])


def vmem(*shape):
    return pltpu.VMEM(shape, jnp.float32)


def diffuse_and_route(volume, owners):
    dma = pltpu.SemaphoreType.DMA
    return pl.pallas_call(
        diffuse_and_route_kernel,
        out_shape=(
            jax.ShapeDtypeStruct((ROWS, NX), jnp.float32),
            jax.ShapeDtypeStruct((4, 4, MOST, BLOCK_ROWS, NX), jnp.float32),
        ),
        in_specs=[
            pl.BlockSpec(memory_space=pltpu.HBM),
            pl.BlockSpec(memory_space=pltpu.HBM),
        ],
        out_specs=(pl.BlockSpec(memory_space=pltpu.VMEM), pl.BlockSpec(memory_space=pl.ANY)),
        scratch_shapes=[
            vmem(ROWS, NX),
            vmem(ROWS, NX),
            vmem(STEPS, 2, CY, NX),
            vmem(STEPS, 2, CZ, NX),
            vmem(STEPS, 2, CZ, NX),
            vmem(ROWS, NX),
            vmem(3, CZ, CY, NX),
            vmem(3, CY, CZ, NX),
            vmem(4, ROWS, NX),
            vmem(ROWS, NX),
            vmem(STEPS, Z_OWNERS * 32, NX),
            vmem(STEPS, N_GZ * 32, NX),
            vmem(STEPS, Y_OWNERS * 32, NX),
            vmem(STEPS, N_XY * 32, NX),
            vmem(STEPS, N_GZ * 8, NX),
            vmem(STEPS, Z_OWNERS * 8, NX),
            vmem(STEPS, N_XY * 8, NX),
            vmem(STEPS, Y_OWNERS * 8, NX),
            dma((STEPS, 4)),
            dma((STEPS, 4)),
        ]
        + [dma((STEPS,))] * 8
        + [
            pltpu.SMEM((BLOCKS_HERE,), jnp.int32),
            dma,
            pltpu.VMEM((8, NX), jnp.int32),
            pltpu.VMEM((2, 4, 8, NX), jnp.int32),
            pltpu.SMEM((2, 4, 8, NX), jnp.int32),
            [[vmem(4, BLOCKS_HERE, CHUNK_ROWS, NX) for _ in range(CHUNKS)] for _ in range(2)],
            vmem(2, 4, 4, MOST, HALF_ROWS, NX),
            dma,
            dma((2,)),
            dma((2,)),
            dma,
        ]
        + [dma((CHUNKS, 2))] * 5,
        compiler_params=pltpu.CompilerParams(
            collective_id=0, has_side_effects=True, vmem_limit_bytes=48 << 20
        ),
    )(pltpu.with_memory_space_constraint(volume, pltpu.HBM), pltpu.with_memory_space_constraint(owners, pltpu.HBM))


def write_kernel(field_ref, routed_ref, field_out, routed_out, semaphores):
    copies = [pltpu.make_async_copy(field_ref, field_out, semaphores.at[0])]
    for part in range(4):
        rows = pl.ds(part * (N_GZ * MOST // 4), N_GZ * MOST // 4)
        copies.append(
            pltpu.make_async_copy(routed_ref.at[rows], routed_out.at[rows], semaphores.at[1 + part])
        )
    for copy in copies[::-1]:
        copy.start()
    for copy in copies:
        copy.wait()


def write_out(field, routed):
    return pl.pallas_call(
        write_kernel,
        out_shape=(
            jax.ShapeDtypeStruct(field.shape, field.dtype),
            jax.ShapeDtypeStruct(routed.shape, routed.dtype),
        ),
        in_specs=[pl.BlockSpec(memory_space=pl.ANY)] * 2,
        out_specs=(pl.BlockSpec(memory_space=pltpu.HBM),) * 2,
        scratch_shapes=[pltpu.SemaphoreType.DMA((1 + 4,))],
        compiler_params=pltpu.CompilerParams(vmem_limit_bytes=8 << 20),
    )(field, routed)


def on_device(volume, owners):
    depth, height, width = volume.shape
    field, routed = diffuse_and_route(volume.reshape(depth * height, width), owners.reshape(-1))
    field, routed = write_out(field, routed.reshape(N_GZ * MOST, BLOCK_ROWS, width))
    return (field.reshape(volume.shape), routed.reshape(1, N_GZ * MOST, BLOCK_ROWS, width))


def solution(mesh):
    in_specs = (P("gz", "xy", None), P("xy", "gz", None))
    out_specs = (P("gz", "xy", None), P("xy", "gz", None, None))
    return jax.shard_map(
        on_device, mesh=mesh, in_specs=in_specs, out_specs=out_specs, check_vma=False
    )
```

```python
import jax
import jax.numpy as jnp
from jax import lax
from jax.experimental import pallas as pl
from jax.experimental.pallas import tpu as pltpu
from jax.sharding import PartitionSpec as P

STEPS = 2
MOST = 2
BLOCK_ROWS = 128

TIME_STEP = 30.0
CONTRAST = 4.0
HALF_K = 1.5 * TIME_STEP

CZ = 16
CY = 32
NX = 128
ROWS = CZ * CY
N_GZ = 16
N_XY = 8
FIELDS = 7
Z_OWNERS = 8
Y_OWNERS = 4
LINES = 4
BLOCKS_HERE = 4
HALF_ROWS = BLOCK_ROWS // 2
CHUNKS = 2
X_FIRST = 4
CHUNK_ROWS = HALF_ROWS // CHUNKS
PASSED_ROWS = CHUNK_ROWS // 2
MESH = pl.DeviceIdType.MESH

Z_PEERS = sorted(
    [(a, b) for a in range(4) for b in range(4) if (a, b) != (0, 0)],
    key=lambda p: -(min(p[0], 4 - p[0]) + min(p[1], 4 - p[1])),
)
Y_PEERS = sorted(
    [(a, b) for a in range(4) for b in range(2) if (a, b) != (0, 0)],
    key=lambda p: -(2 * min(p[0], 4 - p[0]) + p[1]),
)


def recip(value):
    return 1.0 / value


def pcr(diag, coupling, side, count, axis):
    stride = 1
    while stride < count:
        inverse = recip(diag)
        scaled = coupling * inverse
        side_scaled = side * inverse
        side = (
            side
            + pltpu.roll(coupling * side_scaled, stride, axis)
            + coupling * pltpu.roll(side_scaled, count - stride, axis)
        )
        diag = (
            diag
            - pltpu.roll(coupling * scaled, stride, axis)
            - coupling * coupling * pltpu.roll(inverse, count - stride, axis)
        )
        stride *= 2
        if stride < count:
            coupling = coupling * pltpu.roll(scaled, count - stride // 2, axis)
    return side * recip(diag)


def forward_sweep(count, load_v, load_g, store):
    g_here = load_g(0)
    g_first = g_here
    total = jnp.ones_like(g_here)
    side = load_v(0)
    unit = jnp.ones_like(g_here)
    first_side = jnp.zeros_like(g_here)
    first_unit = jnp.zeros_like(g_here)
    for i in range(count - 1):
        g_next = load_g(i + 1)
        weight = HALF_K * (g_here + g_next)
        inverse = recip(total + weight)
        ratio = weight * inverse
        side_scaled = side * inverse
        unit_scaled = unit * inverse
        store(i, ratio, side_scaled, unit_scaled)
        first_side = first_side + unit * side_scaled
        first_unit = first_unit + unit * unit_scaled
        total = 1.0 + ratio * total
        side = load_v(i + 1) + ratio * side
        unit = ratio * unit
        g_here = g_next
    inverse = recip(total)
    last_side = side * inverse
    last_unit = unit * inverse
    store(count - 1, inverse, last_side, last_unit)
    first_side = first_side + unit * last_side
    first_unit = first_unit + unit * last_unit
    return (first_side, last_side, first_unit, last_unit, inverse, g_first, g_here)


def backward_sweep(count, load, store):
    high_unit, side, low_unit = load(count - 1)
    store(count - 1, side, low_unit, high_unit)
    for i in range(count - 2, -1, -1):
        ratio, side_scaled, unit_scaled = load(i)
        side = side_scaled + ratio * side
        low_unit = unit_scaled + ratio * low_unit
        high_unit = ratio * high_unit
        store(i, side, low_unit, high_unit)


def interface_fluxes(received, count):
    first_side, last_side, first_unit, cross, last_unit, g_first, g_last = [received(j) for j in range(FIELDS)]
    index = lax.broadcasted_iota(jnp.int32, (count, NX), 0)

    def following(field):
        return pltpu.roll(field, count - 1, 0)

    weight = HALF_K * (g_last + following(g_first))
    diag = recip(weight) + last_unit + following(first_unit)
    side = last_side - following(first_side)
    diag = jnp.where(index < count - 1, diag, 1.0)
    side = jnp.where(index < count - 1, side, 0.0)
    coupling = jnp.where(index < count - 2, following(cross), 0.0)
    return pcr(diag, coupling, side, count, 0)


def diffuse_and_route_kernel(
    volume_hbm,
    owners_hbm,
    out_ref,
    routed_ref,
    volume_ref,
    middle,
    z_halo,
    y_halo_out,
    y_halo,
    g_ref,
    z_keep,
    y_keep,
    natural,
    base,
    z_out,
    z_in,
    y_out,
    y_in,
    z_back_out,
    z_back,
    y_back_out,
    y_back,
    halo_send,
    halo_recv,
    z_send,
    z_recv,
    y_send,
    y_recv,
    zb_send,
    zb_recv,
    yb_send,
    yb_recv,
    owners_ref,
    owners_sem,
    codes_out,
    codes_in,
    codes,
    choice,
    gathered,
    gathered_far,
    packed,
    volume_sem,
    codes_send,
    codes_recv,
    codes_sem,
    gather_send,
    gather_recv,
    far_send,
    far_recv,
    spread_send,
    spread_recv,
):
    load_volume = pltpu.make_async_copy(volume_hbm, volume_ref, volume_sem)
    load_volume.start()
    load_owners = pltpu.make_async_copy(owners_hbm, owners_ref, owners_sem)
    load_owners.start()
    gz = lax.axis_index("gz")
    xy = lax.axis_index("xy")
    z_targets = [
        lax.rem(gz // 4 + dz, 4) * 4 + lax.rem(lax.rem(gz, 4) + dy, 4) for dz, dy in Z_PEERS
    ]
    y_targets = [
        lax.rem(xy // 2 + dx, 4) * 2 + lax.rem(lax.rem(xy, 2) + core, 2) for dx, core in Y_PEERS
    ]
    odd = lax.rem(gz + xy, 2)
    joins_z = odd == 0
    joins_y = odd == 1
    z_owners = [
        (lax.rem(gz // 4 + dz, 4) * 4 + lax.rem(lax.rem(gz, 4) + dy + odd, 4), (dz, dy) == (0, 0))
        for dz, dy in ((2, 2), (1, 2), (3, 2), (2, 0), (1, 0), (3, 0), (0, 2), (0, 0))
    ]
    y_owners = [
        (lax.rem(xy // 2 + dx, 4) * 2 + lax.rem(lax.rem(xy, 2) + 1 - odd, 2), dx == 0) for dx in (2, 1, 3, 0)
    ]
    barrier = pltpu.get_barrier_semaphore()
    for target in z_targets:
        pl.semaphore_signal(barrier, 1, device_id={"gz": target}, device_id_type=MESH)
    for target in y_targets:
        pl.semaphore_signal(barrier, 1, device_id={"xy": target}, device_id_type=MESH)
    pl.semaphore_wait(barrier, N_GZ + N_XY - 2)

    chip_z, chip_y = gz // 4, lax.rem(gz, 4)
    places = [chip_y, chip_z]

    def partner(way, offset):
        if way == 0:
            return chip_z * 4 + lax.rem(chip_y + offset, 4)
        return lax.rem(chip_z + offset, 4) * 4 + chip_y

    load_owners.wait()
    lanes = lax.broadcasted_iota(jnp.int32, (8, NX), 1)
    code_tile = jnp.zeros((8, NX), jnp.int32)
    for b in range(BLOCKS_HERE):
        rank = 0
        for earlier in range(b):
            rank = rank + (owners_ref[earlier] == owners_ref[b]).astype(jnp.int32)
        code_tile = jnp.where(lanes == b, owners_ref[b] * MOST + rank, code_tile)
    codes_out[...] = code_tile
    for way in range(2):
        codes_in[way, places[way]] = code_tile
        for offset in (2, 1, 3):
            pltpu.make_async_remote_copy(
                codes_out, codes_in.at[way, places[way]], codes_send.at[way], codes_recv.at[way],
                device_id={"gz": partner(way, offset)}, device_id_type=MESH,
            ).start()
    load_volume.wait()

    row_index = lax.broadcasted_iota(jnp.int32, (CY, NX), 0)
    lane_index = lax.broadcasted_iota(jnp.int32, (CY, NX), 1)

    blocks = out_ref.reshape(BLOCKS_HERE, BLOCK_ROWS, NX)
    to_scalars = pltpu.make_async_copy(codes_in, codes, codes_sem)

    def place_of(way, source):
        return lax.rem(places[way] + (0, 3, 1, 2)[source], 4)

    def choose():
        for way in range(2):
            for source in range(4):
                place = place_of(way, source)
                for offset in range(4):
                    target = partner(1 - way, offset)
                    for rank in range(MOST):
                        index, found = 0, 0
                        for b in range(BLOCKS_HERE):
                            hit = (codes[way, place, 0, b] == target * MOST + rank).astype(jnp.int32)
                            index = index + b * hit
                            found = found + hit
                        choice[0, way, source, offset, rank] = index
                        choice[1, way, source, offset, rank] = found

    def send_near(way, chunk):
        here = pl.ds(way * HALF_ROWS + chunk * CHUNK_ROWS, CHUNK_ROWS)
        for side, offset in ((0, 1), (1, 3)):
            pltpu.make_async_remote_copy(
                blocks.at[:, here, :], gathered[way][chunk].at[side],
                gather_send.at[chunk, way], gather_recv.at[chunk, way],
                device_id={"gz": partner(way, offset)}, device_id_type=MESH,
            ).start()

    def pass_on(way, source, offset, first, count, read):
        there = pl.ds(first, count)
        final = pl.ds(way * HALF_ROWS + first, count)
        place = place_of(way, source)
        at = (chip_z, place) if way == 0 else (place, chip_y)
        for rank in range(MOST):
            found = choice[1, way, source, offset, rank]
            rows = jnp.where(found > 0, read(choice[0, way, source, offset, rank]), 0.0)
            if offset:
                packed[way, source, offset, rank, there, :] = rows
            else:
                routed_ref[at[0], at[1], rank, final, :] = rows
        if offset:
            kind = (0, 1, 1, 2)[source]
            pltpu.make_async_remote_copy(
                packed.at[way, source, offset, :, there, :], routed_ref.at[at[0], at[1], :, final, :],
                spread_send.at[way, kind], spread_recv.at[way, kind],
                device_id={"gz": partner(1 - way, offset)}, device_id_type=MESH,
            ).start()

    def send_all(source, landing, send_sem, recv_sem, axis, targets, me):
        for target in targets:
            pltpu.make_async_remote_copy(
                source.at[target], landing.at[me], send_sem, recv_sem,
                device_id={axis: target}, device_id_type=MESH,
            ).start()

    def send_parts(source, landing, send_sem, recv_sem, axis, owners, me, is_owner):
        for target, may_be_self in owners:
            copy = pltpu.make_async_remote_copy(
                source.at[target // 2], landing.at[me], send_sem, recv_sem,
                device_id={axis: target}, device_id_type=MESH,
            )
            if may_be_self:
                pl.when(jnp.logical_not(is_owner))(copy.start)

                @pl.when(is_owner)
                def _():
                    landing[me] = source[target // 2]

            else:
                copy.start()

    def wait_parts(buffer, count, semaphore, is_owner):
        @pl.when(is_owner)
        def _():
            wait_all(buffer, count - 1, semaphore)

        @pl.when(jnp.logical_not(is_owner))
        def _():
            wait_all(buffer, count, semaphore)

    def wait_all(buffer, count, semaphore):
        part = buffer.at[pl.ds(0, count)]
        pltpu.make_async_copy(part, part, semaphore).wait()

    def halo_copies(step, v, which):
        copies = []
        for k, (axis, me, count, forward) in enumerate(
            [("gz", gz, N_GZ, 0), ("gz", gz, N_GZ, 1), ("xy", xy, N_XY, 0), ("xy", xy, N_XY, 1)]
        ):
            if axis != which:
                continue
            target = lax.rem(me + (1 if forward else count - 1), count)
            if axis == "gz":
                source = v.at[pl.ds((CZ - 1) * CY if forward else 0, CY)]
                landing = z_halo.at[step, 1 - forward]
            else:
                source = y_halo_out.at[step, forward]
                landing = y_halo.at[step, 1 - forward]
            copies.append(
                pltpu.make_async_remote_copy(
                    source, landing, halo_send.at[step, k], halo_recv.at[step, k],
                    device_id={axis: target}, device_id_type=MESH,
                )
            )
        return copies

    def send_z_halo(step, v):
        for copy in halo_copies(step, v, "gz"):
            copy.start()

    def send_y_halo(step, v):
        y_halo_out[step, 0] = v[pl.ds(0, CZ, stride=CY), :]
        y_halo_out[step, 1] = v[pl.ds(CY - 1, CZ, stride=CY), :]
        for copy in halo_copies(step, v, "xy"):
            copy.start()

    send_z_halo(0, volume_ref)
    send_y_halo(0, volume_ref)
    for step in range(STEPS):
        v = volume_ref if step == 0 else middle
        new = out_ref if step == STEPS - 1 else middle

        def plane(i):
            return v[i * CY : (i + 1) * CY, :]

        def diffuse(i, before, above):
            here = plane(i)
            slope_z = above - before
            y_low = jnp.where(xy == 0, here[0:1, :], y_halo[step, 0, i : i + 1, :])
            y_high = jnp.where(xy == N_XY - 1, here[CY - 1 : CY, :], y_halo[step, 1, i : i + 1, :])
            y_prev = jnp.where(row_index == 0, y_low, pltpu.roll(here, 1, 0))
            y_next = jnp.where(row_index == CY - 1, y_high, pltpu.roll(here, CY - 1, 0))
            slope_y = y_next - y_prev
            x_prev = jnp.where(lane_index == 0, here, pltpu.roll(here, 1, 1))
            x_next = jnp.where(lane_index == NX - 1, here, pltpu.roll(here, NX - 1, 1))
            slope_x = x_next - x_prev
            squares = slope_z * slope_z + slope_y * slope_y + slope_x * slope_x
            g_ref[i * CY : (i + 1) * CY, :] = recip(1.0 + squares * (0.25 / CONTRAST))

        for copy in halo_copies(step, v, "xy"):
            copy.wait_recv()
        for i in range(1, CZ - 1):
            diffuse(i, plane(i - 1), plane(i + 1))
        for copy in halo_copies(step, v, "gz"):
            copy.wait_recv()
        diffuse(0, jnp.where(gz == 0, plane(0), z_halo[step, 0]), plane(1))
        diffuse(CZ - 1, plane(CZ - 2), jnp.where(gz == N_GZ - 1, plane(CZ - 1), z_halo[step, 1]))

        def z_store(i, ratio, side, unit):
            z_keep[0, i] = ratio
            z_keep[1, i] = side
            z_keep[2, i] = unit

        ends = forward_sweep(CZ, plane, lambda i: g_ref[i * CY : (i + 1) * CY, :], z_store)
        for j, field in enumerate(ends):
            for h in range(LINES):
                z_out[step, pl.ds(LINES * j + h, Z_OWNERS, stride=32), :] = field[h * Z_OWNERS : (h + 1) * Z_OWNERS, :]
        z_in_blocks = z_in.at[step].reshape(N_GZ, 32, NX)
        z_out_blocks = z_out.at[step].reshape(Z_OWNERS, 32, NX)
        send_parts(z_out_blocks, z_in_blocks, z_send.at[step], z_recv.at[step], "gz", z_owners, gz, joins_z)

        def y_store(i, ratio, side, unit):
            y_keep[0, i] = ratio
            y_keep[1, i] = side
            y_keep[2, i] = unit

        ends = forward_sweep(
            CY,
            lambda i: v[pl.ds(i, CZ, stride=CY), :],
            lambda i: g_ref[pl.ds(i, CZ, stride=CY), :],
            y_store,
        )
        for j, field in enumerate(ends):
            for h in range(LINES):
                y_out[step, pl.ds(LINES * j + h, Y_OWNERS, stride=32), :] = field[h * Y_OWNERS : (h + 1) * Y_OWNERS, :]
        y_in_blocks = y_in.at[step].reshape(N_XY, 32, NX)
        y_out_blocks = y_out.at[step].reshape(Y_OWNERS, 32, NX)
        send_parts(y_out_blocks, y_in_blocks, y_send.at[step], y_recv.at[step], "xy", y_owners, xy, joins_y)

        def solve_x(i, carry):
            rows = pl.ds(pl.multiple_of(i * 2 * CY, 2 * CY), 2 * CY)
            g = g_ref[rows, :]
            lanes = lax.broadcasted_iota(jnp.int32, (2 * CY, NX), 1)
            weight = jnp.where(lanes < NX - 1, HALF_K * (g + pltpu.roll(g, NX - 1, 1)), 0.0)
            diag = 1.0 + weight + pltpu.roll(weight, 1, 1)
            base[rows, :] = pcr(diag, weight, v[rows, :], NX, 1)
            return carry

        lax.fori_loop(0, X_FIRST, solve_x, 0)

        def z_load(i):
            return z_keep[0, i], z_keep[1, i], z_keep[2, i]

        def z_restore(i, side, low, high):
            natural[3, i * CY : (i + 1) * CY, :] = side
            z_keep[1, i] = low
            z_keep[2, i] = high

        backward_sweep(CZ, z_load, z_restore)

        def y_load(i):
            return y_keep[0, i], y_keep[1, i], y_keep[2, i]

        def y_restore(i, side, low, high):
            rows = pl.ds(i, CZ, stride=CY)
            natural[0, rows, :] = side
            natural[1, rows, :] = low
            natural[2, rows, :] = high

        backward_sweep(CY, y_load, y_restore)

        zb_out = z_back_out.at[step].reshape(N_GZ, 8, NX)
        zb_in = z_back.at[step].reshape(Z_OWNERS, 8, NX)
        yb_out = y_back_out.at[step].reshape(N_XY, 8, NX)
        yb_in = y_back.at[step].reshape(Y_OWNERS, 8, NX)

        @pl.when(joins_z)
        def _():
            wait_all(z_in_blocks, N_GZ - 1, z_recv.at[step])
            for h in range(LINES):
                flux = interface_fluxes(
                    lambda j: z_in[step, pl.ds(LINES * j + h, N_GZ, stride=32), :], N_GZ
                )
                z_back_out[step, pl.ds(h, N_GZ, stride=8), :] = pltpu.roll(flux, 1, 0)
                z_back_out[step, pl.ds(LINES + h, N_GZ, stride=8), :] = flux
            send_all(zb_out, zb_in, zb_send.at[step], zb_recv.at[step], "gz", z_targets, gz // 2)
            zb_in[gz // 2] = zb_out[gz]

        @pl.when(joins_y)
        def _():
            wait_all(y_in_blocks, N_XY - 1, y_recv.at[step])
            for h in range(LINES):
                flux = interface_fluxes(
                    lambda j: y_in[step, pl.ds(LINES * j + h, N_XY, stride=32), :], N_XY
                )
                y_back_out[step, pl.ds(h, N_XY, stride=8), :] = pltpu.roll(flux, 1, 0)
                y_back_out[step, pl.ds(LINES + h, N_XY, stride=8), :] = flux
            send_all(yb_out, yb_in, yb_send.at[step], yb_recv.at[step], "xy", y_targets, xy // 2)
            yb_in[xy // 2] = yb_out[xy]

        lax.fori_loop(X_FIRST, CZ // 2, solve_x, 0)
        if step == STEPS - 1:
            to_scalars.wait()
            choose()
        wait_parts(yb_in, Y_OWNERS, yb_recv.at[step], joins_y)
        wait_parts(zb_in, Z_OWNERS, zb_recv.at[step], joins_z)
        low_z = jnp.concatenate([z_back[step, pl.ds(h, Z_OWNERS, stride=8), :] for h in range(LINES)], axis=0)
        high_z = jnp.concatenate(
            [z_back[step, pl.ds(LINES + h, Z_OWNERS, stride=8), :] for h in range(LINES)], axis=0
        )

        def combine(i):
            rows = slice(i * CY, (i + 1) * CY)
            at = (i % Y_OWNERS) * 8 + i // Y_OWNERS
            low_y = y_back[step, at : at + 1, :]
            high_y = y_back[step, at + LINES : at + LINES + 1, :]
            total = base[rows, :] + natural[0, rows, :] + natural[3, rows, :]
            total = total + (low_z * z_keep[1, i] - high_z * z_keep[2, i])
            total = total + (low_y * natural[1, rows, :] - high_y * natural[2, rows, :])
            new[rows, :] = total * (1.0 / 3.0)

        if step < STEPS - 1:
            combine(0)
            combine(CZ - 1)
            send_z_halo(step + 1, new)
            for i in range(1, CZ - 1):
                combine(i)
            send_y_halo(step + 1, new)
            for way in range(2):
                wait_all(codes_in.at[way], 3, codes_recv.at[way])
            to_scalars.start()
        else:
            for chunk in range(CHUNKS):
                for way in range(2):
                    for b in range(BLOCKS_HERE):
                        combine(b * 4 + way * 2 + chunk)
                    send_near(way, chunk)

    for offset in (1, 3, 2, 0):
        for way in range(2):
            here = pl.ds(way * HALF_ROWS, HALF_ROWS)
            pass_on(way, 0, offset, 0, HALF_ROWS, lambda index: blocks[index, here, :])
    for chunk in range(CHUNKS):
        for way in range(2):
            near = gathered[way][chunk]
            wait_all(near, 2, gather_recv.at[chunk, way])
            for side, offset in ((0, 1), (1, 3)):
                rows = pl.ds(side * PASSED_ROWS, PASSED_ROWS)
                landing = pl.ds(chunk * CHUNK_ROWS + side * PASSED_ROWS, PASSED_ROWS)
                pltpu.make_async_remote_copy(
                    near.at[side, :, rows, :], gathered_far[way].at[:, landing, :],
                    far_send.at[way], far_recv.at[way],
                    device_id={"gz": partner(way, offset)}, device_id_type=MESH,
                ).start()
    for chunk in range(CHUNKS):
        for offset in (1, 3, 2, 0):
            for side in range(2):
                for way in range(2):
                    near = gathered[way][chunk]
                    pass_on(
                        way, 1 + side, offset, chunk * CHUNK_ROWS, CHUNK_ROWS, lambda index: near[side, index]
                    )
    for way in range(2):
        wait_all(gathered_far[way], BLOCKS_HERE, far_recv.at[way])
    for offset in (1, 3, 2, 0):
        for way in range(2):
            pass_on(way, 3, offset, 0, HALF_ROWS, lambda index: gathered_far[way][index])
    for way in range(2):
        for kind, part in enumerate(
            (
                packed.at[way, 0, pl.ds(0, 3)],
                packed.at[way, pl.ds(1, 2), pl.ds(0, 3)],
                packed.at[way, 3, pl.ds(0, 3)],
            )
        ):
            pltpu.make_async_copy(part, part, spread_recv.at[way, kind]).wait()
            pltpu.make_async_copy(part, part, spread_send.at[way, kind]).wait()
        for chunk in range(CHUNKS):
            wait_all(gathered[way][chunk], 2, gather_send.at[chunk, way])
        wait_all(gathered_far[way], BLOCKS_HERE, far_send.at[way])
        wait_all(codes_in.at[way], 3, codes_send.at[way])
    for step in range(STEPS):
        v = volume_ref if step == 0 else middle
        for k in range(4):
            part = v.at[pl.ds(0, CY)] if k < 2 else y_halo_out.at[step, 0]
            pltpu.make_async_copy(part, part, halo_send.at[step, k]).wait()
        wait_parts(z_out.at[step].reshape(Z_OWNERS, 32, NX), Z_OWNERS, z_send.at[step], joins_z)
        wait_parts(y_out.at[step].reshape(Y_OWNERS, 32, NX), Y_OWNERS, y_send.at[step], joins_y)

        @pl.when(joins_z)
        def _():
            wait_all(z_back_out.at[step].reshape(N_GZ, 8, NX), N_GZ - 1, zb_send.at[step])

        @pl.when(joins_y)
        def _():
            wait_all(y_back_out.at[step].reshape(N_XY, 8, NX), N_XY - 1, yb_send.at[step])


def vmem(*shape):
    return pltpu.VMEM(shape, jnp.float32)


def diffuse_and_route(volume, owners):
    dma = pltpu.SemaphoreType.DMA
    return pl.pallas_call(
        diffuse_and_route_kernel,
        out_shape=(
            jax.ShapeDtypeStruct((ROWS, NX), jnp.float32),
            jax.ShapeDtypeStruct((4, 4, MOST, BLOCK_ROWS, NX), jnp.float32),
        ),
        in_specs=[
            pl.BlockSpec(memory_space=pltpu.HBM),
            pl.BlockSpec(memory_space=pltpu.HBM),
        ],
        out_specs=(pl.BlockSpec(memory_space=pltpu.VMEM),) * 2,
        scratch_shapes=[
            vmem(ROWS, NX),
            vmem(ROWS, NX),
            vmem(STEPS, 2, CY, NX),
            vmem(STEPS, 2, CZ, NX),
            vmem(STEPS, 2, CZ, NX),
            vmem(ROWS, NX),
            vmem(3, CZ, CY, NX),
            vmem(3, CY, CZ, NX),
            vmem(4, ROWS, NX),
            vmem(ROWS, NX),
            vmem(STEPS, Z_OWNERS * 32, NX),
            vmem(STEPS, N_GZ * 32, NX),
            vmem(STEPS, Y_OWNERS * 32, NX),
            vmem(STEPS, N_XY * 32, NX),
            vmem(STEPS, N_GZ * 8, NX),
            vmem(STEPS, Z_OWNERS * 8, NX),
            vmem(STEPS, N_XY * 8, NX),
            vmem(STEPS, Y_OWNERS * 8, NX),
            dma((STEPS, 4)),
            dma((STEPS, 4)),
        ]
        + [dma((STEPS,))] * 8
        + [
            pltpu.SMEM((BLOCKS_HERE,), jnp.int32),
            dma,
            pltpu.VMEM((8, NX), jnp.int32),
            pltpu.VMEM((2, 4, 8, NX), jnp.int32),
            pltpu.SMEM((2, 4, 8, NX), jnp.int32),
            pltpu.SMEM((2, 2, 4, 4, MOST), jnp.int32),
            [[vmem(2, BLOCKS_HERE, CHUNK_ROWS, NX) for _ in range(CHUNKS)] for _ in range(2)],
            [vmem(BLOCKS_HERE, HALF_ROWS, NX) for _ in range(2)],
            vmem(2, 4, 4, MOST, HALF_ROWS, NX),
            dma,
            dma((2,)),
            dma((2,)),
            dma,
        ]
        + [dma((CHUNKS, 2))] * 2
        + [dma((2,))] * 2
        + [dma((2, 3))] * 2,
        compiler_params=pltpu.CompilerParams(
            collective_id=0, has_side_effects=True, vmem_limit_bytes=48 << 20
        ),
    )(pltpu.with_memory_space_constraint(volume, pltpu.HBM), pltpu.with_memory_space_constraint(owners, pltpu.HBM))


def write_kernel(field_ref, routed_ref, field_out, routed_out, semaphores):
    copies = [pltpu.make_async_copy(field_ref, field_out, semaphores.at[0])]
    for part in range(4):
        rows = pl.ds(part * (N_GZ * MOST // 4), N_GZ * MOST // 4)
        copies.append(
            pltpu.make_async_copy(routed_ref.at[rows], routed_out.at[rows], semaphores.at[1 + part])
        )
    for copy in copies[::-1]:
        copy.start()
    for copy in copies:
        copy.wait()


def write_out(field, routed):
    return pl.pallas_call(
        write_kernel,
        out_shape=(
            jax.ShapeDtypeStruct(field.shape, field.dtype),
            jax.ShapeDtypeStruct(routed.shape, routed.dtype),
        ),
        in_specs=[pl.BlockSpec(memory_space=pl.ANY)] * 2,
        out_specs=(pl.BlockSpec(memory_space=pltpu.HBM),) * 2,
        scratch_shapes=[pltpu.SemaphoreType.DMA((1 + 4,))],
        compiler_params=pltpu.CompilerParams(vmem_limit_bytes=8 << 20),
    )(field, routed)


def on_device(volume, owners):
    depth, height, width = volume.shape
    field, routed = diffuse_and_route(volume.reshape(depth * height, width), owners.reshape(-1))
    field, routed = write_out(field, routed.reshape(N_GZ * MOST, BLOCK_ROWS, width))
    return (field.reshape(volume.shape), routed.reshape(1, N_GZ * MOST, BLOCK_ROWS, width))


def solution(mesh):
    in_specs = (P("gz", "xy", None), P("xy", "gz", None))
    out_specs = (P("gz", "xy", None), P("xy", "gz", None, None))
    return jax.shard_map(
        on_device, mesh=mesh, in_specs=in_specs, out_specs=out_specs, check_vma=False
    )
```

```python
import jax
import jax.numpy as jnp
from jax import lax
from jax.experimental import pallas as pl
from jax.experimental.pallas import tpu as pltpu
from jax.sharding import PartitionSpec as P

STEPS = 2
MOST = 2
BLOCK_ROWS = 128

TIME_STEP = 30.0
CONTRAST = 4.0
HALF_K = 1.5 * TIME_STEP

CZ = 16
CY = 32
NX = 128
ROWS = CZ * CY
N_GZ = 16
N_XY = 8
FIELDS = 7
Z_OWNERS = 8
Y_OWNERS = 4
LINES = 4
BLOCKS_HERE = 4
HALF_ROWS = BLOCK_ROWS // 2
CHUNKS = 2
X_ROWS = 4 * CY
X_FIRST = 2
CHUNK_ROWS = HALF_ROWS // CHUNKS
PASSED_ROWS = CHUNK_ROWS // 2
MESH = pl.DeviceIdType.MESH

Z_PEERS = sorted(
    [(a, b) for a in range(4) for b in range(4) if (a, b) != (0, 0)],
    key=lambda p: -(min(p[0], 4 - p[0]) + min(p[1], 4 - p[1])),
)
Y_PEERS = sorted(
    [(a, b) for a in range(4) for b in range(2) if (a, b) != (0, 0)],
    key=lambda p: -(2 * min(p[0], 4 - p[0]) + p[1]),
)


def recip(value):
    return 1.0 / value


def pcr(diag, coupling, side, count, axis):
    stride = 1
    while stride < count:
        inverse = recip(diag)
        scaled = coupling * inverse
        side_scaled = side * inverse
        side = (
            side
            + pltpu.roll(coupling * side_scaled, stride, axis)
            + coupling * pltpu.roll(side_scaled, count - stride, axis)
        )
        diag = (
            diag
            - pltpu.roll(coupling * scaled, stride, axis)
            - coupling * coupling * pltpu.roll(inverse, count - stride, axis)
        )
        stride *= 2
        if stride < count:
            coupling = coupling * pltpu.roll(scaled, count - stride // 2, axis)
    return side * recip(diag)


def forward_sweep(count, load_v, load_g, store):
    g_here = load_g(0)
    g_first = g_here
    total = jnp.ones_like(g_here)
    side = load_v(0)
    unit = jnp.ones_like(g_here)
    first_side = jnp.zeros_like(g_here)
    first_unit = jnp.zeros_like(g_here)
    for i in range(count - 1):
        g_next = load_g(i + 1)
        weight = HALF_K * (g_here + g_next)
        inverse = recip(total + weight)
        ratio = weight * inverse
        side_scaled = side * inverse
        unit_scaled = unit * inverse
        store(i, ratio, side_scaled, unit_scaled)
        first_side = first_side + unit * side_scaled
        first_unit = first_unit + unit * unit_scaled
        total = 1.0 + ratio * total
        side = load_v(i + 1) + ratio * side
        unit = ratio * unit
        g_here = g_next
    inverse = recip(total)
    last_side = side * inverse
    last_unit = unit * inverse
    store(count - 1, inverse, last_side, last_unit)
    first_side = first_side + unit * last_side
    first_unit = first_unit + unit * last_unit
    return (first_side, last_side, first_unit, last_unit, inverse, g_first, g_here)


def backward_sweep(count, load, store):
    high_unit, side, low_unit = load(count - 1)
    store(count - 1, side, low_unit, high_unit)
    for i in range(count - 2, -1, -1):
        ratio, side_scaled, unit_scaled = load(i)
        side = side_scaled + ratio * side
        low_unit = unit_scaled + ratio * low_unit
        high_unit = ratio * high_unit
        store(i, side, low_unit, high_unit)


def interface_fluxes(received, count):
    first_side, last_side, first_unit, cross, last_unit, g_first, g_last = [received(j) for j in range(FIELDS)]
    index = lax.broadcasted_iota(jnp.int32, (count, NX), 0)

    def following(field):
        return pltpu.roll(field, count - 1, 0)

    weight = HALF_K * (g_last + following(g_first))
    diag = recip(weight) + last_unit + following(first_unit)
    side = last_side - following(first_side)
    diag = jnp.where(index < count - 1, diag, 1.0)
    side = jnp.where(index < count - 1, side, 0.0)
    coupling = jnp.where(index < count - 2, following(cross), 0.0)
    return pcr(diag, coupling, side, count, 0)


def diffuse_and_route_kernel(
    volume_hbm,
    owners_hbm,
    out_ref,
    routed_ref,
    volume_ref,
    middle,
    z_halo,
    y_halo_out,
    y_halo,
    g_ref,
    z_keep,
    y_keep,
    natural,
    base,
    z_out,
    z_in,
    y_out,
    y_in,
    z_back_out,
    z_back,
    y_back_out,
    y_back,
    halo_send,
    halo_recv,
    z_send,
    z_recv,
    y_send,
    y_recv,
    zb_send,
    zb_recv,
    yb_send,
    yb_recv,
    owners_ref,
    owners_sem,
    codes_out,
    codes_in,
    codes,
    choice,
    gathered,
    gathered_far,
    packed,
    volume_sem,
    codes_send,
    codes_recv,
    codes_sem,
    gather_send,
    gather_recv,
    far_send,
    far_recv,
    spread_send,
    spread_recv,
):
    gz = lax.axis_index("gz")
    xy = lax.axis_index("xy")
    z_targets = [
        lax.rem(gz // 4 + dz, 4) * 4 + lax.rem(lax.rem(gz, 4) + dy, 4) for dz, dy in Z_PEERS
    ]
    y_targets = [
        lax.rem(xy // 2 + dx, 4) * 2 + lax.rem(lax.rem(xy, 2) + core, 2) for dx, core in Y_PEERS
    ]
    odd = lax.rem(gz + xy, 2)
    joins_z = odd == 0
    joins_y = odd == 1
    z_owners = [
        (lax.rem(gz // 4 + dz, 4) * 4 + lax.rem(lax.rem(gz, 4) + dy + odd, 4), (dz, dy) == (0, 0))
        for dz, dy in ((2, 2), (1, 2), (3, 2), (2, 0), (1, 0), (3, 0), (0, 2), (0, 0))
    ]
    y_owners = [
        (lax.rem(xy // 2 + dx, 4) * 2 + lax.rem(lax.rem(xy, 2) + 1 - odd, 2), dx == 0) for dx in (2, 1, 3, 0)
    ]
    barrier = pltpu.get_barrier_semaphore()
    for target in z_targets:
        pl.semaphore_signal(barrier, 1, device_id={"gz": target}, device_id_type=MESH)
    for target in y_targets:
        pl.semaphore_signal(barrier, 1, device_id={"xy": target}, device_id_type=MESH)
    load_volume = pltpu.make_async_copy(volume_hbm, volume_ref, volume_sem)
    load_volume.start()
    load_owners = pltpu.make_async_copy(owners_hbm, owners_ref, owners_sem)
    load_owners.start()
    pl.semaphore_wait(barrier, N_GZ + N_XY - 2)

    chip_z, chip_y = gz // 4, lax.rem(gz, 4)
    places = [chip_y, chip_z]

    def partner(way, offset):
        if way == 0:
            return chip_z * 4 + lax.rem(chip_y + offset, 4)
        return lax.rem(chip_z + offset, 4) * 4 + chip_y

    load_volume.wait()

    row_index = lax.broadcasted_iota(jnp.int32, (CY, NX), 0)
    lane_index = lax.broadcasted_iota(jnp.int32, (CY, NX), 1)

    blocks = out_ref.reshape(BLOCKS_HERE, BLOCK_ROWS, NX)
    to_scalars = pltpu.make_async_copy(codes_in, codes, codes_sem)

    def place_of(way, source):
        return lax.rem(places[way] + (0, 3, 1, 2)[source], 4)

    def choose():
        for way in range(2):
            for source in range(4):
                place = place_of(way, source)
                for offset in range(4):
                    target = partner(1 - way, offset)
                    for rank in range(MOST):
                        index, found = 0, 0
                        for b in range(BLOCKS_HERE):
                            hit = (codes[way, place, 0, b] == target * MOST + rank).astype(jnp.int32)
                            index = index + b * hit
                            found = found + hit
                        choice[0, way, source, offset, rank] = index
                        choice[1, way, source, offset, rank] = found

    def send_near(way, chunk):
        here = pl.ds(way * HALF_ROWS + chunk * CHUNK_ROWS, CHUNK_ROWS)
        for side, offset in ((0, 1), (1, 3)):
            pltpu.make_async_remote_copy(
                blocks.at[:, here, :], gathered[way][chunk].at[side],
                gather_send.at[chunk, way], gather_recv.at[chunk, way],
                device_id={"gz": partner(way, offset)}, device_id_type=MESH,
            ).start()

    def pass_on(way, source, offset, first, count, read):
        there = pl.ds(first, count)
        final = pl.ds(way * HALF_ROWS + first, count)
        place = place_of(way, source)
        at = (chip_z, place) if way == 0 else (place, chip_y)
        for rank in range(MOST):
            found = choice[1, way, source, offset, rank]
            rows = jnp.where(found > 0, read(choice[0, way, source, offset, rank]), 0.0)
            if offset:
                packed[way, source, offset, rank, there, :] = rows
            else:
                routed_ref[at[0], at[1], rank, final, :] = rows
        if offset:
            kind = (0, 1, 1, 2)[source]
            pltpu.make_async_remote_copy(
                packed.at[way, source, offset, :, there, :], routed_ref.at[at[0], at[1], :, final, :],
                spread_send.at[way, kind], spread_recv.at[way, kind],
                device_id={"gz": partner(1 - way, offset)}, device_id_type=MESH,
            ).start()

    def send_all(source, landing, send_sem, recv_sem, axis, targets, me):
        for target in targets:
            pltpu.make_async_remote_copy(
                source.at[target], landing.at[me], send_sem, recv_sem,
                device_id={axis: target}, device_id_type=MESH,
            ).start()

    def send_parts(source, landing, send_sem, recv_sem, axis, owners, me, is_owner):
        for target, may_be_self in owners:
            copy = pltpu.make_async_remote_copy(
                source.at[target // 2], landing.at[me], send_sem, recv_sem,
                device_id={axis: target}, device_id_type=MESH,
            )
            if may_be_self:
                pl.when(jnp.logical_not(is_owner))(copy.start)

                @pl.when(is_owner)
                def _():
                    landing[me] = source[target // 2]

            else:
                copy.start()

    def wait_parts(buffer, count, semaphore, is_owner):
        @pl.when(is_owner)
        def _():
            wait_all(buffer, count - 1, semaphore)

        @pl.when(jnp.logical_not(is_owner))
        def _():
            wait_all(buffer, count, semaphore)

    def wait_all(buffer, count, semaphore):
        part = buffer.at[pl.ds(0, count)]
        pltpu.make_async_copy(part, part, semaphore).wait()

    def halo_copies(step, v, which):
        copies = []
        for k, (axis, me, count, forward) in enumerate(
            [("gz", gz, N_GZ, 0), ("gz", gz, N_GZ, 1), ("xy", xy, N_XY, 0), ("xy", xy, N_XY, 1)]
        ):
            if axis != which:
                continue
            target = lax.rem(me + (1 if forward else count - 1), count)
            if axis == "gz":
                source = v.at[pl.ds((CZ - 1) * CY if forward else 0, CY)]
                landing = z_halo.at[step, 1 - forward]
            else:
                source = y_halo_out.at[step, forward]
                landing = y_halo.at[step, 1 - forward]
            copies.append(
                pltpu.make_async_remote_copy(
                    source, landing, halo_send.at[step, k], halo_recv.at[step, k],
                    device_id={axis: target}, device_id_type=MESH,
                )
            )
        return copies

    def send_z_halo(step, v):
        for copy in halo_copies(step, v, "gz"):
            copy.start()

    def send_y_halo(step, v):
        y_halo_out[step, 0] = v[pl.ds(0, CZ, stride=CY), :]
        y_halo_out[step, 1] = v[pl.ds(CY - 1, CZ, stride=CY), :]
        for copy in halo_copies(step, v, "xy"):
            copy.start()

    send_z_halo(0, volume_ref)
    send_y_halo(0, volume_ref)
    load_owners.wait()
    lanes = lax.broadcasted_iota(jnp.int32, (8, NX), 1)
    code_tile = jnp.zeros((8, NX), jnp.int32)
    for b in range(BLOCKS_HERE):
        rank = 0
        for earlier in range(b):
            rank = rank + (owners_ref[earlier] == owners_ref[b]).astype(jnp.int32)
        code_tile = jnp.where(lanes == b, owners_ref[b] * MOST + rank, code_tile)
    codes_out[...] = code_tile
    for way in range(2):
        codes_in[way, places[way]] = code_tile
        for offset in (2, 1, 3):
            pltpu.make_async_remote_copy(
                codes_out, codes_in.at[way, places[way]], codes_send.at[way], codes_recv.at[way],
                device_id={"gz": partner(way, offset)}, device_id_type=MESH,
            ).start()
    for step in range(STEPS):
        v = volume_ref if step == 0 else middle
        new = out_ref if step == STEPS - 1 else middle

        def plane(i):
            return v[i * CY : (i + 1) * CY, :]

        def diffuse(i, before, above):
            here = plane(i)
            slope_z = above - before
            y_low = jnp.where(xy == 0, here[0:1, :], y_halo[step, 0, i : i + 1, :])
            y_high = jnp.where(xy == N_XY - 1, here[CY - 1 : CY, :], y_halo[step, 1, i : i + 1, :])
            y_prev = jnp.where(row_index == 0, y_low, pltpu.roll(here, 1, 0))
            y_next = jnp.where(row_index == CY - 1, y_high, pltpu.roll(here, CY - 1, 0))
            slope_y = y_next - y_prev
            x_prev = jnp.where(lane_index == 0, here, pltpu.roll(here, 1, 1))
            x_next = jnp.where(lane_index == NX - 1, here, pltpu.roll(here, NX - 1, 1))
            slope_x = x_next - x_prev
            squares = slope_z * slope_z + slope_y * slope_y + slope_x * slope_x
            g_ref[i * CY : (i + 1) * CY, :] = recip(1.0 + squares * (0.25 / CONTRAST))

        for copy in halo_copies(step, v, "xy"):
            copy.wait_recv()
        for i in range(1, CZ - 1):
            diffuse(i, plane(i - 1), plane(i + 1))
        for copy in halo_copies(step, v, "gz"):
            copy.wait_recv()
        diffuse(0, jnp.where(gz == 0, plane(0), z_halo[step, 0]), plane(1))
        diffuse(CZ - 1, plane(CZ - 2), jnp.where(gz == N_GZ - 1, plane(CZ - 1), z_halo[step, 1]))

        def z_store(i, ratio, side, unit):
            z_keep[0, i] = ratio
            z_keep[1, i] = side
            z_keep[2, i] = unit

        ends = forward_sweep(CZ, plane, lambda i: g_ref[i * CY : (i + 1) * CY, :], z_store)
        for j, field in enumerate(ends):
            for h in range(LINES):
                z_out[step, pl.ds(LINES * j + h, Z_OWNERS, stride=32), :] = field[h * Z_OWNERS : (h + 1) * Z_OWNERS, :]
        z_in_blocks = z_in.at[step].reshape(N_GZ, 32, NX)
        z_out_blocks = z_out.at[step].reshape(Z_OWNERS, 32, NX)
        send_parts(z_out_blocks, z_in_blocks, z_send.at[step], z_recv.at[step], "gz", z_owners, gz, joins_z)

        def y_store(i, ratio, side, unit):
            y_keep[0, i] = ratio
            y_keep[1, i] = side
            y_keep[2, i] = unit

        ends = forward_sweep(
            CY,
            lambda i: v[pl.ds(i, CZ, stride=CY), :],
            lambda i: g_ref[pl.ds(i, CZ, stride=CY), :],
            y_store,
        )
        for j, field in enumerate(ends):
            for h in range(LINES):
                y_out[step, pl.ds(LINES * j + h, Y_OWNERS, stride=32), :] = field[h * Y_OWNERS : (h + 1) * Y_OWNERS, :]
        y_in_blocks = y_in.at[step].reshape(N_XY, 32, NX)
        y_out_blocks = y_out.at[step].reshape(Y_OWNERS, 32, NX)
        send_parts(y_out_blocks, y_in_blocks, y_send.at[step], y_recv.at[step], "xy", y_owners, xy, joins_y)

        def solve_x(i, carry):
            rows = pl.ds(pl.multiple_of(i * X_ROWS, X_ROWS), X_ROWS)
            g = g_ref[rows, :]
            lanes = lax.broadcasted_iota(jnp.int32, (X_ROWS, NX), 1)
            weight = jnp.where(lanes < NX - 1, HALF_K * (g + pltpu.roll(g, NX - 1, 1)), 0.0)
            diag = 1.0 + weight + pltpu.roll(weight, 1, 1)
            base[rows, :] = pcr(diag, weight, v[rows, :], NX, 1)
            return carry

        lax.fori_loop(0, X_FIRST, solve_x, 0)

        def z_load(i):
            return z_keep[0, i], z_keep[1, i], z_keep[2, i]

        def z_restore(i, side, low, high):
            natural[3, i * CY : (i + 1) * CY, :] = side
            z_keep[1, i] = low
            z_keep[2, i] = high

        backward_sweep(CZ, z_load, z_restore)

        def y_load(i):
            return y_keep[0, i], y_keep[1, i], y_keep[2, i]

        def y_restore(i, side, low, high):
            rows = pl.ds(i, CZ, stride=CY)
            natural[0, rows, :] = side
            natural[1, rows, :] = low
            natural[2, rows, :] = high

        backward_sweep(CY, y_load, y_restore)

        zb_out = z_back_out.at[step].reshape(N_GZ, 8, NX)
        zb_in = z_back.at[step].reshape(Z_OWNERS, 8, NX)
        yb_out = y_back_out.at[step].reshape(N_XY, 8, NX)
        yb_in = y_back.at[step].reshape(Y_OWNERS, 8, NX)

        @pl.when(joins_z)
        def _():
            wait_all(z_in_blocks, N_GZ - 1, z_recv.at[step])
            for h in range(LINES):
                flux = interface_fluxes(
                    lambda j: z_in[step, pl.ds(LINES * j + h, N_GZ, stride=32), :], N_GZ
                )
                z_back_out[step, pl.ds(h, N_GZ, stride=8), :] = pltpu.roll(flux, 1, 0)
                z_back_out[step, pl.ds(LINES + h, N_GZ, stride=8), :] = flux
            send_all(zb_out, zb_in, zb_send.at[step], zb_recv.at[step], "gz", z_targets, gz // 2)
            zb_in[gz // 2] = zb_out[gz]

        @pl.when(joins_y)
        def _():
            wait_all(y_in_blocks, N_XY - 1, y_recv.at[step])
            for h in range(LINES):
                flux = interface_fluxes(
                    lambda j: y_in[step, pl.ds(LINES * j + h, N_XY, stride=32), :], N_XY
                )
                y_back_out[step, pl.ds(h, N_XY, stride=8), :] = pltpu.roll(flux, 1, 0)
                y_back_out[step, pl.ds(LINES + h, N_XY, stride=8), :] = flux
            send_all(yb_out, yb_in, yb_send.at[step], yb_recv.at[step], "xy", y_targets, xy // 2)
            yb_in[xy // 2] = yb_out[xy]

        lax.fori_loop(X_FIRST, ROWS // X_ROWS, solve_x, 0)
        wait_parts(yb_in, Y_OWNERS, yb_recv.at[step], joins_y)
        wait_parts(zb_in, Z_OWNERS, zb_recv.at[step], joins_z)
        low_z = jnp.concatenate([z_back[step, pl.ds(h, Z_OWNERS, stride=8), :] for h in range(LINES)], axis=0)
        high_z = jnp.concatenate(
            [z_back[step, pl.ds(LINES + h, Z_OWNERS, stride=8), :] for h in range(LINES)], axis=0
        )

        def combine(i):
            rows = slice(i * CY, (i + 1) * CY)
            at = (i % Y_OWNERS) * 8 + i // Y_OWNERS
            low_y = y_back[step, at : at + 1, :]
            high_y = y_back[step, at + LINES : at + LINES + 1, :]
            total = base[rows, :] + natural[0, rows, :] + natural[3, rows, :]
            total = total + (low_z * z_keep[1, i] - high_z * z_keep[2, i])
            total = total + (low_y * natural[1, rows, :] - high_y * natural[2, rows, :])
            new[rows, :] = total * (1.0 / 3.0)

        if step < STEPS - 1:
            combine(0)
            combine(CZ - 1)
            send_z_halo(step + 1, new)
            for i in range(1, CZ - 1):
                combine(i)
            send_y_halo(step + 1, new)
            for way in range(2):
                wait_all(codes_in.at[way], 3, codes_recv.at[way])
            to_scalars.start()
            to_scalars.wait()
            choose()
        else:
            for chunk in range(CHUNKS):
                for way in range(2):
                    for b in range(BLOCKS_HERE):
                        combine(b * 4 + way * 2 + chunk)
                    send_near(way, chunk)

    for offset in (1, 3, 2, 0):
        for way in range(2):
            here = pl.ds(way * HALF_ROWS, HALF_ROWS)
            pass_on(way, 0, offset, 0, HALF_ROWS, lambda index: blocks[index, here, :])
    for chunk in range(CHUNKS):
        for way in range(2):
            near = gathered[way][chunk]
            wait_all(near, 2, gather_recv.at[chunk, way])
            for side, offset in ((0, 1), (1, 3)):
                rows = pl.ds(side * PASSED_ROWS, PASSED_ROWS)
                landing = pl.ds(chunk * CHUNK_ROWS + side * PASSED_ROWS, PASSED_ROWS)
                pltpu.make_async_remote_copy(
                    near.at[side, :, rows, :], gathered_far[way].at[:, landing, :],
                    far_send.at[way], far_recv.at[way],
                    device_id={"gz": partner(way, offset)}, device_id_type=MESH,
                ).start()
    for chunk in range(CHUNKS):
        for offset in (1, 3, 2, 0):
            for side in range(2):
                for way in range(2):
                    near = gathered[way][chunk]
                    pass_on(
                        way, 1 + side, offset, chunk * CHUNK_ROWS, CHUNK_ROWS, lambda index: near[side, index]
                    )
    for way in range(2):
        wait_all(gathered_far[way], BLOCKS_HERE, far_recv.at[way])
    for offset in (1, 3, 2, 0):
        for way in range(2):
            pass_on(way, 3, offset, 0, HALF_ROWS, lambda index: gathered_far[way][index])
    for way in range(2):
        for kind, part in enumerate(
            (
                packed.at[way, 0, pl.ds(0, 3)],
                packed.at[way, pl.ds(1, 2), pl.ds(0, 3)],
                packed.at[way, 3, pl.ds(0, 3)],
            )
        ):
            pltpu.make_async_copy(part, part, spread_recv.at[way, kind]).wait()
            pltpu.make_async_copy(part, part, spread_send.at[way, kind]).wait()
        for chunk in range(CHUNKS):
            wait_all(gathered[way][chunk], 2, gather_send.at[chunk, way])
        wait_all(gathered_far[way], BLOCKS_HERE, far_send.at[way])
        wait_all(codes_in.at[way], 3, codes_send.at[way])
    for step in range(STEPS):
        v = volume_ref if step == 0 else middle
        for k in range(4):
            part = v.at[pl.ds(0, CY)] if k < 2 else y_halo_out.at[step, 0]
            pltpu.make_async_copy(part, part, halo_send.at[step, k]).wait()
        wait_parts(z_out.at[step].reshape(Z_OWNERS, 32, NX), Z_OWNERS, z_send.at[step], joins_z)
        wait_parts(y_out.at[step].reshape(Y_OWNERS, 32, NX), Y_OWNERS, y_send.at[step], joins_y)

        @pl.when(joins_z)
        def _():
            wait_all(z_back_out.at[step].reshape(N_GZ, 8, NX), N_GZ - 1, zb_send.at[step])

        @pl.when(joins_y)
        def _():
            wait_all(y_back_out.at[step].reshape(N_XY, 8, NX), N_XY - 1, yb_send.at[step])


def vmem(*shape):
    return pltpu.VMEM(shape, jnp.float32)


def diffuse_and_route(volume, owners):
    dma = pltpu.SemaphoreType.DMA
    return pl.pallas_call(
        diffuse_and_route_kernel,
        out_shape=(
            jax.ShapeDtypeStruct((ROWS, NX), jnp.float32),
            jax.ShapeDtypeStruct((4, 4, MOST, BLOCK_ROWS, NX), jnp.float32),
        ),
        in_specs=[
            pl.BlockSpec(memory_space=pltpu.HBM),
            pl.BlockSpec(memory_space=pltpu.HBM),
        ],
        out_specs=(pl.BlockSpec(memory_space=pltpu.VMEM),) * 2,
        scratch_shapes=[
            vmem(ROWS, NX),
            vmem(ROWS, NX),
            vmem(STEPS, 2, CY, NX),
            vmem(STEPS, 2, CZ, NX),
            vmem(STEPS, 2, CZ, NX),
            vmem(ROWS, NX),
            vmem(3, CZ, CY, NX),
            vmem(3, CY, CZ, NX),
            vmem(4, ROWS, NX),
            vmem(ROWS, NX),
            vmem(STEPS, Z_OWNERS * 32, NX),
            vmem(STEPS, N_GZ * 32, NX),
            vmem(STEPS, Y_OWNERS * 32, NX),
            vmem(STEPS, N_XY * 32, NX),
            vmem(STEPS, N_GZ * 8, NX),
            vmem(STEPS, Z_OWNERS * 8, NX),
            vmem(STEPS, N_XY * 8, NX),
            vmem(STEPS, Y_OWNERS * 8, NX),
            dma((STEPS, 4)),
            dma((STEPS, 4)),
        ]
        + [dma((STEPS,))] * 8
        + [
            pltpu.SMEM((BLOCKS_HERE,), jnp.int32),
            dma,
            pltpu.VMEM((8, NX), jnp.int32),
            pltpu.VMEM((2, 4, 8, NX), jnp.int32),
            pltpu.SMEM((2, 4, 8, NX), jnp.int32),
            pltpu.SMEM((2, 2, 4, 4, MOST), jnp.int32),
            [[vmem(2, BLOCKS_HERE, CHUNK_ROWS, NX) for _ in range(CHUNKS)] for _ in range(2)],
            [vmem(BLOCKS_HERE, HALF_ROWS, NX) for _ in range(2)],
            vmem(2, 4, 4, MOST, HALF_ROWS, NX),
            dma,
            dma((2,)),
            dma((2,)),
            dma,
        ]
        + [dma((CHUNKS, 2))] * 2
        + [dma((2,))] * 2
        + [dma((2, 3))] * 2,
        compiler_params=pltpu.CompilerParams(
            collective_id=0, has_side_effects=True, vmem_limit_bytes=48 << 20
        ),
    )(pltpu.with_memory_space_constraint(volume, pltpu.HBM), pltpu.with_memory_space_constraint(owners, pltpu.HBM))


def write_kernel(field_ref, routed_ref, field_out, routed_out, semaphores):
    copies = [pltpu.make_async_copy(field_ref, field_out, semaphores.at[0])]
    for part in range(4):
        rows = pl.ds(part * (N_GZ * MOST // 4), N_GZ * MOST // 4)
        copies.append(
            pltpu.make_async_copy(routed_ref.at[rows], routed_out.at[rows], semaphores.at[1 + part])
        )
    for copy in copies[::-1]:
        copy.start()
    for copy in copies:
        copy.wait()


def write_out(field, routed):
    return pl.pallas_call(
        write_kernel,
        out_shape=(
            jax.ShapeDtypeStruct(field.shape, field.dtype),
            jax.ShapeDtypeStruct(routed.shape, routed.dtype),
        ),
        in_specs=[pl.BlockSpec(memory_space=pl.ANY)] * 2,
        out_specs=(pl.BlockSpec(memory_space=pltpu.HBM),) * 2,
        scratch_shapes=[pltpu.SemaphoreType.DMA((1 + 4,))],
        compiler_params=pltpu.CompilerParams(vmem_limit_bytes=8 << 20),
    )(field, routed)


def on_device(volume, owners):
    depth, height, width = volume.shape
    field, routed = diffuse_and_route(volume.reshape(depth * height, width), owners.reshape(-1))
    field, routed = write_out(field, routed.reshape(N_GZ * MOST, BLOCK_ROWS, width))
    return (field.reshape(volume.shape), routed.reshape(1, N_GZ * MOST, BLOCK_ROWS, width))


def solution(mesh):
    in_specs = (P("gz", "xy", None), P("xy", "gz", None))
    out_specs = (P("gz", "xy", None), P("xy", "gz", None, None))
    return jax.shard_map(
        on_device, mesh=mesh, in_specs=in_specs, out_specs=out_specs, check_vma=False
    )
```

```python
import jax
import jax.numpy as jnp
from jax import lax
from jax.experimental import pallas as pl
from jax.experimental.pallas import tpu as pltpu
from jax.sharding import PartitionSpec as P

STEPS = 2
MOST = 2
BLOCK_ROWS = 128

TIME_STEP = 30.0
CONTRAST = 4.0
HALF_K = 1.5 * TIME_STEP

CZ = 16
CY = 32
NX = 128
ROWS = CZ * CY
N_GZ = 16
N_XY = 8
FIELDS = 7
Z_OWNERS = 8
Y_OWNERS = 4
LINES = 4
BLOCKS_HERE = 4
HALF_ROWS = BLOCK_ROWS // 2
CHUNKS = 2
X_ROWS = 4 * CY
X_FIRST = 2
CHUNK_ROWS = HALF_ROWS // CHUNKS
MESH = pl.DeviceIdType.MESH

Z_PEERS = sorted(
    [(a, b) for a in range(4) for b in range(4) if (a, b) != (0, 0)],
    key=lambda p: -(min(p[0], 4 - p[0]) + min(p[1], 4 - p[1])),
)
Y_PEERS = sorted(
    [(a, b) for a in range(4) for b in range(2) if (a, b) != (0, 0)],
    key=lambda p: -(2 * min(p[0], 4 - p[0]) + p[1]),
)


def recip(value):
    return 1.0 / value


def pcr(diag, coupling, side, count, axis):
    stride = 1
    while stride < count:
        inverse = recip(diag)
        scaled = coupling * inverse
        side_scaled = side * inverse
        side = (
            side
            + pltpu.roll(coupling * side_scaled, stride, axis)
            + coupling * pltpu.roll(side_scaled, count - stride, axis)
        )
        diag = (
            diag
            - pltpu.roll(coupling * scaled, stride, axis)
            - coupling * coupling * pltpu.roll(inverse, count - stride, axis)
        )
        stride *= 2
        if stride < count:
            coupling = coupling * pltpu.roll(scaled, count - stride // 2, axis)
    return side * recip(diag)


def forward_sweep(count, load_v, load_g, store):
    g_here = load_g(0)
    g_first = g_here
    total = jnp.ones_like(g_here)
    side = load_v(0)
    unit = jnp.ones_like(g_here)
    first_side = jnp.zeros_like(g_here)
    first_unit = jnp.zeros_like(g_here)
    for i in range(count - 1):
        g_next = load_g(i + 1)
        weight = HALF_K * (g_here + g_next)
        inverse = recip(total + weight)
        ratio = weight * inverse
        side_scaled = side * inverse
        unit_scaled = unit * inverse
        store(i, ratio, side_scaled, unit_scaled)
        first_side = first_side + unit * side_scaled
        first_unit = first_unit + unit * unit_scaled
        total = 1.0 + ratio * total
        side = load_v(i + 1) + ratio * side
        unit = ratio * unit
        g_here = g_next
    inverse = recip(total)
    last_side = side * inverse
    last_unit = unit * inverse
    store(count - 1, inverse, last_side, last_unit)
    first_side = first_side + unit * last_side
    first_unit = first_unit + unit * last_unit
    return (first_side, last_side, first_unit, last_unit, inverse, g_first, g_here)


def backward_sweep(count, load, store):
    high_unit, side, low_unit = load(count - 1)
    store(count - 1, side, low_unit, high_unit)
    for i in range(count - 2, -1, -1):
        ratio, side_scaled, unit_scaled = load(i)
        side = side_scaled + ratio * side
        low_unit = unit_scaled + ratio * low_unit
        high_unit = ratio * high_unit
        store(i, side, low_unit, high_unit)


def interface_fluxes(received, count):
    first_side, last_side, first_unit, cross, last_unit, g_first, g_last = [received(j) for j in range(FIELDS)]
    index = lax.broadcasted_iota(jnp.int32, (count, NX), 0)

    def following(field):
        return pltpu.roll(field, count - 1, 0)

    weight = HALF_K * (g_last + following(g_first))
    diag = recip(weight) + last_unit + following(first_unit)
    side = last_side - following(first_side)
    diag = jnp.where(index < count - 1, diag, 1.0)
    side = jnp.where(index < count - 1, side, 0.0)
    coupling = jnp.where(index < count - 2, following(cross), 0.0)
    return pcr(diag, coupling, side, count, 0)


def diffuse_and_route_kernel(
    volume_hbm,
    owners_hbm,
    out_ref,
    routed_ref,
    volume_ref,
    middle,
    z_halo,
    y_halo_out,
    y_halo,
    g_ref,
    z_keep,
    y_keep,
    natural,
    base,
    z_out,
    z_in,
    y_out,
    y_in,
    z_back_out,
    z_back,
    y_back_out,
    y_back,
    halo_send,
    halo_recv,
    z_send,
    z_recv,
    y_send,
    y_recv,
    zb_send,
    zb_recv,
    yb_send,
    yb_recv,
    owners_ref,
    owners_sem,
    codes_out,
    codes_in,
    codes,
    choice,
    gathered,
    gathered_far,
    packed,
    volume_sem,
    codes_send,
    codes_recv,
    codes_sem,
    gather_send,
    gather_recv,
    far_send,
    far_recv,
    spread_send,
    spread_recv,
):
    gz = lax.axis_index("gz")
    xy = lax.axis_index("xy")
    z_targets = [
        lax.rem(gz // 4 + dz, 4) * 4 + lax.rem(lax.rem(gz, 4) + dy, 4) for dz, dy in Z_PEERS
    ]
    y_targets = [
        lax.rem(xy // 2 + dx, 4) * 2 + lax.rem(lax.rem(xy, 2) + core, 2) for dx, core in Y_PEERS
    ]
    odd = lax.rem(gz + xy, 2)
    joins_z = odd == 0
    joins_y = odd == 1
    z_owners = [
        (lax.rem(gz // 4 + dz, 4) * 4 + lax.rem(lax.rem(gz, 4) + dy + odd, 4), (dz, dy) == (0, 0))
        for dz, dy in ((2, 2), (1, 2), (3, 2), (2, 0), (1, 0), (3, 0), (0, 2), (0, 0))
    ]
    y_owners = [
        (lax.rem(xy // 2 + dx, 4) * 2 + lax.rem(lax.rem(xy, 2) + 1 - odd, 2), dx == 0) for dx in (2, 1, 3, 0)
    ]
    barrier = pltpu.get_barrier_semaphore()
    for target in z_targets:
        pl.semaphore_signal(barrier, 1, device_id={"gz": target}, device_id_type=MESH)
    for target in y_targets:
        pl.semaphore_signal(barrier, 1, device_id={"xy": target}, device_id_type=MESH)
    load_volume = pltpu.make_async_copy(volume_hbm, volume_ref, volume_sem)
    load_volume.start()
    load_owners = pltpu.make_async_copy(owners_hbm, owners_ref, owners_sem)
    load_owners.start()
    pl.semaphore_wait(barrier, N_GZ + N_XY - 2)

    chip_z, chip_y = gz // 4, lax.rem(gz, 4)
    places = [chip_y, chip_z]

    def partner(way, offset):
        if way == 0:
            return chip_z * 4 + lax.rem(chip_y + offset, 4)
        return lax.rem(chip_z + offset, 4) * 4 + chip_y

    load_volume.wait()

    row_index = lax.broadcasted_iota(jnp.int32, (CY, NX), 0)
    lane_index = lax.broadcasted_iota(jnp.int32, (CY, NX), 1)

    blocks = out_ref.reshape(BLOCKS_HERE, BLOCK_ROWS, NX)
    to_scalars = pltpu.make_async_copy(codes_in, codes, codes_sem)

    def place_of(way, source):
        return lax.rem(places[way] + (0, 3, 1, 2)[source], 4)

    def choose():
        for way in range(2):
            for source in range(4):
                place = place_of(way, source)
                for offset in range(4):
                    target = partner(1 - way, offset)
                    for rank in range(MOST):
                        index, found = 0, 0
                        for b in range(BLOCKS_HERE):
                            hit = (codes[way, place, 0, b] == target * MOST + rank).astype(jnp.int32)
                            index = index + b * hit
                            found = found + hit
                        choice[0, way, source, offset, rank] = index
                        choice[1, way, source, offset, rank] = found

    def send_near(way, chunk):
        here = pl.ds(way * HALF_ROWS + chunk * CHUNK_ROWS, CHUNK_ROWS)
        for side, offset in ((0, 1), (1, 3)):
            pltpu.make_async_remote_copy(
                blocks.at[:, here, :], gathered[way][chunk].at[side],
                gather_send.at[chunk, way], gather_recv.at[chunk, way],
                device_id={"gz": partner(way, offset)}, device_id_type=MESH,
            ).start()

    def pass_on(way, source, offset, first, count, read):
        there = pl.ds(first, count)
        final = pl.ds(way * HALF_ROWS + first, count)
        place = place_of(way, source)
        at = (chip_z, place) if way == 0 else (place, chip_y)
        for rank in range(MOST):
            found = choice[1, way, source, offset, rank]
            rows = jnp.where(found > 0, read(choice[0, way, source, offset, rank]), 0.0)
            if offset:
                packed[way, source, offset, rank, there, :] = rows
            else:
                routed_ref[at[0], at[1], rank, final, :] = rows
        if offset:
            kind = (0, 1, 1, 2)[source]
            pltpu.make_async_remote_copy(
                packed.at[way, source, offset, :, there, :], routed_ref.at[at[0], at[1], :, final, :],
                spread_send.at[way, kind], spread_recv.at[way, kind],
                device_id={"gz": partner(1 - way, offset)}, device_id_type=MESH,
            ).start()

    def send_all(source, landing, send_sem, recv_sem, axis, targets, me):
        for target in targets:
            pltpu.make_async_remote_copy(
                source.at[target], landing.at[me], send_sem, recv_sem,
                device_id={axis: target}, device_id_type=MESH,
            ).start()

    def send_parts(source, landing, send_sem, recv_sem, axis, owners, me, is_owner):
        for target, may_be_self in owners:
            copy = pltpu.make_async_remote_copy(
                source.at[target // 2], landing.at[me], send_sem, recv_sem,
                device_id={axis: target}, device_id_type=MESH,
            )
            if may_be_self:
                pl.when(jnp.logical_not(is_owner))(copy.start)

                @pl.when(is_owner)
                def _():
                    landing[me] = source[target // 2]

            else:
                copy.start()

    def wait_parts(buffer, count, semaphore, is_owner):
        @pl.when(is_owner)
        def _():
            wait_all(buffer, count - 1, semaphore)

        @pl.when(jnp.logical_not(is_owner))
        def _():
            wait_all(buffer, count, semaphore)

    def wait_all(buffer, count, semaphore):
        part = buffer.at[pl.ds(0, count)]
        pltpu.make_async_copy(part, part, semaphore).wait()

    def halo_copies(step, v, which):
        copies = []
        for k, (axis, me, count, forward) in enumerate(
            [("gz", gz, N_GZ, 0), ("gz", gz, N_GZ, 1), ("xy", xy, N_XY, 0), ("xy", xy, N_XY, 1)]
        ):
            if axis != which:
                continue
            target = lax.rem(me + (1 if forward else count - 1), count)
            if axis == "gz":
                source = v.at[pl.ds((CZ - 1) * CY if forward else 0, CY)]
                landing = z_halo.at[step, 1 - forward]
            else:
                source = y_halo_out.at[step, forward]
                landing = y_halo.at[step, 1 - forward]
            copies.append(
                pltpu.make_async_remote_copy(
                    source, landing, halo_send.at[step, k], halo_recv.at[step, k],
                    device_id={axis: target}, device_id_type=MESH,
                )
            )
        return copies

    def send_z_halo(step, v):
        for copy in halo_copies(step, v, "gz"):
            copy.start()

    def send_y_halo(step, v):
        y_halo_out[step, 0] = v[pl.ds(0, CZ, stride=CY), :]
        y_halo_out[step, 1] = v[pl.ds(CY - 1, CZ, stride=CY), :]
        for copy in halo_copies(step, v, "xy"):
            copy.start()

    send_z_halo(0, volume_ref)
    send_y_halo(0, volume_ref)
    load_owners.wait()
    lanes = lax.broadcasted_iota(jnp.int32, (8, NX), 1)
    code_tile = jnp.zeros((8, NX), jnp.int32)
    for b in range(BLOCKS_HERE):
        rank = 0
        for earlier in range(b):
            rank = rank + (owners_ref[earlier] == owners_ref[b]).astype(jnp.int32)
        code_tile = jnp.where(lanes == b, owners_ref[b] * MOST + rank, code_tile)
    codes_out[...] = code_tile
    for way in range(2):
        codes_in[way, places[way]] = code_tile
        for offset in (2, 1, 3):
            pltpu.make_async_remote_copy(
                codes_out, codes_in.at[way, places[way]], codes_send.at[way], codes_recv.at[way],
                device_id={"gz": partner(way, offset)}, device_id_type=MESH,
            ).start()
    for step in range(STEPS):
        v = volume_ref if step == 0 else middle
        new = out_ref if step == STEPS - 1 else middle

        def plane(i):
            return v[i * CY : (i + 1) * CY, :]

        def diffuse(i, before, above):
            here = plane(i)
            slope_z = above - before
            y_low = jnp.where(xy == 0, here[0:1, :], y_halo[step, 0, i : i + 1, :])
            y_high = jnp.where(xy == N_XY - 1, here[CY - 1 : CY, :], y_halo[step, 1, i : i + 1, :])
            y_prev = jnp.where(row_index == 0, y_low, pltpu.roll(here, 1, 0))
            y_next = jnp.where(row_index == CY - 1, y_high, pltpu.roll(here, CY - 1, 0))
            slope_y = y_next - y_prev
            x_prev = jnp.where(lane_index == 0, here, pltpu.roll(here, 1, 1))
            x_next = jnp.where(lane_index == NX - 1, here, pltpu.roll(here, NX - 1, 1))
            slope_x = x_next - x_prev
            squares = slope_z * slope_z + slope_y * slope_y + slope_x * slope_x
            g_ref[i * CY : (i + 1) * CY, :] = recip(1.0 + squares * (0.25 / CONTRAST))

        for copy in halo_copies(step, v, "xy"):
            copy.wait_recv()
        for i in range(1, CZ - 1):
            diffuse(i, plane(i - 1), plane(i + 1))
        for copy in halo_copies(step, v, "gz"):
            copy.wait_recv()
        diffuse(0, jnp.where(gz == 0, plane(0), z_halo[step, 0]), plane(1))
        diffuse(CZ - 1, plane(CZ - 2), jnp.where(gz == N_GZ - 1, plane(CZ - 1), z_halo[step, 1]))

        def z_store(i, ratio, side, unit):
            z_keep[0, i] = ratio
            z_keep[1, i] = side
            z_keep[2, i] = unit

        ends = forward_sweep(CZ, plane, lambda i: g_ref[i * CY : (i + 1) * CY, :], z_store)
        for j, field in enumerate(ends):
            for h in range(LINES):
                z_out[step, pl.ds(LINES * j + h, Z_OWNERS, stride=32), :] = field[h * Z_OWNERS : (h + 1) * Z_OWNERS, :]
        z_in_blocks = z_in.at[step].reshape(N_GZ, 32, NX)
        z_out_blocks = z_out.at[step].reshape(Z_OWNERS, 32, NX)
        send_parts(z_out_blocks, z_in_blocks, z_send.at[step], z_recv.at[step], "gz", z_owners, gz, joins_z)

        def y_store(i, ratio, side, unit):
            y_keep[0, i] = ratio
            y_keep[1, i] = side
            y_keep[2, i] = unit

        ends = forward_sweep(
            CY,
            lambda i: v[pl.ds(i, CZ, stride=CY), :],
            lambda i: g_ref[pl.ds(i, CZ, stride=CY), :],
            y_store,
        )
        for j, field in enumerate(ends):
            for h in range(LINES):
                y_out[step, pl.ds(LINES * j + h, Y_OWNERS, stride=32), :] = field[h * Y_OWNERS : (h + 1) * Y_OWNERS, :]
        y_in_blocks = y_in.at[step].reshape(N_XY, 32, NX)
        y_out_blocks = y_out.at[step].reshape(Y_OWNERS, 32, NX)
        send_parts(y_out_blocks, y_in_blocks, y_send.at[step], y_recv.at[step], "xy", y_owners, xy, joins_y)

        def solve_x(i, carry):
            rows = pl.ds(pl.multiple_of(i * X_ROWS, X_ROWS), X_ROWS)
            g = g_ref[rows, :]
            lanes = lax.broadcasted_iota(jnp.int32, (X_ROWS, NX), 1)
            weight = jnp.where(lanes < NX - 1, HALF_K * (g + pltpu.roll(g, NX - 1, 1)), 0.0)
            diag = 1.0 + weight + pltpu.roll(weight, 1, 1)
            base[rows, :] = pcr(diag, weight, v[rows, :], NX, 1)
            return carry

        lax.fori_loop(0, X_FIRST, solve_x, 0)

        def z_load(i):
            return z_keep[0, i], z_keep[1, i], z_keep[2, i]

        def z_restore(i, side, low, high):
            natural[3, i * CY : (i + 1) * CY, :] = side
            z_keep[1, i] = low
            z_keep[2, i] = high

        backward_sweep(CZ, z_load, z_restore)

        def y_load(i):
            return y_keep[0, i], y_keep[1, i], y_keep[2, i]

        def y_restore(i, side, low, high):
            rows = pl.ds(i, CZ, stride=CY)
            natural[0, rows, :] = side
            natural[1, rows, :] = low
            natural[2, rows, :] = high

        backward_sweep(CY, y_load, y_restore)

        zb_out = z_back_out.at[step].reshape(N_GZ, 8, NX)
        zb_in = z_back.at[step].reshape(Z_OWNERS, 8, NX)
        yb_out = y_back_out.at[step].reshape(N_XY, 8, NX)
        yb_in = y_back.at[step].reshape(Y_OWNERS, 8, NX)

        @pl.when(joins_z)
        def _():
            wait_all(z_in_blocks, N_GZ - 1, z_recv.at[step])
            for h in range(LINES):
                flux = interface_fluxes(
                    lambda j: z_in[step, pl.ds(LINES * j + h, N_GZ, stride=32), :], N_GZ
                )
                z_back_out[step, pl.ds(h, N_GZ, stride=8), :] = pltpu.roll(flux, 1, 0)
                z_back_out[step, pl.ds(LINES + h, N_GZ, stride=8), :] = flux
            send_all(zb_out, zb_in, zb_send.at[step], zb_recv.at[step], "gz", z_targets, gz // 2)
            zb_in[gz // 2] = zb_out[gz]

        @pl.when(joins_y)
        def _():
            wait_all(y_in_blocks, N_XY - 1, y_recv.at[step])
            for h in range(LINES):
                flux = interface_fluxes(
                    lambda j: y_in[step, pl.ds(LINES * j + h, N_XY, stride=32), :], N_XY
                )
                y_back_out[step, pl.ds(h, N_XY, stride=8), :] = pltpu.roll(flux, 1, 0)
                y_back_out[step, pl.ds(LINES + h, N_XY, stride=8), :] = flux
            send_all(yb_out, yb_in, yb_send.at[step], yb_recv.at[step], "xy", y_targets, xy // 2)
            yb_in[xy // 2] = yb_out[xy]

        lax.fori_loop(X_FIRST, ROWS // X_ROWS, solve_x, 0)
        wait_parts(yb_in, Y_OWNERS, yb_recv.at[step], joins_y)
        wait_parts(zb_in, Z_OWNERS, zb_recv.at[step], joins_z)
        low_z = jnp.concatenate([z_back[step, pl.ds(h, Z_OWNERS, stride=8), :] for h in range(LINES)], axis=0)
        high_z = jnp.concatenate(
            [z_back[step, pl.ds(LINES + h, Z_OWNERS, stride=8), :] for h in range(LINES)], axis=0
        )

        def combine(i):
            rows = slice(i * CY, (i + 1) * CY)
            at = (i % Y_OWNERS) * 8 + i // Y_OWNERS
            low_y = y_back[step, at : at + 1, :]
            high_y = y_back[step, at + LINES : at + LINES + 1, :]
            total = base[rows, :] + natural[0, rows, :] + natural[3, rows, :]
            total = total + (low_z * z_keep[1, i] - high_z * z_keep[2, i])
            total = total + (low_y * natural[1, rows, :] - high_y * natural[2, rows, :])
            new[rows, :] = total * (1.0 / 3.0)

        if step < STEPS - 1:
            combine(0)
            combine(CZ - 1)
            send_z_halo(step + 1, new)
            for i in range(1, CZ - 1):
                combine(i)
            send_y_halo(step + 1, new)
            for way in range(2):
                wait_all(codes_in.at[way], 3, codes_recv.at[way])
            to_scalars.start()
            to_scalars.wait()
            choose()
        else:
            for chunk in range(CHUNKS):
                for way in range(2):
                    for b in range(BLOCKS_HERE):
                        combine(b * 4 + way * 2 + chunk)
                    send_near(way, chunk)

    for offset in (1, 3, 2, 0):
        for way in range(2):
            here = pl.ds(way * HALF_ROWS, HALF_ROWS)
            pass_on(way, 0, offset, 0, HALF_ROWS, lambda index: blocks[index, here, :])
    for chunk in range(CHUNKS):
        for way in range(2):
            near = gathered[way][chunk]
            wait_all(near, 2, gather_recv.at[chunk, way])
            side, offset = ((0, 1), (1, 3))[chunk % 2]
            landing = pl.ds(chunk * CHUNK_ROWS, CHUNK_ROWS)
            pltpu.make_async_remote_copy(
                near.at[side], gathered_far[way].at[:, landing, :],
                far_send.at[way], far_recv.at[way],
                device_id={"gz": partner(way, offset)}, device_id_type=MESH,
            ).start()
    for offset in (1, 3, 2, 0):
        for side in range(2):
            for way in range(2):
                pass_on(
                    way, 1 + side, offset, 0, HALF_ROWS,
                    lambda index: jnp.concatenate([gathered[way][chunk][side, index] for chunk in range(CHUNKS)], axis=0),
                )
    for way in range(2):
        wait_all(gathered_far[way], BLOCKS_HERE, far_recv.at[way])
        for offset in (1, 3, 2, 0):
            pass_on(way, 3, offset, 0, HALF_ROWS, lambda index: gathered_far[way][index])
    for way in range(2):
        for kind, part in enumerate(
            (
                packed.at[way, 0, pl.ds(0, 3)],
                packed.at[way, pl.ds(1, 2), pl.ds(0, 3)],
                packed.at[way, 3, pl.ds(0, 3)],
            )
        ):
            pltpu.make_async_copy(part, part, spread_recv.at[way, kind]).wait()
            pltpu.make_async_copy(part, part, spread_send.at[way, kind]).wait()
        for chunk in range(CHUNKS):
            wait_all(gathered[way][chunk], 2, gather_send.at[chunk, way])
        wait_all(gathered_far[way], BLOCKS_HERE, far_send.at[way])
        wait_all(codes_in.at[way], 3, codes_send.at[way])
    for step in range(STEPS):
        v = volume_ref if step == 0 else middle
        for k in range(4):
            part = v.at[pl.ds(0, CY)] if k < 2 else y_halo_out.at[step, 0]
            pltpu.make_async_copy(part, part, halo_send.at[step, k]).wait()
        wait_parts(z_out.at[step].reshape(Z_OWNERS, 32, NX), Z_OWNERS, z_send.at[step], joins_z)
        wait_parts(y_out.at[step].reshape(Y_OWNERS, 32, NX), Y_OWNERS, y_send.at[step], joins_y)

        @pl.when(joins_z)
        def _():
            wait_all(z_back_out.at[step].reshape(N_GZ, 8, NX), N_GZ - 1, zb_send.at[step])

        @pl.when(joins_y)
        def _():
            wait_all(y_back_out.at[step].reshape(N_XY, 8, NX), N_XY - 1, yb_send.at[step])


def vmem(*shape):
    return pltpu.VMEM(shape, jnp.float32)


def diffuse_and_route(volume, owners):
    dma = pltpu.SemaphoreType.DMA
    return pl.pallas_call(
        diffuse_and_route_kernel,
        out_shape=(
            jax.ShapeDtypeStruct((ROWS, NX), jnp.float32),
            jax.ShapeDtypeStruct((4, 4, MOST, BLOCK_ROWS, NX), jnp.float32),
        ),
        in_specs=[
            pl.BlockSpec(memory_space=pltpu.HBM),
            pl.BlockSpec(memory_space=pltpu.HBM),
        ],
        out_specs=(pl.BlockSpec(memory_space=pltpu.VMEM),) * 2,
        scratch_shapes=[
            vmem(ROWS, NX),
            vmem(ROWS, NX),
            vmem(STEPS, 2, CY, NX),
            vmem(STEPS, 2, CZ, NX),
            vmem(STEPS, 2, CZ, NX),
            vmem(ROWS, NX),
            vmem(3, CZ, CY, NX),
            vmem(3, CY, CZ, NX),
            vmem(4, ROWS, NX),
            vmem(ROWS, NX),
            vmem(STEPS, Z_OWNERS * 32, NX),
            vmem(STEPS, N_GZ * 32, NX),
            vmem(STEPS, Y_OWNERS * 32, NX),
            vmem(STEPS, N_XY * 32, NX),
            vmem(STEPS, N_GZ * 8, NX),
            vmem(STEPS, Z_OWNERS * 8, NX),
            vmem(STEPS, N_XY * 8, NX),
            vmem(STEPS, Y_OWNERS * 8, NX),
            dma((STEPS, 4)),
            dma((STEPS, 4)),
        ]
        + [dma((STEPS,))] * 8
        + [
            pltpu.SMEM((BLOCKS_HERE,), jnp.int32),
            dma,
            pltpu.VMEM((8, NX), jnp.int32),
            pltpu.VMEM((2, 4, 8, NX), jnp.int32),
            pltpu.SMEM((2, 4, 8, NX), jnp.int32),
            pltpu.SMEM((2, 2, 4, 4, MOST), jnp.int32),
            [[vmem(2, BLOCKS_HERE, CHUNK_ROWS, NX) for _ in range(CHUNKS)] for _ in range(2)],
            [vmem(BLOCKS_HERE, HALF_ROWS, NX) for _ in range(2)],
            vmem(2, 4, 4, MOST, HALF_ROWS, NX),
            dma,
            dma((2,)),
            dma((2,)),
            dma,
        ]
        + [dma((CHUNKS, 2))] * 2
        + [dma((2,))] * 2
        + [dma((2, 3))] * 2,
        compiler_params=pltpu.CompilerParams(
            collective_id=0, has_side_effects=True, vmem_limit_bytes=48 << 20
        ),
    )(pltpu.with_memory_space_constraint(volume, pltpu.HBM), pltpu.with_memory_space_constraint(owners, pltpu.HBM))


def write_kernel(field_ref, routed_ref, field_out, routed_out, semaphores):
    copies = [pltpu.make_async_copy(field_ref, field_out, semaphores.at[0])]
    for part in range(4):
        rows = pl.ds(part * (N_GZ * MOST // 4), N_GZ * MOST // 4)
        copies.append(
            pltpu.make_async_copy(routed_ref.at[rows], routed_out.at[rows], semaphores.at[1 + part])
        )
    for copy in copies[::-1]:
        copy.start()
    for copy in copies:
        copy.wait()


def write_out(field, routed):
    return pl.pallas_call(
        write_kernel,
        out_shape=(
            jax.ShapeDtypeStruct(field.shape, field.dtype),
            jax.ShapeDtypeStruct(routed.shape, routed.dtype),
        ),
        in_specs=[pl.BlockSpec(memory_space=pl.ANY)] * 2,
        out_specs=(pl.BlockSpec(memory_space=pltpu.HBM),) * 2,
        scratch_shapes=[pltpu.SemaphoreType.DMA((1 + 4,))],
        compiler_params=pltpu.CompilerParams(vmem_limit_bytes=8 << 20),
    )(field, routed)


def on_device(volume, owners):
    depth, height, width = volume.shape
    field, routed = diffuse_and_route(volume.reshape(depth * height, width), owners.reshape(-1))
    field, routed = write_out(field, routed.reshape(N_GZ * MOST, BLOCK_ROWS, width))
    return (field.reshape(volume.shape), routed.reshape(1, N_GZ * MOST, BLOCK_ROWS, width))


def solution(mesh):
    in_specs = (P("gz", "xy", None), P("xy", "gz", None))
    out_specs = (P("gz", "xy", None), P("xy", "gz", None, None))
    return jax.shard_map(
        on_device, mesh=mesh, in_specs=in_specs, out_specs=out_specs, check_vma=False
    )
```

```python
import jax
import jax.numpy as jnp
from jax import lax
from jax.experimental import pallas as pl
from jax.experimental.pallas import tpu as pltpu
from jax.sharding import PartitionSpec as P

STEPS = 2
MOST = 2
BLOCK_ROWS = 128

TIME_STEP = 30.0
CONTRAST = 4.0
HALF_K = 1.5 * TIME_STEP

CZ = 16
CY = 32
NX = 128
ROWS = CZ * CY
N_GZ = 16
N_XY = 8
FIELDS = 7
Z_OWNERS = 8
Y_OWNERS = 4
LINES = 4
BLOCKS_HERE = 4
HALF_ROWS = BLOCK_ROWS // 2
CHUNKS = 2
X_ROWS = 4 * CY
X_FIRST = 2
CHUNK_ROWS = HALF_ROWS // CHUNKS
MESH = pl.DeviceIdType.MESH

Z_PEERS = sorted(
    [(a, b) for a in range(4) for b in range(4) if (a, b) != (0, 0)],
    key=lambda p: -(min(p[0], 4 - p[0]) + min(p[1], 4 - p[1])),
)
Y_PEERS = sorted(
    [(a, b) for a in range(4) for b in range(2) if (a, b) != (0, 0)],
    key=lambda p: -(2 * min(p[0], 4 - p[0]) + p[1]),
)


def recip(value):
    return 1.0 / value


def pcr(diag, coupling, side, count, axis):
    stride = 1
    while stride < count:
        inverse = recip(diag)
        scaled = coupling * inverse
        side_scaled = side * inverse
        side = (
            side
            + pltpu.roll(coupling * side_scaled, stride, axis)
            + coupling * pltpu.roll(side_scaled, count - stride, axis)
        )
        diag = (
            diag
            - pltpu.roll(coupling * scaled, stride, axis)
            - coupling * coupling * pltpu.roll(inverse, count - stride, axis)
        )
        stride *= 2
        if stride < count:
            coupling = coupling * pltpu.roll(scaled, count - stride // 2, axis)
    return side * recip(diag)


def forward_sweep(count, load_v, load_g, store):
    g_here = load_g(0)
    g_first = g_here
    total = jnp.ones_like(g_here)
    side = load_v(0)
    unit = jnp.ones_like(g_here)
    first_side = jnp.zeros_like(g_here)
    first_unit = jnp.zeros_like(g_here)
    for i in range(count - 1):
        g_next = load_g(i + 1)
        weight = HALF_K * (g_here + g_next)
        inverse = recip(total + weight)
        ratio = weight * inverse
        side_scaled = side * inverse
        unit_scaled = unit * inverse
        store(i, ratio, side_scaled, unit_scaled)
        first_side = first_side + unit * side_scaled
        first_unit = first_unit + unit * unit_scaled
        total = 1.0 + ratio * total
        side = load_v(i + 1) + ratio * side
        unit = ratio * unit
        g_here = g_next
    inverse = recip(total)
    last_side = side * inverse
    last_unit = unit * inverse
    store(count - 1, inverse, last_side, last_unit)
    first_side = first_side + unit * last_side
    first_unit = first_unit + unit * last_unit
    return (first_side, last_side, first_unit, last_unit, inverse, g_first, g_here)


def backward_sweep(count, load, store):
    high_unit, side, low_unit = load(count - 1)
    store(count - 1, side, low_unit, high_unit)
    for i in range(count - 2, -1, -1):
        ratio, side_scaled, unit_scaled = load(i)
        side = side_scaled + ratio * side
        low_unit = unit_scaled + ratio * low_unit
        high_unit = ratio * high_unit
        store(i, side, low_unit, high_unit)


def interface_fluxes(received, count):
    first_side, last_side, first_unit, cross, last_unit, g_first, g_last = [received(j) for j in range(FIELDS)]
    index = lax.broadcasted_iota(jnp.int32, (count, NX), 0)

    def following(field):
        return pltpu.roll(field, count - 1, 0)

    weight = HALF_K * (g_last + following(g_first))
    diag = recip(weight) + last_unit + following(first_unit)
    side = last_side - following(first_side)
    diag = jnp.where(index < count - 1, diag, 1.0)
    side = jnp.where(index < count - 1, side, 0.0)
    coupling = jnp.where(index < count - 2, following(cross), 0.0)
    return pcr(diag, coupling, side, count, 0)


def diffuse_and_route_kernel(
    volume_hbm,
    owners_hbm,
    out_ref,
    routed_ref,
    volume_ref,
    middle,
    z_halo,
    y_halo_out,
    y_halo,
    g_ref,
    z_keep,
    y_keep,
    natural,
    base,
    z_out,
    z_in,
    y_out,
    y_in,
    z_back_out,
    z_back,
    y_back_out,
    y_back,
    halo_send,
    halo_recv,
    z_send,
    z_recv,
    y_send,
    y_recv,
    zb_send,
    zb_recv,
    yb_send,
    yb_recv,
    owners_ref,
    owners_sem,
    codes_out,
    codes_in,
    codes,
    choice,
    gathered,
    gathered_far,
    packed,
    volume_sem,
    codes_send,
    codes_recv,
    codes_sem,
    gather_send,
    gather_recv,
    far_send,
    far_recv,
    spread_send,
    spread_recv,
):
    gz = lax.axis_index("gz")
    xy = lax.axis_index("xy")
    z_targets = [
        lax.rem(gz // 4 + dz, 4) * 4 + lax.rem(lax.rem(gz, 4) + dy, 4) for dz, dy in Z_PEERS
    ]
    y_targets = [
        lax.rem(xy // 2 + dx, 4) * 2 + lax.rem(lax.rem(xy, 2) + core, 2) for dx, core in Y_PEERS
    ]
    odd = lax.rem(gz + xy, 2)
    joins_z = odd == 0
    joins_y = odd == 1
    z_owners = [
        (lax.rem(gz // 4 + dz, 4) * 4 + lax.rem(lax.rem(gz, 4) + dy + odd, 4), (dz, dy) == (0, 0))
        for dz, dy in ((2, 2), (1, 2), (3, 2), (2, 0), (1, 0), (3, 0), (0, 2), (0, 0))
    ]
    y_owners = [
        (lax.rem(xy // 2 + dx, 4) * 2 + lax.rem(lax.rem(xy, 2) + 1 - odd, 2), dx == 0) for dx in (2, 1, 3, 0)
    ]
    barrier = pltpu.get_barrier_semaphore()
    for target in z_targets:
        pl.semaphore_signal(barrier, 1, device_id={"gz": target}, device_id_type=MESH)
    for target in y_targets:
        pl.semaphore_signal(barrier, 1, device_id={"xy": target}, device_id_type=MESH)
    load_volume = pltpu.make_async_copy(volume_hbm, volume_ref, volume_sem)
    load_volume.start()
    load_owners = pltpu.make_async_copy(owners_hbm, owners_ref, owners_sem)
    load_owners.start()
    pl.semaphore_wait(barrier, N_GZ + N_XY - 2)

    chip_z, chip_y = gz // 4, lax.rem(gz, 4)
    places = [chip_y, chip_z]

    def partner(way, offset):
        if way == 0:
            return chip_z * 4 + lax.rem(chip_y + offset, 4)
        return lax.rem(chip_z + offset, 4) * 4 + chip_y

    load_volume.wait()

    row_index = lax.broadcasted_iota(jnp.int32, (CY, NX), 0)
    lane_index = lax.broadcasted_iota(jnp.int32, (CY, NX), 1)

    blocks = out_ref.reshape(BLOCKS_HERE, BLOCK_ROWS, NX)
    to_scalars = pltpu.make_async_copy(codes_in, codes, codes_sem)

    def place_of(way, source):
        return lax.rem(places[way] + (0, 3, 1, 2)[source], 4)

    def choose():
        for way in range(2):
            for source in range(4):
                place = place_of(way, source)
                for offset in range(4):
                    target = partner(1 - way, offset)
                    for rank in range(MOST):
                        index, found = 0, 0
                        for b in range(BLOCKS_HERE):
                            hit = (codes[way, place, 0, b] == target * MOST + rank).astype(jnp.int32)
                            index = index + b * hit
                            found = found + hit
                        choice[0, way, source, offset, rank] = index
                        choice[1, way, source, offset, rank] = found

    def send_near(way, chunk):
        here = pl.ds(way * HALF_ROWS + chunk * CHUNK_ROWS, CHUNK_ROWS)
        for side, offset in ((0, 1), (1, 3)):
            pltpu.make_async_remote_copy(
                blocks.at[:, here, :], gathered[way][chunk].at[side],
                gather_send.at[chunk, way], gather_recv.at[chunk, way],
                device_id={"gz": partner(way, offset)}, device_id_type=MESH,
            ).start()

    def pass_on(way, source, offset, first, count, read):
        there = pl.ds(first, count)
        final = pl.ds(way * HALF_ROWS + first, count)
        place = place_of(way, source)
        at = (chip_z, place) if way == 0 else (place, chip_y)
        for rank in range(MOST):
            found = choice[1, way, source, offset, rank]
            rows = jnp.where(found > 0, read(choice[0, way, source, offset, rank]), 0.0)
            if offset:
                packed[way, source, offset, rank, there, :] = rows
            else:
                routed_ref[at[0], at[1], rank, final, :] = rows
        if offset:
            kind = (0, 1, 1, 2)[source]
            pltpu.make_async_remote_copy(
                packed.at[way, source, offset, :, there, :], routed_ref.at[at[0], at[1], :, final, :],
                spread_send.at[way, kind], spread_recv.at[way, kind],
                device_id={"gz": partner(1 - way, offset)}, device_id_type=MESH,
            ).start()

    def send_all(source, landing, send_sem, recv_sem, axis, targets, me):
        for target in targets:
            pltpu.make_async_remote_copy(
                source.at[target], landing.at[me], send_sem, recv_sem,
                device_id={axis: target}, device_id_type=MESH,
            ).start()

    def send_parts(source, landing, send_sem, recv_sem, axis, owners, me, is_owner):
        for target, may_be_self in owners:
            copy = pltpu.make_async_remote_copy(
                source.at[target // 2], landing.at[me], send_sem, recv_sem,
                device_id={axis: target}, device_id_type=MESH,
            )
            if may_be_self:
                pl.when(jnp.logical_not(is_owner))(copy.start)

                @pl.when(is_owner)
                def _():
                    landing[me] = source[target // 2]

            else:
                copy.start()

    def wait_parts(buffer, count, semaphore, is_owner):
        @pl.when(is_owner)
        def _():
            wait_all(buffer, count - 1, semaphore)

        @pl.when(jnp.logical_not(is_owner))
        def _():
            wait_all(buffer, count, semaphore)

    def wait_all(buffer, count, semaphore):
        part = buffer.at[pl.ds(0, count)]
        pltpu.make_async_copy(part, part, semaphore).wait()

    def halo_copies(step, v, which):
        copies = []
        for k, (axis, me, count, forward) in enumerate(
            [("gz", gz, N_GZ, 0), ("gz", gz, N_GZ, 1), ("xy", xy, N_XY, 0), ("xy", xy, N_XY, 1)]
        ):
            if axis != which:
                continue
            target = lax.rem(me + (1 if forward else count - 1), count)
            if axis == "gz":
                source = v.at[pl.ds((CZ - 1) * CY if forward else 0, CY)]
                landing = z_halo.at[step, 1 - forward]
            else:
                source = y_halo_out.at[step, forward]
                landing = y_halo.at[step, 1 - forward]
            copies.append(
                pltpu.make_async_remote_copy(
                    source, landing, halo_send.at[step, k], halo_recv.at[step, k],
                    device_id={axis: target}, device_id_type=MESH,
                )
            )
        return copies

    def send_z_halo(step, v):
        for copy in halo_copies(step, v, "gz"):
            copy.start()

    def send_y_halo(step, v):
        y_halo_out[step, 0] = v[pl.ds(0, CZ, stride=CY), :]
        y_halo_out[step, 1] = v[pl.ds(CY - 1, CZ, stride=CY), :]
        for copy in halo_copies(step, v, "xy"):
            copy.start()

    send_z_halo(0, volume_ref)
    send_y_halo(0, volume_ref)
    load_owners.wait()
    lanes = lax.broadcasted_iota(jnp.int32, (8, NX), 1)
    code_tile = jnp.zeros((8, NX), jnp.int32)
    for b in range(BLOCKS_HERE):
        rank = 0
        for earlier in range(b):
            rank = rank + (owners_ref[earlier] == owners_ref[b]).astype(jnp.int32)
        code_tile = jnp.where(lanes == b, owners_ref[b] * MOST + rank, code_tile)
    codes_out[...] = code_tile
    for way in range(2):
        codes_in[way, places[way]] = code_tile
        for offset in (2, 1, 3):
            pltpu.make_async_remote_copy(
                codes_out, codes_in.at[way, places[way]], codes_send.at[way], codes_recv.at[way],
                device_id={"gz": partner(way, offset)}, device_id_type=MESH,
            ).start()
    for step in range(STEPS):
        v = volume_ref if step == 0 else middle
        new = out_ref if step == STEPS - 1 else middle

        def plane(i):
            return v[i * CY : (i + 1) * CY, :]

        def diffuse(i, before, above):
            here = plane(i)
            slope_z = above - before
            y_low = jnp.where(xy == 0, here[0:1, :], y_halo[step, 0, i : i + 1, :])
            y_high = jnp.where(xy == N_XY - 1, here[CY - 1 : CY, :], y_halo[step, 1, i : i + 1, :])
            y_prev = jnp.where(row_index == 0, y_low, pltpu.roll(here, 1, 0))
            y_next = jnp.where(row_index == CY - 1, y_high, pltpu.roll(here, CY - 1, 0))
            slope_y = y_next - y_prev
            x_prev = jnp.where(lane_index == 0, here, pltpu.roll(here, 1, 1))
            x_next = jnp.where(lane_index == NX - 1, here, pltpu.roll(here, NX - 1, 1))
            slope_x = x_next - x_prev
            squares = slope_z * slope_z + slope_y * slope_y + slope_x * slope_x
            g_ref[i * CY : (i + 1) * CY, :] = recip(1.0 + squares * (0.25 / CONTRAST))

        for copy in halo_copies(step, v, "xy"):
            copy.wait_recv()
        for i in range(1, CZ - 1):
            diffuse(i, plane(i - 1), plane(i + 1))
        for copy in halo_copies(step, v, "gz"):
            copy.wait_recv()
        diffuse(0, jnp.where(gz == 0, plane(0), z_halo[step, 0]), plane(1))
        diffuse(CZ - 1, plane(CZ - 2), jnp.where(gz == N_GZ - 1, plane(CZ - 1), z_halo[step, 1]))

        def z_store(i, ratio, side, unit):
            z_keep[0, i] = ratio
            z_keep[1, i] = side
            z_keep[2, i] = unit

        ends = forward_sweep(CZ, plane, lambda i: g_ref[i * CY : (i + 1) * CY, :], z_store)
        for j, field in enumerate(ends):
            for h in range(LINES):
                z_out[step, pl.ds(LINES * j + h, Z_OWNERS, stride=32), :] = field[h * Z_OWNERS : (h + 1) * Z_OWNERS, :]
        z_in_blocks = z_in.at[step].reshape(N_GZ, 32, NX)
        z_out_blocks = z_out.at[step].reshape(Z_OWNERS, 32, NX)
        send_parts(z_out_blocks, z_in_blocks, z_send.at[step], z_recv.at[step], "gz", z_owners, gz, joins_z)

        def y_store(i, ratio, side, unit):
            y_keep[0, i] = ratio
            y_keep[1, i] = side
            y_keep[2, i] = unit

        ends = forward_sweep(
            CY,
            lambda i: v[pl.ds(i, CZ, stride=CY), :],
            lambda i: g_ref[pl.ds(i, CZ, stride=CY), :],
            y_store,
        )
        for j, field in enumerate(ends):
            for h in range(LINES):
                y_out[step, pl.ds(LINES * j + h, Y_OWNERS, stride=32), :] = field[h * Y_OWNERS : (h + 1) * Y_OWNERS, :]
        y_in_blocks = y_in.at[step].reshape(N_XY, 32, NX)
        y_out_blocks = y_out.at[step].reshape(Y_OWNERS, 32, NX)
        send_parts(y_out_blocks, y_in_blocks, y_send.at[step], y_recv.at[step], "xy", y_owners, xy, joins_y)

        def solve_x(i, carry):
            rows = pl.ds(pl.multiple_of(i * X_ROWS, X_ROWS), X_ROWS)
            g = g_ref[rows, :]
            lanes = lax.broadcasted_iota(jnp.int32, (X_ROWS, NX), 1)
            weight = jnp.where(lanes < NX - 1, HALF_K * (g + pltpu.roll(g, NX - 1, 1)), 0.0)
            diag = 1.0 + weight + pltpu.roll(weight, 1, 1)
            base[rows, :] = pcr(diag, weight, v[rows, :], NX, 1)
            return carry

        lax.fori_loop(0, X_FIRST, solve_x, 0, unroll=True)

        def z_load(i):
            return z_keep[0, i], z_keep[1, i], z_keep[2, i]

        def z_restore(i, side, low, high):
            natural[3, i * CY : (i + 1) * CY, :] = side
            z_keep[1, i] = low
            z_keep[2, i] = high

        backward_sweep(CZ, z_load, z_restore)

        def y_load(i):
            return y_keep[0, i], y_keep[1, i], y_keep[2, i]

        def y_restore(i, side, low, high):
            rows = pl.ds(i, CZ, stride=CY)
            natural[0, rows, :] = side
            natural[1, rows, :] = low
            natural[2, rows, :] = high

        backward_sweep(CY, y_load, y_restore)

        zb_out = z_back_out.at[step].reshape(N_GZ, 8, NX)
        zb_in = z_back.at[step].reshape(Z_OWNERS, 8, NX)
        yb_out = y_back_out.at[step].reshape(N_XY, 8, NX)
        yb_in = y_back.at[step].reshape(Y_OWNERS, 8, NX)

        @pl.when(joins_z)
        def _():
            wait_all(z_in_blocks, N_GZ - 1, z_recv.at[step])
            for h in range(LINES):
                flux = interface_fluxes(
                    lambda j: z_in[step, pl.ds(LINES * j + h, N_GZ, stride=32), :], N_GZ
                )
                z_back_out[step, pl.ds(h, N_GZ, stride=8), :] = pltpu.roll(flux, 1, 0)
                z_back_out[step, pl.ds(LINES + h, N_GZ, stride=8), :] = flux
            send_all(zb_out, zb_in, zb_send.at[step], zb_recv.at[step], "gz", z_targets, gz // 2)
            zb_in[gz // 2] = zb_out[gz]

        @pl.when(joins_y)
        def _():
            wait_all(y_in_blocks, N_XY - 1, y_recv.at[step])
            for h in range(LINES):
                flux = interface_fluxes(
                    lambda j: y_in[step, pl.ds(LINES * j + h, N_XY, stride=32), :], N_XY
                )
                y_back_out[step, pl.ds(h, N_XY, stride=8), :] = pltpu.roll(flux, 1, 0)
                y_back_out[step, pl.ds(LINES + h, N_XY, stride=8), :] = flux
            send_all(yb_out, yb_in, yb_send.at[step], yb_recv.at[step], "xy", y_targets, xy // 2)
            yb_in[xy // 2] = yb_out[xy]

        lax.fori_loop(X_FIRST, ROWS // X_ROWS, solve_x, 0)
        wait_parts(yb_in, Y_OWNERS, yb_recv.at[step], joins_y)
        wait_parts(zb_in, Z_OWNERS, zb_recv.at[step], joins_z)
        low_z = jnp.concatenate([z_back[step, pl.ds(h, Z_OWNERS, stride=8), :] for h in range(LINES)], axis=0)
        high_z = jnp.concatenate(
            [z_back[step, pl.ds(LINES + h, Z_OWNERS, stride=8), :] for h in range(LINES)], axis=0
        )

        def combine(i):
            rows = slice(i * CY, (i + 1) * CY)
            at = (i % Y_OWNERS) * 8 + i // Y_OWNERS
            low_y = y_back[step, at : at + 1, :]
            high_y = y_back[step, at + LINES : at + LINES + 1, :]
            total = base[rows, :] + natural[0, rows, :] + natural[3, rows, :]
            total = total + (low_z * z_keep[1, i] - high_z * z_keep[2, i])
            total = total + (low_y * natural[1, rows, :] - high_y * natural[2, rows, :])
            new[rows, :] = total * (1.0 / 3.0)

        if step < STEPS - 1:
            combine(0)
            combine(CZ - 1)
            send_z_halo(step + 1, new)
            for i in range(1, CZ - 1):
                combine(i)
            send_y_halo(step + 1, new)
            for way in range(2):
                wait_all(codes_in.at[way], 3, codes_recv.at[way])
            to_scalars.start()
            to_scalars.wait()
            choose()
        else:
            for chunk in range(CHUNKS):
                for way in range(2):
                    for b in range(BLOCKS_HERE):
                        combine(b * 4 + way * 2 + chunk)
                    send_near(way, chunk)

    for offset in (1, 3, 2, 0):
        for way in range(2):
            here = pl.ds(way * HALF_ROWS, HALF_ROWS)
            pass_on(way, 0, offset, 0, HALF_ROWS, lambda index: blocks[index, here, :])
    for chunk in range(CHUNKS):
        for way in range(2):
            near = gathered[way][chunk]
            wait_all(near, 2, gather_recv.at[chunk, way])
            side, offset = ((0, 1), (1, 3))[chunk % 2]
            landing = pl.ds(chunk * CHUNK_ROWS, CHUNK_ROWS)
            pltpu.make_async_remote_copy(
                near.at[side], gathered_far[way].at[:, landing, :],
                far_send.at[way], far_recv.at[way],
                device_id={"gz": partner(way, offset)}, device_id_type=MESH,
            ).start()
    for offset in (1, 3, 2, 0):
        for side in range(2):
            for way in range(2):
                pass_on(
                    way, 1 + side, offset, 0, HALF_ROWS,
                    lambda index: jnp.concatenate([gathered[way][chunk][side, index] for chunk in range(CHUNKS)], axis=0),
                )
    for way in range(2):
        wait_all(gathered_far[way], BLOCKS_HERE, far_recv.at[way])
        for offset in (1, 3, 2, 0):
            pass_on(way, 3, offset, 0, HALF_ROWS, lambda index: gathered_far[way][index])
    for way in range(2):
        for kind, part in enumerate(
            (
                packed.at[way, 0, pl.ds(0, 3)],
                packed.at[way, pl.ds(1, 2), pl.ds(0, 3)],
                packed.at[way, 3, pl.ds(0, 3)],
            )
        ):
            pltpu.make_async_copy(part, part, spread_recv.at[way, kind]).wait()
            pltpu.make_async_copy(part, part, spread_send.at[way, kind]).wait()
        for chunk in range(CHUNKS):
            wait_all(gathered[way][chunk], 2, gather_send.at[chunk, way])
        wait_all(gathered_far[way], BLOCKS_HERE, far_send.at[way])
        wait_all(codes_in.at[way], 3, codes_send.at[way])
    for step in range(STEPS):
        v = volume_ref if step == 0 else middle
        for k in range(4):
            part = v.at[pl.ds(0, CY)] if k < 2 else y_halo_out.at[step, 0]
            pltpu.make_async_copy(part, part, halo_send.at[step, k]).wait()
        wait_parts(z_out.at[step].reshape(Z_OWNERS, 32, NX), Z_OWNERS, z_send.at[step], joins_z)
        wait_parts(y_out.at[step].reshape(Y_OWNERS, 32, NX), Y_OWNERS, y_send.at[step], joins_y)

        @pl.when(joins_z)
        def _():
            wait_all(z_back_out.at[step].reshape(N_GZ, 8, NX), N_GZ - 1, zb_send.at[step])

        @pl.when(joins_y)
        def _():
            wait_all(y_back_out.at[step].reshape(N_XY, 8, NX), N_XY - 1, yb_send.at[step])


def vmem(*shape):
    return pltpu.VMEM(shape, jnp.float32)


def diffuse_and_route(volume, owners):
    dma = pltpu.SemaphoreType.DMA
    return pl.pallas_call(
        diffuse_and_route_kernel,
        out_shape=(
            jax.ShapeDtypeStruct((ROWS, NX), jnp.float32),
            jax.ShapeDtypeStruct((4, 4, MOST, BLOCK_ROWS, NX), jnp.float32),
        ),
        in_specs=[
            pl.BlockSpec(memory_space=pltpu.HBM),
            pl.BlockSpec(memory_space=pltpu.HBM),
        ],
        out_specs=(pl.BlockSpec(memory_space=pltpu.VMEM),) * 2,
        scratch_shapes=[
            vmem(ROWS, NX),
            vmem(ROWS, NX),
            vmem(STEPS, 2, CY, NX),
            vmem(STEPS, 2, CZ, NX),
            vmem(STEPS, 2, CZ, NX),
            vmem(ROWS, NX),
            vmem(3, CZ, CY, NX),
            vmem(3, CY, CZ, NX),
            vmem(4, ROWS, NX),
            vmem(ROWS, NX),
            vmem(STEPS, Z_OWNERS * 32, NX),
            vmem(STEPS, N_GZ * 32, NX),
            vmem(STEPS, Y_OWNERS * 32, NX),
            vmem(STEPS, N_XY * 32, NX),
            vmem(STEPS, N_GZ * 8, NX),
            vmem(STEPS, Z_OWNERS * 8, NX),
            vmem(STEPS, N_XY * 8, NX),
            vmem(STEPS, Y_OWNERS * 8, NX),
            dma((STEPS, 4)),
            dma((STEPS, 4)),
        ]
        + [dma((STEPS,))] * 8
        + [
            pltpu.SMEM((BLOCKS_HERE,), jnp.int32),
            dma,
            pltpu.VMEM((8, NX), jnp.int32),
            pltpu.VMEM((2, 4, 8, NX), jnp.int32),
            pltpu.SMEM((2, 4, 8, NX), jnp.int32),
            pltpu.SMEM((2, 2, 4, 4, MOST), jnp.int32),
            [[vmem(2, BLOCKS_HERE, CHUNK_ROWS, NX) for _ in range(CHUNKS)] for _ in range(2)],
            [vmem(BLOCKS_HERE, HALF_ROWS, NX) for _ in range(2)],
            vmem(2, 4, 4, MOST, HALF_ROWS, NX),
            dma,
            dma((2,)),
            dma((2,)),
            dma,
        ]
        + [dma((CHUNKS, 2))] * 2
        + [dma((2,))] * 2
        + [dma((2, 3))] * 2,
        compiler_params=pltpu.CompilerParams(
            collective_id=0, has_side_effects=True, vmem_limit_bytes=48 << 20
        ),
    )(pltpu.with_memory_space_constraint(volume, pltpu.HBM), pltpu.with_memory_space_constraint(owners, pltpu.HBM))


def write_kernel(field_ref, routed_ref, field_out, routed_out, semaphores):
    copies = [pltpu.make_async_copy(field_ref, field_out, semaphores.at[0])]
    for part in range(4):
        rows = pl.ds(part * (N_GZ * MOST // 4), N_GZ * MOST // 4)
        copies.append(
            pltpu.make_async_copy(routed_ref.at[rows], routed_out.at[rows], semaphores.at[1 + part])
        )
    for copy in copies[::-1]:
        copy.start()
    for copy in copies:
        copy.wait()


def write_out(field, routed):
    return pl.pallas_call(
        write_kernel,
        out_shape=(
            jax.ShapeDtypeStruct(field.shape, field.dtype),
            jax.ShapeDtypeStruct(routed.shape, routed.dtype),
        ),
        in_specs=[pl.BlockSpec(memory_space=pl.ANY)] * 2,
        out_specs=(pl.BlockSpec(memory_space=pltpu.HBM),) * 2,
        scratch_shapes=[pltpu.SemaphoreType.DMA((1 + 4,))],
        compiler_params=pltpu.CompilerParams(vmem_limit_bytes=8 << 20),
    )(field, routed)


def on_device(volume, owners):
    depth, height, width = volume.shape
    field, routed = diffuse_and_route(volume.reshape(depth * height, width), owners.reshape(-1))
    field, routed = write_out(field, routed.reshape(N_GZ * MOST, BLOCK_ROWS, width))
    return (field.reshape(volume.shape), routed.reshape(1, N_GZ * MOST, BLOCK_ROWS, width))


def solution(mesh):
    in_specs = (P("gz", "xy", None), P("xy", "gz", None))
    out_specs = (P("gz", "xy", None), P("xy", "gz", None, None))
    return jax.shard_map(
        on_device, mesh=mesh, in_specs=in_specs, out_specs=out_specs, check_vma=False
    )
```
